128 devices in a mesh: seq: 32 (over y, x, core), song: 4 (over z).
Axes of the slice: x: 4, y: 4, z: 4, core: 2. Of those that a mesh axis runs over, the one named last changes fastest.
Arguments:
- spectrum: bfloat16 [4, 2048, 8196], P('song', 'seq'), may hold values from -6 to 6
- widths: int32 [32], replicated, may hold values from 4 to 257, as said below
- lengths: int32 [4], P('song'), may hold values from 1024 to 2048, as said below
- bin_gain: float32 [8196], replicated, may hold values from 0.5 to 2
- embed_weight: bfloat16 [8196, 384], replicated, may hold values from -0.375 to 0.375
- embed_bias: float32 [32, 384], replicated, may hold values from -3 to 3
- time_gain: float32 [384], replicated, may hold values from 0.5 to 2
- time_qkv: bfloat16 [384, 1536], replicated
- time_out: bfloat16 [512, 384], replicated, may hold values from -2 to 2
- band_gain: float32 [384], replicated, may hold values from 0.5 to 2
- band_qkv: bfloat16 [384, 1536], replicated
- band_out: bfloat16 [512, 384], replicated, may hold values from -1 to 1
- cotangent: bfloat16 [4, 2048, 32, 384], P('song', 'seq'), may hold values from -0.125 to 0.125
Outputs:
- features_out: bfloat16 [4, 2048, 32, 384], P('song', 'seq')
- out_grad: float32 [512, 384], replicated
The draws below stay inside these ranges and needn't reach their ends.
Inputs may be any that keep to these rules, and one draw needn't show every extreme that they name: The widths sum to 2049, each is at least 4, one is exactly 257. Frames from lengths[s] on are padding; at least one song fills all 2048 frames.
All inputs are finite; a program needn't handle non-finite values.
Results may differ from the reference program's by a relative error of at most 0.024.
The reference program's roundings to bfloat16 on the way count: a program that leaves them out, or rounds other values in their place, can miss the bound.
Values may be sent and summed in bfloat16 or wider, within the bound.
A program may use at most 192 MiB of HBM per device.

```python
import math
import jax
import jax.numpy as jnp
from jax import lax

BINS = 2049
BANDS = 32
WMAX = 257
D = 384
HEADS = 8
DH = 64
FEAT = 8196
INNER = 512
FRAMES = 2048
SONGS = 4


def draw_widths(key, part):
    key = jax.random.fold_in(key, 1)
    key_dev, key_perm = jax.random.split(key, 2)
    rest_bins = BINS - WMAX
    pair_count = (BANDS - 2) // 2
    base_width = rest_bins // (BANDS - 1)
    single_width = rest_bins - base_width * 2 * pair_count
    spread_max = base_width - 4
    deviation = jax.random.randint(key_dev, (pair_count,), -spread_max, spread_max + 1, dtype=jnp.int32)
    values_all = jnp.concatenate([jnp.array([WMAX, single_width], jnp.int32), base_width + deviation, base_width - deviation])
    order_perm = jax.random.permutation(key_perm, BANDS)
    return values_all[order_perm].astype(jnp.int32)


def draw_lengths(key, part):
    key = jax.random.fold_in(key, 2)
    key_len, key_full = jax.random.split(key, 2)
    drawn = jax.random.randint(key_len, (SONGS,), FRAMES // 2, FRAMES + 1, dtype=jnp.int32)
    full_song = jax.random.randint(key_full, (), 0, SONGS, dtype=jnp.int32)
    return jnp.where(jnp.arange(SONGS, dtype=jnp.int32) == full_song, FRAMES, drawn).astype(jnp.int32)


def qkv_weights(key, strength):
    key_q, key_k, key_v, key_lift, key_pick = jax.random.split(key, 5)
    inner_width = HEADS * DH
    base_q = jax.random.normal(key_q, (D, inner_width), jnp.float32) / jnp.sqrt(float(D))
    base_k = jax.random.normal(key_k, (D, inner_width), jnp.float32) / jnp.sqrt(float(D))
    base_v = jax.random.normal(key_v, (D, inner_width), jnp.float32) / jnp.sqrt(float(D))
    head_of = jnp.arange(inner_width) // DH
    picked = (jax.random.uniform(key_pick, (HEADS,)) < 0.5).astype(jnp.float32)
    lifted = 3.0 + 3.0 * jax.random.uniform(key_lift, (HEADS,))
    factor = (1.0 + picked * (lifted - 1.0))[head_of]
    share = picked[head_of]
    scaling = 1.0 + strength * (factor - 1.0)
    query_part = base_q * scaling
    key_part = base_k * (1.0 - 0.7 * strength * share) * scaling
    return jnp.concatenate([query_part, key_part, base_v], axis=1).astype(jnp.bfloat16)


def draw_time_qkv(key, part):
    key = jax.random.fold_in(key, 5)
    return qkv_weights(key, 0.0)


def draw_band_qkv(key, part):
    key = jax.random.fold_in(key, 7)
    return qkv_weights(key, 0.0)


def steps_of(key, dims, pieces, smallest, high):
    def one(axis_at, blocks):
        draws = jax.random.uniform(jax.random.fold_in(jax.random.fold_in(key, 6), axis_at), (blocks,), jnp.float32, smallest / len(pieces), high / len(pieces))
        return jnp.repeat(jnp.exp(draws), dims[axis_at] // blocks).reshape((-1,) + (1,) * (len(dims) - axis_at - 1))

    factor_of = one(*pieces[0])
    for cut in pieces[1:]:
        factor_of = factor_of * one(*cut)
    return factor_of


def scatter_about(rng, dims, width, most, shards=(), kind=jnp.bfloat16):
    values = width * jax.random.normal(rng, dims, jnp.float32)
    if shards:
        values = values * steps_of(rng, dims, shards, -0.22, 0.18)
    return jnp.clip(values, -most, most).astype(kind)


def setup_inputs(seed: int = 0) -> dict:
    key_list = jax.random.split(jax.random.key(seed), 14)
    return {
        "spectrum": scatter_about(key_list[0], (SONGS, FRAMES, FEAT), 1.0, 6.0, ((0, 4), (1, 32))),
        "widths": draw_widths(jax.random.fold_in(key_list[13], 71), 0),
        "lengths": draw_lengths(jax.random.fold_in(key_list[13], 71), 0),
        "bin_gain": jnp.clip(jnp.exp(jax.random.uniform(key_list[3], (FEAT,), jnp.float32, math.log(0.5), math.log(2.0))), 0.5, 2.0),
        "embed_weight": scatter_about(key_list[4], (FEAT, D), (4 * (BINS // BANDS)) ** -0.5, 0.375),
        "embed_bias": scatter_about(key_list[5], (BANDS, D), 0.5, 3.0, (), jnp.float32),
        "time_gain": jnp.clip(jnp.exp(jax.random.uniform(key_list[6], (D,), jnp.float32, math.log(0.5), math.log(2.0))), 0.5, 2.0),
        "time_qkv": draw_time_qkv(jax.random.fold_in(key_list[13], 71), 0),
        "time_out": scatter_about(key_list[8], (INNER, D), (max(INNER // 64, 1)) ** -0.5, 2.0),
        "band_gain": jnp.clip(jnp.exp(jax.random.uniform(key_list[9], (D,), jnp.float32, math.log(0.5), math.log(2.0))), 0.5, 2.0),
        "band_qkv": draw_band_qkv(jax.random.fold_in(key_list[13], 71), 0),
        "band_out": scatter_about(key_list[11], (INNER, D), (max(INNER // 16, 1)) ** -0.5, 1.0),
        "cotangent": scatter_about(key_list[12], (SONGS, FRAMES, BANDS, D), (4.0 / (SONGS * FRAMES * BANDS) ** 0.5), 0.125, ((0, 4), (1, 32))),
    }


FLOOR = 0.25
EPSILON = 1e-05

def rotate(values, position):
    half_dim = values.shape[-1] // 2
    frequency = jnp.exp(-(2.0 * jnp.arange(half_dim, dtype=jnp.float32) / values.shape[-1]) * jnp.log(10000.0))
    angles = position[..., None, None] * frequency
    cosine = jnp.cos(angles)
    sines = jnp.sin(angles)
    leading = values[..., :half_dim]
    second = values[..., half_dim:]
    return jnp.concatenate([leading * cosine - second * sines, second * cosine + leading * sines], axis=-1)

def norm_rows(inputs, gain):
    floats = inputs.astype(jnp.float32)
    square = lax.optimization_barrier(jnp.mean(floats * floats, axis=-1, keepdims=True))
    return (floats * lax.rsqrt(square + EPSILON) * gain).astype(jnp.bfloat16)

def softmax_rows(scores):
    maximum = lax.optimization_barrier(jnp.max(scores, axis=-1, keepdims=True))
    powers = jnp.exp(scores - maximum)
    return (powers / lax.optimization_barrier(jnp.sum(powers, axis=-1, keepdims=True))).astype(jnp.bfloat16)

def reference(spectrum, widths, lengths, bin_gain, embed_weight, embed_bias, time_gain, time_qkv, time_out, band_gain, band_qkv, band_out, cotangent):
    songs_all, frame_count, feature_count = spectrum.shape
    bin_count = feature_count // 4
    band_count = widths.shape[0]
    model_width = embed_weight.shape[1]
    inner_width = time_out.shape[0]
    head_size = inner_width // HEADS
    slice_width = WMAX * 4
    attn_scale = head_size ** (-0.5)
    starts = (jnp.cumsum(widths) - widths).astype(jnp.int32)
    bin_index = jnp.arange(bin_count, dtype=jnp.int32)
    band_of_bin = lax.optimization_barrier(jnp.sum((bin_index[:, None] >= starts[None, :]).astype(jnp.int32), axis=1)) - 1
    onehot = (band_of_bin[:, None] == jnp.arange(band_count, dtype=jnp.int32)[None, :]).astype(jnp.float32)
    bin_rows = spectrum.reshape(songs_all * frame_count, bin_count, 4).astype(jnp.float32)
    bin_square = lax.optimization_barrier(jnp.sum(bin_rows * bin_rows, axis=2))
    band_square = jnp.dot(bin_square, onehot, precision=lax.Precision.HIGHEST) / (4 * widths).astype(jnp.float32)
    band_scale = 1.0 / jnp.sqrt(jnp.maximum(band_square, FLOOR))
    bin_scale = jnp.dot(band_scale, onehot.T, precision=lax.Precision.HIGHEST)
    normed = (bin_rows * bin_scale[:, :, None] * bin_gain.reshape(bin_count, 4)).astype(jnp.bfloat16)
    normed = normed.reshape(songs_all * frame_count, feature_count)
    normed_pad = jnp.concatenate([normed, jnp.zeros((normed.shape[0], slice_width), jnp.bfloat16)], axis=1)
    weight_pad = jnp.concatenate([embed_weight, jnp.zeros((slice_width, model_width), jnp.bfloat16)], axis=0)
    column = jnp.arange(slice_width, dtype=jnp.int32)

    def embed_band(band_id):
        offset = (starts[band_id] * 4).astype(jnp.int32)
        band_piece = lax.dynamic_slice_in_dim(normed_pad, offset, slice_width, 1)
        band_piece = jnp.where((column < widths[band_id] * 4)[None, :], band_piece, jnp.zeros_like(band_piece))
        weight_rows = lax.dynamic_slice_in_dim(weight_pad, offset, slice_width, 0)
        summed = jnp.dot(band_piece, weight_rows, preferred_element_type=jnp.float32) + embed_bias[band_id]
        return summed.astype(jnp.bfloat16)
    embedded = lax.map(embed_band, jnp.arange(band_count, dtype=jnp.int32))
    sequences = embedded.reshape(band_count, songs_all, frame_count, model_width).transpose(1, 0, 2, 3)
    sequences = sequences.reshape(songs_all * band_count, frame_count, model_width)
    song_length = jnp.repeat(lengths, band_count)
    frame_pos = jnp.arange(frame_count, dtype=jnp.float32)
    frame_index = jnp.arange(frame_count, dtype=jnp.int32)

    def time_pass(pair_item):
        sequence, length = pair_item
        normal_rows = norm_rows(sequence, time_gain)
        project = jnp.dot(normal_rows, time_qkv, preferred_element_type=jnp.float32)
        queries = rotate(project[:, :inner_width].reshape(frame_count, HEADS, head_size), frame_pos).astype(jnp.bfloat16)
        key_rows = rotate(project[:, inner_width:2 * inner_width].reshape(frame_count, HEADS, head_size), frame_pos).astype(jnp.bfloat16)
        values_v = project[:, 2 * inner_width:].reshape(frame_count, HEADS, head_size).astype(jnp.bfloat16)
        scores = jnp.einsum('qhd,khd->hqk', queries.astype(jnp.float32), key_rows.astype(jnp.float32)) * attn_scale
        scores = jnp.where((frame_index < length)[None, None, :], scores, -1e+30)
        weights = softmax_rows(scores)
        head_out = jnp.einsum('hqk,khd->qhd', weights.astype(jnp.float32), values_v.astype(jnp.float32))
        head_out = head_out.astype(jnp.bfloat16).reshape(frame_count, inner_width)
        mixed = sequence.astype(jnp.float32) + jnp.dot(head_out, time_out, preferred_element_type=jnp.float32)
        return mixed.astype(jnp.bfloat16)
    timed = lax.map(time_pass, (sequences, song_length))
    timed = timed.reshape(songs_all, band_count, frame_count, model_width).transpose(0, 2, 1, 3)
    band_pos = jnp.arange(band_count, dtype=jnp.float32)[None, :]

    def band_pass(pair_item):
        frame_rows, tangent, length = pair_item
        normal_rows = norm_rows(frame_rows, band_gain)
        project = jnp.dot(normal_rows.reshape(-1, model_width), band_qkv, preferred_element_type=jnp.float32)
        project = project.reshape(frame_count, band_count, 3 * inner_width)
        queries = rotate(project[..., :inner_width].reshape(frame_count, band_count, HEADS, head_size), band_pos).astype(jnp.bfloat16)
        key_rows = rotate(project[..., inner_width:2 * inner_width].reshape(frame_count, band_count, HEADS, head_size), band_pos).astype(jnp.bfloat16)
        values_v = project[..., 2 * inner_width:].reshape(frame_count, band_count, HEADS, head_size).astype(jnp.bfloat16)
        scores = jnp.einsum('fbhd,fchd->fhbc', queries.astype(jnp.float32), key_rows.astype(jnp.float32)) * attn_scale
        weights = softmax_rows(scores)
        head_out = jnp.einsum('fhbc,fchd->fbhd', weights.astype(jnp.float32), values_v.astype(jnp.float32))
        head_out = head_out.astype(jnp.bfloat16).reshape(frame_count, band_count, inner_width)
        projected = jnp.dot(head_out.reshape(-1, inner_width), band_out, preferred_element_type=jnp.float32)
        output = (frame_rows.astype(jnp.float32) + projected.reshape(frame_count, band_count, model_width)).astype(jnp.bfloat16)
        live_frame = (frame_index < length)[:, None, None]
        masked = jnp.where(live_frame, head_out, jnp.zeros_like(head_out))
        gradient = jnp.dot(masked.reshape(-1, inner_width).T, tangent.reshape(-1, model_width), preferred_element_type=jnp.float32)
        return (output, gradient)
    outputs, gradients = lax.map(band_pass, (timed, cotangent, lengths))
    return (outputs, lax.optimization_barrier(jnp.sum(gradients, axis=0)))
```

```python
import functools

import jax
import jax.numpy as jnp
import numpy as np
from jax import lax
from jax.experimental import pallas as pl
from jax.experimental.pallas import tpu as pltpu
from jax.sharding import PartitionSpec as P

HEADS = 8
DH = 64
HALF = DH // 2
GROUP = 4 * DH
FLOOR = 0.25
EPSILON = 1e-05
LOG2E = 1.4426950408889634
WINDOW = 1152
NT = (((1,), (1,)), ((), ()))
TN = (((0,), (0,)), ((), ()))
MESH = pl.DeviceIdType.MESH
BF = jnp.bfloat16
F32 = jnp.float32
SAFE = 60.0
VSAFE = 2.0**40
VMEM = pltpu.VMEM
LIMIT = 56 * 2**20


def whole():
    return pl.BlockSpec(memory_space=pltpu.VMEM)


def smem():
    return pl.BlockSpec(memory_space=pltpu.SMEM)


def rotary_tables(positions, repeat):
    frequency = np.exp(-(2.0 * np.arange(HALF, dtype=np.float64) / DH) * np.log(10000.0))
    angles = positions.astype(np.float64)[:, None] * frequency
    cosine = np.tile(np.cos(angles), (1, repeat)).astype(np.float32)
    sines = np.tile(np.sin(angles), (1, repeat)).astype(np.float32)
    return cosine, sines


def split_halves(weights):
    row = lax.broadcasted_iota(jnp.int32, (GROUP, GROUP), 0)
    col = lax.broadcasted_iota(jnp.int32, (GROUP, GROUP), 1)
    source = (col % 128) // HALF * DH + col // 128 * HALF + col % HALF
    one_hot = (row == source).astype(F32).astype(BF)
    return jnp.dot(weights, one_hot, preferred_element_type=F32).astype(BF)


def rms_norm(rows, gain):
    square = jnp.mean(rows * rows, axis=-1, keepdims=True)
    return (rows * lax.rsqrt(square + EPSILON) * gain).astype(BF)


def rope(values, cosine, sines):
    leading = values[:, :128]
    second = values[:, 128:]
    return leading * cosine - second * sines, second * cosine + leading * sines


def embed_kernel(bands, limit, meta_ref, x_ref, gain_ref, w_ref, xt_ref, gt_ref, wt_ref, bias_ref, out_ref):
    lane = lax.broadcasted_iota(jnp.int32, (1, WINDOW), 1)

    def band(k, last):
        first = meta_ref[0, k]
        end = meta_ref[1, k]
        begin = pl.multiple_of(meta_ref[2, k] * 128, 128)
        window = pl.ds(begin, WINDOW)
        entry = lane + begin
        piece = x_ref[:, window].astype(F32)
        piece = jnp.where((entry >= first) & (entry < end), piece, 0.0)
        total = jnp.sum(piece * piece, axis=1, keepdims=True)
        if last:
            tail = xt_ref[...].astype(F32)
            total = total + jnp.sum(tail * tail, axis=1, keepdims=True)
        mean = total / (end - first + (limit - first - (end - first) if last else 0)).astype(F32)
        scale = 1.0 / jnp.sqrt(jnp.maximum(mean, FLOOR))
        normed = (piece * scale * gain_ref[:, window]).astype(BF)
        summed = jnp.dot(normed, w_ref[window, :], preferred_element_type=F32)
        if last:
            normed = (tail * scale * gt_ref[...]).astype(BF)
            summed = summed + jnp.dot(normed, wt_ref[...], preferred_element_type=F32)
        out_ref[k] = (summed + bias_ref[pl.ds(k, 1), :]).astype(BF)

    def step(i, carry):
        for j in range(4):
            band(i * 4 + j, False)
        return carry

    lax.fori_loop(0, bands // 4 - 1, step, 0)
    for k in range(bands - 4, bands - 1):
        band(k, False)
    band(bands - 1, True)


def embed(spectrum, widths, bin_gain, embed_weight, embed_bias):
    frames, feature_count = spectrum.shape
    bands, width = embed_bias.shape
    main = feature_count // 128 * 128
    tail = feature_count - main
    starts = (jnp.cumsum(widths) - widths) * 4
    ends = jnp.minimum(starts + widths * 4, main)
    begins = jnp.minimum(starts // 128, (main - WINDOW) // 128)
    meta = jnp.stack([starts, ends, begins]).astype(jnp.int32)
    x_tail = jnp.pad(spectrum[:, main:], ((0, 0), (0, 128 - tail)))
    gain_tail = jnp.pad(bin_gain[main:], (0, 128 - tail))[None]
    w_tail = jnp.pad(embed_weight[main:], ((0, 128 - tail), (0, 0)))
    return pl.pallas_call(
        functools.partial(embed_kernel, bands, feature_count),
        out_shape=jax.ShapeDtypeStruct((bands, frames, width), BF),
        in_specs=[smem()] + [whole()] * 7,
        out_specs=whole(),
        compiler_params=pltpu.CompilerParams(vmem_limit_bytes=LIMIT),
        cost_estimate=pl.CostEstimate(flops=2 * 10**9, bytes_accessed=9 * 10**6, transcendentals=0),
    )(meta, spectrum, bin_gain[None], embed_weight, x_tail, gain_tail, w_tail, embed_bias)


VROWS = 80


def time_kernel(columns, length_ref, x_ref, gain_ref, wqkv_ref, wout_ref, cos_ref, sin_ref, out_ref, q_ref, k_ref, v_ref, heads_ref):
    frames, width = x_ref.shape
    inner = HEADS * DH
    length = length_ref[0]
    rows_each = 512
    lane = lax.broadcasted_iota(jnp.int32, (1, GROUP), 1)
    wq = [split_halves(wqkv_ref[:, g * GROUP : (g + 1) * GROUP]) for g in range(2)]
    wk = [split_halves(wqkv_ref[:, inner + g * GROUP : inner + (g + 1) * GROUP]) for g in range(2)]
    wv = wqkv_ref[:, 2 * inner :]
    bound = jnp.zeros((1, 1), F32)
    vmost = jnp.zeros((1, 1), F32)
    first_key = [None, None]
    qmost = [jnp.zeros((1, 1), F32)] * HEADS
    kmost = [jnp.zeros((1, 1), F32)] * HEADS
    for b in range(frames // rows_each):
        rows = slice(b * rows_each, (b + 1) * rows_each)
        normed = rms_norm(x_ref[rows, :].astype(F32), gain_ref[...])
        cosine = cos_ref[rows, :]
        sines = sin_ref[rows, :]
        alive_row = (lax.broadcasted_iota(jnp.int32, (rows_each, 1), 0) + b * rows_each) < length
        alive_col = (lax.broadcasted_iota(jnp.int32, (1, rows_each), 1) + b * rows_each) < length
        for g in range(2):
            qa, qb = rope(jnp.dot(normed, wq[g], preferred_element_type=F32), cosine, sines)
            scaled = jnp.concatenate([qa, qb], axis=1) * (LOG2E * DH**-0.5)
            q_ref[g, rows, :] = scaled.astype(BF)
            ka, kb = rope(jnp.dot(normed, wk[g], preferred_element_type=F32), cosine, sines)
            keys = jnp.concatenate([ka, kb], axis=1)
            if b == 0:
                first_key[g] = keys[:1]
            keys = jnp.where(alive_row, keys, first_key[g])
            k_ref[g, rows, :] = keys.astype(BF)
            qq = scaled * scaled
            kk = keys * keys
            for h in range(4):
                mine = (lane % 128) // HALF == h
                qn = jnp.max(jnp.sum(jnp.where(mine, qq, 0.0), axis=1, keepdims=True), axis=0, keepdims=True)
                kn = jnp.max(jnp.sum(jnp.where(mine, kk, 0.0), axis=1, keepdims=True), axis=0, keepdims=True)
                qmost[4 * g + h] = jnp.maximum(qmost[4 * g + h], qn)
                kmost[4 * g + h] = jnp.maximum(kmost[4 * g + h], kn)
        values = lax.dot_general(wv, normed, (((0,), (1,)), ((), ())), preferred_element_type=F32)
        values = jnp.where(alive_col, values, 0.0)
        vmost = jnp.maximum(vmost, jnp.max(jnp.max(jnp.abs(values), axis=0, keepdims=True), axis=1, keepdims=True))
        values = values.astype(BF)
        ones = jnp.broadcast_to(jnp.where(alive_col, 1.0, 0.0), (VROWS - DH, rows_each)).astype(BF)
        for h in range(HEADS):
            v_ref[h, :DH, rows] = values[h * DH : (h + 1) * DH]
            v_ref[h, DH:, rows] = ones
    for h in range(HEADS):
        bound = jnp.maximum(bound, qmost[h] * kmost[h])
    fits = (jnp.max(bound) * 1.05 < SAFE * SAFE) & (jnp.max(vmost) < VSAFE)

    def attend(shift):
        def block(qb, carry):
            rows = pl.ds(pl.multiple_of(qb * columns, columns), columns)

            def head(h, inner_carry):
                g = h // 4
                mine = (lane % 128) // HALF == h % 4
                queries = jnp.where(mine, q_ref[g, rows, :], jnp.zeros((), BF))
                scores = lax.dot_general(k_ref[g], queries, NT, preferred_element_type=F32)
                if shift:
                    scores = scores - jnp.max(scores, axis=0, keepdims=True)
                powers = jnp.exp2(scores).astype(BF)
                mixed = jnp.dot(v_ref[h], powers, preferred_element_type=F32)
                mixed = mixed[:DH] / mixed[DH : DH + 1]
                heads_ref[pl.ds(pl.multiple_of(h * DH, DH), DH), :] = mixed.astype(BF)
                return inner_carry

            lax.fori_loop(0, HEADS, head, 0)
            projected = lax.dot_general(heads_ref[...], wout_ref[...], TN, preferred_element_type=F32)
            out_ref[rows, :] = (x_ref[rows, :].astype(F32) + projected).astype(BF)
            return carry

        lax.fori_loop(0, frames // columns, block, 0)

    @pl.when(fits)
    def _():
        attend(False)

    @pl.when(jnp.logical_not(fits))
    def _():
        attend(True)


def time_attention(sequence, lengths, gain, wqkv, wout):
    frames, width = sequence.shape
    columns = min(1024, frames)
    cosine, sines = rotary_tables(np.arange(frames), 4)
    return pl.pallas_call(
        functools.partial(time_kernel, columns),
        out_shape=jax.ShapeDtypeStruct((frames, width), BF),
        in_specs=[smem()] + [whole()] * 6,
        out_specs=whole(),
        scratch_shapes=[
            VMEM((2, frames, GROUP), BF),
            VMEM((2, frames, GROUP), BF),
            VMEM((HEADS, VROWS, frames), BF),
            VMEM((HEADS * DH, columns), BF),
        ],
        compiler_params=pltpu.CompilerParams(vmem_limit_bytes=LIMIT),
        cost_estimate=pl.CostEstimate(flops=4 * 10**10, bytes_accessed=6 * 10**6, transcendentals=0),
    )(lengths, sequence, gain[None], wqkv, wout, jnp.asarray(cosine), jnp.asarray(sines))


FRAMES_EACH = 16


def band_kernel(place_ref, x_ref, gain_ref, wqkv_ref, wout_ref, cot_ref, cos_ref, sin_ref, out_ref, grad_ref, heads_ref):
    bands, frames, width = x_ref.shape
    inner = HEADS * DH
    rows = bands * FRAMES_EACH
    half = 256
    lane = lax.broadcasted_iota(jnp.int32, (1, GROUP), 1)
    lane128 = lax.broadcasted_iota(jnp.int32, (1, 128), 1)
    wq = [split_halves(wqkv_ref[:, g * GROUP : (g + 1) * GROUP]) for g in range(2)]
    wk = [split_halves(wqkv_ref[:, inner + g * GROUP : inner + (g + 1) * GROUP]) for g in range(2)]
    wv = wqkv_ref[:, 2 * inner :]
    length = place_ref[0]
    base = place_ref[1]
    to = lax.broadcasted_iota(jnp.int32, (rows, rows), 0)
    src = lax.broadcasted_iota(jnp.int32, (rows, rows), 1)
    order = (src == to % bands * FRAMES_EACH + to // bands).astype(F32).astype(BF)
    same = lax.broadcasted_iota(jnp.int32, (half, half), 0) // bands == lax.broadcasted_iota(jnp.int32, (half, half), 1) // bands
    grad_ref[...] = jnp.zeros_like(grad_ref)

    def block(i, carry):
        piece = x_ref[:, pl.ds(pl.multiple_of(i * FRAMES_EACH, FRAMES_EACH), FRAMES_EACH), :].reshape(rows, width)
        x = jnp.dot(order, piece, preferred_element_type=F32)
        normed = rms_norm(x, gain_ref[...])
        cosine = cos_ref[...]
        sines = sin_ref[...]
        values = jnp.dot(normed, wv, preferred_element_type=F32)
        for g in range(2):
            qa, qb = rope(jnp.dot(normed, wq[g], preferred_element_type=F32), cosine, sines)
            queries = (jnp.concatenate([qa, qb], axis=1) * (LOG2E * DH**-0.5)).astype(BF)
            ka, kb = rope(jnp.dot(normed, wk[g], preferred_element_type=F32), cosine, sines)
            keys = jnp.concatenate([ka, kb], axis=1).astype(BF)
            for s in range(rows // half):
                part = slice(s * half, (s + 1) * half)
                for pair in range(2):
                    column = (2 * g + pair) * 128
                    v = values[part, column : column + 128]
                    outs = []
                    for odd in range(2):
                        mine = (lane % 128) // HALF == 2 * pair + odd
                        masked = jnp.where(mine, queries[part], jnp.zeros((), BF))
                        scores = lax.dot_general(masked, keys[part], NT, preferred_element_type=F32)
                        scores = jnp.where(same, scores, -1e30)
                        powers = jnp.exp2(scores - jnp.max(scores, axis=1, keepdims=True)).astype(BF)
                        own = (lane128 < DH) if odd == 0 else (lane128 >= DH)
                        extended = jnp.where(own, v, 1.0).astype(BF)
                        mixed = jnp.dot(powers, extended, preferred_element_type=F32)
                        outs.append(mixed / pltpu.roll(mixed, DH, 1))
                    joined = jnp.where(lane128 < DH, outs[0], outs[1])
                    heads_ref[part, column : column + 128] = joined.astype(BF)
        heads = heads_ref[...]
        projected = jnp.dot(heads, wout_ref[...], preferred_element_type=F32)
        here = pl.ds(pl.multiple_of(i * rows, rows), rows)
        out_ref[here, :] = (x + projected).astype(BF)
        frame = base + i * FRAMES_EACH + lax.broadcasted_iota(jnp.int32, (rows, 1), 0) // bands
        tangent = jnp.where(frame < length, cot_ref[here, :].astype(F32), 0.0).astype(BF)
        grad_ref[...] += lax.dot_general(heads, tangent, TN, preferred_element_type=F32)
        return carry

    lax.fori_loop(0, frames // FRAMES_EACH, block, 0)


def band_attention(returned, place, gain, wqkv, wout, cotangent):
    bands, frames, width = returned.shape
    inner = HEADS * DH
    rows = bands * FRAMES_EACH
    cosine, sines = rotary_tables(np.tile(np.arange(bands), FRAMES_EACH), 4)
    return pl.pallas_call(
        band_kernel,
        out_shape=(
            jax.ShapeDtypeStruct((frames * bands, width), BF),
            jax.ShapeDtypeStruct((inner, width), F32),
        ),
        in_specs=[smem()] + [whole()] * 7,
        out_specs=(whole(), whole()),
        scratch_shapes=[VMEM((rows, inner), BF)],
        compiler_params=pltpu.CompilerParams(vmem_limit_bytes=LIMIT),
        cost_estimate=pl.CostEstimate(flops=10**10, bytes_accessed=7 * 10**6, transcendentals=0),
    )(place, returned, gain[None], wqkv, wout, cotangent.reshape(frames * bands, width), jnp.asarray(cosine), jnp.asarray(sines))


def sum_kernel(seq, songs, part_ref, out_ref, small, got, mid, full, send1, recv1, send2, recv2, send3, recv3):
    me = lax.axis_index("seq")
    song = lax.axis_index("song")
    rows = small.shape[1]
    barrier = pltpu.get_barrier_semaphore()

    def greet(d, carry):
        pl.semaphore_signal(barrier, inc=1, device_id=(lax.rem(me + d, seq), song), device_id_type=MESH)
        return carry

    lax.fori_loop(1, seq, greet, 0)
    for d in range(1, songs):
        pl.semaphore_signal(barrier, inc=1, device_id=(me, lax.rem(song + d, songs)), device_id_type=MESH)
    for r in range(seq):
        small[r] = part_ref[r * rows : (r + 1) * rows, :].astype(BF)
    pl.semaphore_wait(barrier, seq - 1 + songs - 1)

    def first(d):
        peer = lax.rem(me + d, seq)
        return pltpu.make_async_remote_copy(
            src_ref=small.at[peer], dst_ref=got.at[d], send_sem=send1.at[d], recv_sem=recv1.at[d],
            device_id=(peer, song), device_id_type=MESH)

    def start1(d, carry):
        first(d).start()
        return carry

    def wait1(d, carry):
        first(d).wait()
        return carry

    lax.fori_loop(1, seq, start1, 0)
    got[0] = small[me]
    lax.fori_loop(1, seq, wait1, 0)
    total = got[0].astype(F32)
    for d in range(1, seq):
        total = total + got[d].astype(F32)
    mid[song] = total
    copies = []
    for d in range(1, songs):
        copies.append(pltpu.make_async_remote_copy(
            src_ref=mid.at[song], dst_ref=mid.at[song], send_sem=send2.at[d], recv_sem=recv2.at[d],
            device_id=(me, lax.rem(song + d, songs)), device_id_type=MESH))
    for c in copies:
        c.start()
    for c in copies:
        c.wait()
    total = mid[0]
    for s in range(1, songs):
        total = total + mid[s]
    full[me] = total.astype(BF)

    def third(d):
        return pltpu.make_async_remote_copy(
            src_ref=full.at[me], dst_ref=full.at[me], send_sem=send3.at[d], recv_sem=recv3.at[d],
            device_id=(lax.rem(me + d, seq), song), device_id_type=MESH)

    def start3(d, carry):
        third(d).start()
        return carry

    def wait3(d, carry):
        third(d).wait()
        return carry

    lax.fori_loop(1, seq, start3, 0)
    lax.fori_loop(1, seq, wait3, 0)
    for r in range(seq):
        out_ref[r * rows : (r + 1) * rows, :] = full[r].astype(F32)


def gradient_sum(partial):
    seq = lax.axis_size("seq")
    songs = lax.axis_size("song")
    inner, width = partial.shape
    rows = inner // seq
    dma = pltpu.SemaphoreType.DMA
    return pl.pallas_call(
        functools.partial(sum_kernel, seq, songs),
        out_shape=jax.ShapeDtypeStruct((inner, width), F32),
        in_specs=[whole()],
        out_specs=whole(),
        scratch_shapes=[
            VMEM((seq, rows, width), BF),
            VMEM((seq, rows, width), BF),
            VMEM((songs, rows, width), F32),
            VMEM((seq, rows, width), BF),
            dma((seq,)), dma((seq,)), dma((songs,)), dma((songs,)), dma((seq,)), dma((seq,)),
        ],
        compiler_params=pltpu.CompilerParams(collective_id=0, has_side_effects=True, vmem_limit_bytes=LIMIT),
        cost_estimate=pl.CostEstimate(flops=10**7, bytes_accessed=4 * 10**6, transcendentals=0),
    )(partial)


def per_device(spectrum, widths, lengths, bin_gain, embed_weight, embed_bias, time_gain, time_qkv, time_out, band_gain, band_qkv, band_out, cotangent):
    local_frames = spectrum.shape[1]
    bands, width = embed_bias.shape
    computed = embed(spectrum[0], widths, bin_gain, embed_weight, embed_bias)
    owned = lax.all_to_all(computed, "seq", split_axis=0, concat_axis=1, tiled=True)
    timed = time_attention(owned[0], lengths, time_gain, time_qkv, time_out)
    returned = lax.all_to_all(timed.reshape(-1, local_frames, width), "seq", split_axis=0, concat_axis=0, tiled=True)
    place = jnp.stack([lengths[0], lax.axis_index("seq") * local_frames]).astype(jnp.int32)
    output, partial = band_attention(returned, place, band_gain, band_qkv, band_out, cotangent[0])
    gradient = gradient_sum(partial)
    return output.reshape(1, local_frames, bands, width), gradient


def solution(mesh):
    return jax.shard_map(
        per_device,
        mesh=mesh,
        in_specs=(P("song", "seq", None), P(), P("song"), P(), P(), P(), P(), P(), P(), P(), P(), P(), P("song", "seq", None, None)),
        out_specs=(P("song", "seq", None, None), P()),
        check_vma=False,
    )
```

```python
import functools

import jax
import jax.numpy as jnp
import numpy as np
from jax import lax
from jax.experimental import pallas as pl
from jax.experimental.pallas import tpu as pltpu
from jax.sharding import PartitionSpec as P

HEADS = 8
DH = 64
HALF = DH // 2
GROUP = 4 * DH
FLOOR = 0.25
EPSILON = 1e-05
LOG2E = 1.4426950408889634
WINDOW = 1152
NT = (((1,), (1,)), ((), ()))
TN = (((0,), (0,)), ((), ()))
MESH = pl.DeviceIdType.MESH
BF = jnp.bfloat16
F32 = jnp.float32
SAFE = 100.0
VSAFE = 2.0**12
VMEM = pltpu.VMEM
LIMIT = 56 * 2**20


def whole():
    return pl.BlockSpec(memory_space=pltpu.VMEM)


def smem():
    return pl.BlockSpec(memory_space=pltpu.SMEM)


def rotary_tables(positions, repeat):
    frequency = np.exp(-(2.0 * np.arange(HALF, dtype=np.float64) / DH) * np.log(10000.0))
    angles = positions.astype(np.float64)[:, None] * frequency
    cosine = np.tile(np.cos(angles), (1, repeat)).astype(np.float32)
    sines = np.tile(np.sin(angles), (1, repeat)).astype(np.float32)
    return cosine, sines


def split_halves(weights):
    row = lax.broadcasted_iota(jnp.int32, (GROUP, GROUP), 0)
    col = lax.broadcasted_iota(jnp.int32, (GROUP, GROUP), 1)
    source = (col % 128) // HALF * DH + col // 128 * HALF + col % HALF
    one_hot = (row == source).astype(F32).astype(BF)
    return jnp.dot(weights, one_hot, preferred_element_type=F32).astype(BF)


def rms_norm(rows, gain):
    square = jnp.mean(rows * rows, axis=-1, keepdims=True)
    return (rows * lax.rsqrt(square + EPSILON) * gain).astype(BF)


def rope(values, cosine, sines):
    leading = values[:, :128]
    second = values[:, 128:]
    return leading * cosine - second * sines, second * cosine + leading * sines


NARROW = 640


def embed_kernel(bands, meta_ref, x_ref, gain_ref, w_ref, bias_ref, out_ref):
    limit = x_ref.shape[1]
    main = limit // 128 * 128

    def band(k, size):
        first = meta_ref[0, k]
        count = meta_ref[1, k]
        begin = pl.multiple_of(jnp.minimum(meta_ref[2, k], (main - size) // 128) * 128, 128)
        window = pl.ds(begin, size)
        entry = lax.broadcasted_iota(jnp.int32, (1, size), 1) + begin
        piece = x_ref[:, window].astype(F32)
        piece = jnp.where((entry >= first) & (entry < first + count), piece, 0.0)
        tail = jnp.where(k == bands - 1, x_ref[:, main:].astype(F32), 0.0)
        square = jnp.sum(piece * piece, axis=1, keepdims=True) + jnp.sum(tail * tail, axis=1, keepdims=True)
        scale = 1.0 / jnp.sqrt(jnp.maximum(square / count.astype(F32), FLOOR))
        normed = (piece * scale * gain_ref[:, window]).astype(BF)
        summed = jnp.dot(normed, w_ref[window, :], preferred_element_type=F32) + bias_ref[pl.ds(k, 1), :]
        normed = (tail * scale * gain_ref[:, main:]).astype(BF).astype(F32)
        rows = w_ref[main:, :].astype(F32)
        for e in range(limit - main):
            summed = summed + normed[:, e : e + 1] * rows[e : e + 1, :]
        out_ref[k] = summed.astype(BF)

    def step(i, carry):
        narrow = meta_ref[1, 4 * i] <= NARROW - 124
        for j in range(1, 4):
            narrow = narrow & (meta_ref[1, 4 * i + j] <= NARROW - 124)

        @pl.when(narrow)
        def _():
            for j in range(4):
                band(4 * i + j, NARROW)

        @pl.when(jnp.logical_not(narrow))
        def _():
            for j in range(4):
                band(4 * i + j, WINDOW)

        return carry

    lax.fori_loop(0, bands // 4, step, 0)


def embed(spectrum, widths, bin_gain, embed_weight, embed_bias):
    frames, feature_count = spectrum.shape
    bands, width = embed_bias.shape
    starts = (jnp.cumsum(widths) - widths) * 4
    meta = jnp.stack([starts, widths * 4, starts // 128]).astype(jnp.int32)
    return pl.pallas_call(
        functools.partial(embed_kernel, bands),
        out_shape=jax.ShapeDtypeStruct((bands, frames, width), BF),
        in_specs=[smem()] + [whole()] * 4,
        out_specs=whole(),
        compiler_params=pltpu.CompilerParams(vmem_limit_bytes=32 * 2**20),
        cost_estimate=pl.CostEstimate(flops=2 * 10**9, bytes_accessed=9 * 10**6, transcendentals=0),
    )(meta, spectrum, bin_gain[None], embed_weight, embed_bias)


VROWS = 80


def exchange_kernel(
    seq, length_ref, bands_ref, gain_ref, wqkv_ref, cos_ref, sin_ref,
    x_ref, qa_ref, qb_ref, k_ref, v_ref, most_ref, got, send_sem, recv_sem,
):
    frames, width = got.shape[1:]
    half = frames // 2
    inner = HEADS * DH
    me = lax.axis_index("seq")
    song = lax.axis_index("song")
    y, x, core = me // 8, me // 2 % 4, me % 2

    def other(i, sign):
        return (y + sign * (i // 8) + 4) % 4 * 8 + (x + sign * (i // 2 % 4) + 4) % 4 * 2 + (core + i % 2) % 2

    barrier = pltpu.get_barrier_semaphore()

    def greet(i, carry):
        pl.semaphore_signal(barrier, inc=1, device_id=(other(i, 1), song), device_id_type=MESH)
        return carry

    lax.fori_loop(1, seq, greet, 0)
    lane = lax.broadcasted_iota(jnp.int32, (1, GROUP), 1)
    wq = [split_halves(wqkv_ref[:, g * GROUP : (g + 1) * GROUP]) for g in range(2)]
    wk = [split_halves(wqkv_ref[:, inner + g * GROUP : inner + (g + 1) * GROUP]) for g in range(2)]
    wv = wqkv_ref[:, 2 * inner :]
    pl.semaphore_wait(barrier, seq - 1)

    def copy(i):
        k = other(i, 1)
        return pltpu.make_async_remote_copy(
            src_ref=bands_ref.at[k], dst_ref=got.at[me], send_sem=send_sem.at[i], recv_sem=recv_sem.at[i],
            device_id=(k, song), device_id_type=MESH)

    def start(j, carry):
        copy(8 * (1 + 2 * (j % 2)) + j // 2).start()
        return carry

    def start_rest(j, carry):
        copy(16 + j).start()
        copy(j).start()
        return carry

    lax.fori_loop(0, 16, start, 0)
    copy(16).start()
    lax.fori_loop(1, 8, start_rest, 0)
    got[me] = bands_ref[me]
    length = length_ref[0]

    heads_of = lax.broadcasted_iota(jnp.int32, (GROUP, 128), 0) % 128 // HALF
    per_head = (heads_of == lax.broadcasted_iota(jnp.int32, (GROUP, 128), 1)).astype(F32).astype(BF)

    def longest(rows):
        squares = jnp.dot((rows * rows).astype(BF), per_head, preferred_element_type=F32)
        return jnp.max(squares, axis=0, keepdims=True)

    def project(dy, stats):
        row = (y - dy + 4) % 4

        def wait(i, carry):
            copy(8 * dy + i).wait_recv()
            return carry

        lax.fori_loop(1 if dy == 0 else 0, 8, wait, 0)
        owners = pl.ds(pl.multiple_of(row * 8, 8), 8)
        count = 8 * frames
        base = pl.multiple_of(row * count, count)
        rows = pl.ds(base, count)
        received = got[owners]
        x_ref[owners] = received
        normed = rms_norm(received.reshape(count, width).astype(F32), gain_ref[...])
        cosine = cos_ref[rows, :]
        sines = sin_ref[rows, :]
        alive_row = (lax.broadcasted_iota(jnp.int32, (count, 1), 0) + base) < length
        alive_col = (lax.broadcasted_iota(jnp.int32, (1, count), 1) + base) < length
        here = pl.ds(pl.multiple_of(row * 8 * half, 8 * half), 8 * half)
        kinds = []
        for g in range(2):
            qa, qb = rope(jnp.dot(normed, wq[g], preferred_element_type=F32), cosine, sines)
            scaled = jnp.concatenate([qa, qb], axis=1) * (LOG2E * DH**-0.5)
            parts = scaled.reshape(8, frames, GROUP)
            qa_ref[g, here, :] = parts[:, :half].reshape(8 * half, GROUP).astype(BF)
            qb_ref[g, here, :] = parts[:, half:].reshape(8 * half, GROUP).astype(BF)
            ka, kb = rope(jnp.dot(normed, wk[g], preferred_element_type=F32), cosine, sines)
            keys = jnp.concatenate([ka, kb], axis=1)
            keys = jnp.where(alive_row, keys, 0.0)
            k_ref[g, rows, :] = keys.astype(BF)
            kinds.append(longest(scaled))
            kinds.append(longest(keys))
        values = lax.dot_general(wv, normed, (((0,), (1,)), ((), ())), preferred_element_type=F32)
        values = jnp.where(alive_col, values, 0.0)
        vmost = jnp.max(jnp.max(jnp.abs(values), axis=0, keepdims=True), axis=1, keepdims=True)
        kinds.append(jnp.broadcast_to(vmost, (1, 128)))
        values = values.astype(BF)
        ones = jnp.broadcast_to(jnp.where(alive_col, 1.0, 0.0), (VROWS - DH, count)).astype(BF)
        for h in range(HEADS):
            v_ref[h, :DH, rows] = values[h * DH : (h + 1) * DH]
            v_ref[h, DH:, rows] = ones
        if stats is None:
            return kinds
        return [jnp.maximum(p, n) for p, n in zip(stats, kinds)]

    stats = None
    for dy in (1, 3, 0, 2):
        stats = project(dy, stats)
    for n, row in enumerate(stats):
        most_ref[n : n + 1, :] = row

    def finish(i, carry):
        copy(i).wait_send()
        return carry

    lax.fori_loop(1, seq, finish, 0)


def exchange(computed, lengths, gain, wqkv):
    seq = lax.axis_size("seq")
    bands, frames, width = computed.shape
    count = seq * frames
    cosine, sines = rotary_tables(np.arange(count), 4)
    dma = pltpu.SemaphoreType.DMA
    return pl.pallas_call(
        functools.partial(exchange_kernel, seq),
        out_shape=(
            jax.ShapeDtypeStruct((seq, frames, width), BF),
            jax.ShapeDtypeStruct((2, count // 2, GROUP), BF),
            jax.ShapeDtypeStruct((2, count // 2, GROUP), BF),
            jax.ShapeDtypeStruct((2, count, GROUP), BF),
            jax.ShapeDtypeStruct((HEADS, VROWS, count), BF),
            jax.ShapeDtypeStruct((5, 128), F32),
        ),
        in_specs=[smem()] + [whole()] * 5,
        out_specs=[whole()] * 6,
        scratch_shapes=[VMEM((seq, frames, width), BF), dma((seq,)), dma((seq,))],
        compiler_params=pltpu.CompilerParams(collective_id=1, has_side_effects=True, vmem_limit_bytes=TIME_LIMIT),
        cost_estimate=pl.CostEstimate(flops=4 * 10**9, bytes_accessed=10 * 10**6, transcendentals=0),
    )(lengths, computed, gain[None], wqkv, jnp.asarray(cosine), jnp.asarray(sines))


TIME_LIMIT = 36 * 2**20


def time_kernel(chunk, length_ref, most_ref, x_ref, wout_ref, q_ref, k_ref, v_ref, out_ref, heads_ref):
    owners, frames, width = x_ref.shape
    half = frames // 2
    lane = lax.broadcasted_iota(jnp.int32, (1, GROUP), 1)
    bound = jnp.maximum(most_ref[0:1, :] * most_ref[1:2, :], most_ref[2:3, :] * most_ref[3:4, :])
    fits = (jnp.max(bound) * 1.05 < SAFE * SAFE) & (jnp.max(most_ref[4:5, :]) < VSAFE)

    def attend(shift):
        def head(h, carry):
            g = h // 4
            mine = (lane % 128) // HALF == h % 4
            queries = jnp.where(mine, q_ref[g], jnp.zeros((), BF))
            scores = lax.dot_general(k_ref[g], queries, NT, preferred_element_type=F32)
            if shift:
                alive = lax.broadcasted_iota(jnp.int32, (owners * frames, 1), 0) < length_ref[0]
                scores = jnp.where(alive, scores, -1e30)
                scores = scores - jnp.max(scores, axis=0, keepdims=True)
            powers = jnp.exp2(scores).astype(BF)
            mixed = jnp.dot(v_ref[h], powers, preferred_element_type=F32)
            mixed = mixed[:DH] / mixed[DH : DH + 1]
            heads_ref[pl.ds(pl.multiple_of(h * DH, DH), DH), :] = mixed.astype(BF)
            return carry

        lax.fori_loop(0, HEADS, head, 0)

    @pl.when(fits)
    def _():
        attend(False)

    @pl.when(jnp.logical_not(fits))
    def _():
        attend(True)

    projected = lax.dot_general(heads_ref[...], wout_ref[...], TN, preferred_element_type=F32)
    before = x_ref[:, chunk * half : (chunk + 1) * half, :].astype(F32)
    out_ref[...] = (before + projected.reshape(owners, half, width)).astype(BF)


def time_attention(chunk, lengths, most, sequence, wout, q, k, v):
    owners, frames, width = sequence.shape
    return pl.pallas_call(
        functools.partial(time_kernel, chunk),
        out_shape=jax.ShapeDtypeStruct((owners, frames // 2, width), BF),
        in_specs=[smem()] + [whole()] * 6,
        out_specs=whole(),
        scratch_shapes=[VMEM((HEADS * DH, owners * frames // 2), BF)],
        compiler_params=pltpu.CompilerParams(vmem_limit_bytes=TIME_LIMIT),
        cost_estimate=pl.CostEstimate(flops=2 * 10**10, bytes_accessed=8 * 10**6, transcendentals=0),
    )(lengths, most, sequence, wout, q, k, v)


FRAMES_EACH = 16


def band_kernel(chunk, chunks, place_ref, x_ref, gain_ref, wqkv_ref, wout_ref, cot_ref, cos_ref, sin_ref, *rest):
    if chunk:
        before_ref, _, out_ref, grad_ref, heads_ref = rest
        grad_ref[...] = before_ref[...]
    else:
        out_ref, grad_ref, heads_ref = rest
        grad_ref[...] = jnp.zeros_like(grad_ref)
    bands, frames, width = x_ref.shape
    inner = HEADS * DH
    rows = bands * FRAMES_EACH
    half = 256
    lane = lax.broadcasted_iota(jnp.int32, (1, GROUP), 1)
    lane128 = lax.broadcasted_iota(jnp.int32, (1, 128), 1)
    wq = [split_halves(wqkv_ref[:, g * GROUP : (g + 1) * GROUP]) for g in range(2)]
    wk = [split_halves(wqkv_ref[:, inner + g * GROUP : inner + (g + 1) * GROUP]) for g in range(2)]
    wv = wqkv_ref[:, 2 * inner :]
    length = place_ref[0]
    base = place_ref[1] + chunk * frames
    to = lax.broadcasted_iota(jnp.int32, (rows, rows), 0)
    src = lax.broadcasted_iota(jnp.int32, (rows, rows), 1)
    order = (src == to % bands * FRAMES_EACH + to // bands).astype(F32).astype(BF)
    same = lax.broadcasted_iota(jnp.int32, (half, half), 0) // bands == lax.broadcasted_iota(jnp.int32, (half, half), 1) // bands

    def block(i, carry):
        piece = x_ref[:, pl.ds(pl.multiple_of(i * FRAMES_EACH, FRAMES_EACH), FRAMES_EACH), :].reshape(rows, width)
        x = jnp.dot(order, piece, preferred_element_type=F32)
        normed = rms_norm(x, gain_ref[...])
        cosine = cos_ref[...]
        sines = sin_ref[...]
        values = jnp.dot(normed, wv, preferred_element_type=F32)
        for g in range(2):
            qa, qb = rope(jnp.dot(normed, wq[g], preferred_element_type=F32), cosine, sines)
            queries = (jnp.concatenate([qa, qb], axis=1) * (LOG2E * DH**-0.5)).astype(BF)
            ka, kb = rope(jnp.dot(normed, wk[g], preferred_element_type=F32), cosine, sines)
            keys = jnp.concatenate([ka, kb], axis=1).astype(BF)
            for s in range(rows // half):
                part = slice(s * half, (s + 1) * half)
                for pair in range(2):
                    column = (2 * g + pair) * 128
                    v = values[part, column : column + 128]
                    outs = []
                    for odd in range(2):
                        mine = (lane % 128) // HALF == 2 * pair + odd
                        masked = jnp.where(mine, queries[part], jnp.zeros((), BF))
                        scores = lax.dot_general(masked, keys[part], NT, preferred_element_type=F32)
                        scores = jnp.where(same, scores, -1e30)
                        powers = jnp.exp2(scores - jnp.max(scores, axis=1, keepdims=True)).astype(BF)
                        own = (lane128 < DH) if odd == 0 else (lane128 >= DH)
                        extended = jnp.where(own, v, 1.0).astype(BF)
                        mixed = jnp.dot(powers, extended, preferred_element_type=F32)
                        outs.append(mixed / pltpu.roll(mixed, DH, 1))
                    joined = jnp.where(lane128 < DH, outs[0], outs[1])
                    heads_ref[part, column : column + 128] = joined.astype(BF)
        heads = heads_ref[...]
        projected = jnp.dot(heads, wout_ref[...], preferred_element_type=F32)
        here = pl.ds(pl.multiple_of(i * rows, rows), rows)
        out_ref[here, :] = (x + projected).astype(BF)
        frame = base + i * FRAMES_EACH + lax.broadcasted_iota(jnp.int32, (rows, 1), 0) // bands
        tangent = jnp.where(frame < length, cot_ref[here, :].astype(F32), 0.0).astype(BF)
        grad_ref[...] += lax.dot_general(heads, tangent, TN, preferred_element_type=F32)
        return carry

    lax.fori_loop(0, frames // FRAMES_EACH, block, 0)


def band_attention(chunk, chunks, returned, place, gain, wqkv, wout, cotangent, output=None, grad=None):
    bands, frames, width = returned.shape
    inner = HEADS * DH
    rows = bands * FRAMES_EACH
    cosine, sines = rotary_tables(np.tile(np.arange(bands), FRAMES_EACH), 4)
    part = pl.BlockSpec((frames * bands, width), lambda i: (chunk, 0))

    def full(*shape):
        return pl.BlockSpec(shape, lambda i: (0,) * len(shape))

    operands = [place, returned, gain[None], wqkv, wout, cotangent, jnp.asarray(cosine), jnp.asarray(sines)]
    specs = [smem(), full(*returned.shape), full(1, width), full(*wqkv.shape), full(*wout.shape), part, full(*cosine.shape), full(*sines.shape)]
    aliases = {}
    if chunk:
        operands += [grad, output]
        specs += [full(inner, width), pl.BlockSpec(memory_space=pl.ANY)]
        aliases = {len(operands) - 1: 0}
    return pl.pallas_call(
        functools.partial(band_kernel, chunk, chunks),
        grid=(1,),
        out_shape=(
            jax.ShapeDtypeStruct((frames * chunks * bands, width), BF),
            jax.ShapeDtypeStruct((inner, width), F32),
        ),
        in_specs=specs,
        out_specs=(part, full(inner, width)),
        scratch_shapes=[VMEM((rows, inner), BF)],
        input_output_aliases=aliases,
        compiler_params=pltpu.CompilerParams(vmem_limit_bytes=TIME_LIMIT),
        cost_estimate=pl.CostEstimate(flops=10**10, bytes_accessed=5 * 10**6, transcendentals=0),
    )(*operands)


def sum_kernel(seq, songs, part_ref, out_ref, small, got, mid, full, send1, recv1, send2, recv2, send3, recv3):
    me = lax.axis_index("seq")
    song = lax.axis_index("song")
    rows = small.shape[1]
    barrier = pltpu.get_barrier_semaphore()

    def greet(d, carry):
        pl.semaphore_signal(barrier, inc=1, device_id=(lax.rem(me + d, seq), song), device_id_type=MESH)
        return carry

    lax.fori_loop(1, seq, greet, 0)
    for d in range(1, songs):
        pl.semaphore_signal(barrier, inc=1, device_id=(me, lax.rem(song + d, songs)), device_id_type=MESH)
    for r in range(seq):
        small[r] = part_ref[r * rows : (r + 1) * rows, :].astype(BF)
    pl.semaphore_wait(barrier, seq - 1 + songs - 1)

    def first(d):
        peer = lax.rem(me + d, seq)
        return pltpu.make_async_remote_copy(
            src_ref=small.at[peer], dst_ref=got.at[d], send_sem=send1.at[d], recv_sem=recv1.at[d],
            device_id=(peer, song), device_id_type=MESH)

    def start1(d, carry):
        first(d).start()
        return carry

    def wait1(d, carry):
        first(d).wait()
        return carry

    lax.fori_loop(1, seq, start1, 0)
    got[0] = small[me]
    lax.fori_loop(1, seq, wait1, 0)
    total = got[0].astype(F32)
    for d in range(1, seq):
        total = total + got[d].astype(F32)
    mid[song] = total
    copies = []
    for d in range(1, songs):
        copies.append(pltpu.make_async_remote_copy(
            src_ref=mid.at[song], dst_ref=mid.at[song], send_sem=send2.at[d], recv_sem=recv2.at[d],
            device_id=(me, lax.rem(song + d, songs)), device_id_type=MESH))
    for c in copies:
        c.start()
    for c in copies:
        c.wait()
    total = mid[0]
    for s in range(1, songs):
        total = total + mid[s]
    full[me] = total.astype(BF)

    def third(d):
        return pltpu.make_async_remote_copy(
            src_ref=full.at[me], dst_ref=full.at[me], send_sem=send3.at[d], recv_sem=recv3.at[d],
            device_id=(lax.rem(me + d, seq), song), device_id_type=MESH)

    def start3(d, carry):
        third(d).start()
        return carry

    def wait3(d, carry):
        third(d).wait()
        return carry

    lax.fori_loop(1, seq, start3, 0)
    lax.fori_loop(1, seq, wait3, 0)
    for r in range(seq):
        out_ref[r * rows : (r + 1) * rows, :] = full[r].astype(F32)


def gradient_sum(partial):
    seq = lax.axis_size("seq")
    songs = lax.axis_size("song")
    inner, width = partial.shape
    rows = inner // seq
    dma = pltpu.SemaphoreType.DMA
    return pl.pallas_call(
        functools.partial(sum_kernel, seq, songs),
        out_shape=jax.ShapeDtypeStruct((inner, width), F32),
        in_specs=[whole()],
        out_specs=whole(),
        scratch_shapes=[
            VMEM((seq, rows, width), BF),
            VMEM((seq, rows, width), BF),
            VMEM((songs, rows, width), F32),
            VMEM((seq, rows, width), BF),
            dma((seq,)), dma((seq,)), dma((songs,)), dma((songs,)), dma((seq,)), dma((seq,)),
        ],
        compiler_params=pltpu.CompilerParams(collective_id=0, has_side_effects=True, vmem_limit_bytes=LIMIT),
        cost_estimate=pl.CostEstimate(flops=10**7, bytes_accessed=4 * 10**6, transcendentals=0),
    )(partial)


def per_device(spectrum, widths, lengths, bin_gain, embed_weight, embed_bias, time_gain, time_qkv, time_out, band_gain, band_qkv, band_out, cotangent):
    local_frames = spectrum.shape[1]
    bands, width = embed_bias.shape
    computed = embed(spectrum[0], widths, bin_gain, embed_weight, embed_bias)
    place = jnp.stack([lengths[0], lax.axis_index("seq") * local_frames]).astype(jnp.int32)
    tangent = cotangent.reshape(local_frames * bands, width)
    owned, early, late, k, v, most = exchange(computed, lengths, time_gain, time_qkv)
    first = time_attention(0, lengths, most, owned, time_out, early, k, v)
    first = lax.all_to_all(first, "seq", split_axis=0, concat_axis=0, tiled=True)
    second = time_attention(1, lengths, most, owned, time_out, late, k, v)
    second = lax.all_to_all(second, "seq", split_axis=0, concat_axis=0, tiled=True)
    output, partial = band_attention(0, 2, first, place, band_gain, band_qkv, band_out, tangent)
    output, partial = band_attention(1, 2, second, place, band_gain, band_qkv, band_out, tangent, output, partial)
    gradient = gradient_sum(partial)
    return output.reshape(1, local_frames, bands, width), gradient


def solution(mesh):
    return jax.shard_map(
        per_device,
        mesh=mesh,
        in_specs=(P("song", "seq", None), P(), P("song"), P(), P(), P(), P(), P(), P(), P(), P(), P(), P("song", "seq", None, None)),
        out_specs=(P("song", "seq", None, None), P()),
        check_vma=False,
    )
```

```python
import functools

import jax
import jax.numpy as jnp
import numpy as np
from jax import lax
from jax.experimental import pallas as pl
from jax.experimental.pallas import tpu as pltpu
from jax.sharding import PartitionSpec as P

HEADS = 8
DH = 64
HALF = DH // 2
GROUP = 4 * DH
FLOOR = 0.25
EPSILON = 1e-05
LOG2E = 1.4426950408889634
WINDOW = 1152
NT = (((1,), (1,)), ((), ()))
TN = (((0,), (0,)), ((), ()))
MESH = pl.DeviceIdType.MESH
BF = jnp.bfloat16
F32 = jnp.float32
SAFE = 100.0
VSAFE = 2.0**12
VMEM = pltpu.VMEM
LIMIT = 56 * 2**20


def whole():
    return pl.BlockSpec(memory_space=pltpu.VMEM)


def smem():
    return pl.BlockSpec(memory_space=pltpu.SMEM)


def rotary_tables(positions, repeat):
    frequency = np.exp(-(2.0 * np.arange(HALF, dtype=np.float64) / DH) * np.log(10000.0))
    angles = positions.astype(np.float64)[:, None] * frequency
    cosine = np.tile(np.cos(angles), (1, repeat)).astype(np.float32)
    sines = np.tile(np.sin(angles), (1, repeat)).astype(np.float32)
    return cosine, sines


def split_halves(weights):
    row = lax.broadcasted_iota(jnp.int32, (GROUP, GROUP), 0)
    col = lax.broadcasted_iota(jnp.int32, (GROUP, GROUP), 1)
    source = (col % 128) // HALF * DH + col // 128 * HALF + col % HALF
    one_hot = (row == source).astype(F32).astype(BF)
    return jnp.dot(weights, one_hot, preferred_element_type=F32).astype(BF)


def rms_norm(rows, gain):
    square = jnp.mean(rows * rows, axis=-1, keepdims=True)
    return (rows * lax.rsqrt(square + EPSILON) * gain).astype(BF)


def rope(values, cosine, sines):
    leading = values[:, :128]
    second = values[:, 128:]
    return leading * cosine - second * sines, second * cosine + leading * sines


NARROW = 640


def embed_kernel(bands, widths_ref, x_ref, gain_ref, w_ref, bias_ref, out_ref, starts_ref):
    limit = x_ref.shape[1]
    main = limit // 128 * 128
    total = 0
    for k in range(bands):
        starts_ref[k] = total
        total = total + widths_ref[k] * 4

    def band(k, size):
        first = starts_ref[k]
        count = widths_ref[k] * 4
        begin = pl.multiple_of(jnp.minimum(first // 128, (main - size) // 128) * 128, 128)
        window = pl.ds(begin, size)
        entry = lax.broadcasted_iota(jnp.int32, (1, size), 1) + begin
        piece = x_ref[:, window].astype(F32)
        piece = jnp.where((entry >= first) & (entry < first + count), piece, 0.0)
        tail = jnp.where(k == bands - 1, x_ref[:, main:].astype(F32), 0.0)
        square = jnp.sum(piece * piece, axis=1, keepdims=True) + jnp.sum(tail * tail, axis=1, keepdims=True)
        scale = 1.0 / jnp.sqrt(jnp.maximum(square / count.astype(F32), FLOOR))
        normed = (piece * scale * gain_ref[:, window]).astype(BF)
        summed = jnp.dot(normed, w_ref[window, :], preferred_element_type=F32) + bias_ref[pl.ds(k, 1), :]
        normed = (tail * scale * gain_ref[:, main:]).astype(BF).astype(F32)
        rows = w_ref[main:, :].astype(F32)
        for e in range(limit - main):
            summed = summed + normed[:, e : e + 1] * rows[e : e + 1, :]
        out_ref[k] = summed.astype(BF)

    def step(i, carry):
        narrow = widths_ref[4 * i] * 4 <= NARROW - 124
        for j in range(1, 4):
            narrow = narrow & (widths_ref[4 * i + j] * 4 <= NARROW - 124)

        @pl.when(narrow)
        def _():
            for j in range(4):
                band(4 * i + j, NARROW)

        @pl.when(jnp.logical_not(narrow))
        def _():
            for j in range(4):
                band(4 * i + j, WINDOW)

        return carry

    lax.fori_loop(0, bands // 4, step, 0)


def embed(spectrum, widths, bin_gain, embed_weight, embed_bias):
    frames, feature_count = spectrum.shape
    bands, width = embed_bias.shape
    return pl.pallas_call(
        functools.partial(embed_kernel, bands),
        out_shape=jax.ShapeDtypeStruct((bands, frames, width), BF),
        in_specs=[smem()] + [whole()] * 4,
        out_specs=whole(),
        scratch_shapes=[pltpu.SMEM((bands,), jnp.int32)],
        compiler_params=pltpu.CompilerParams(vmem_limit_bytes=32 * 2**20),
        cost_estimate=pl.CostEstimate(flops=2 * 10**9, bytes_accessed=9 * 10**6, transcendentals=0),
    )(widths, spectrum, bin_gain[None], embed_weight, embed_bias)


VROWS = 80


def exchange_kernel(
    seq, length_ref, bands_ref, gain_ref, wqkv_ref, cos_ref, sin_ref,
    x_ref, qa_ref, qb_ref, k_ref, v_ref, most_ref, got, send_sem, recv_sem,
):
    frames, width = got.shape[1:]
    half = frames // 2
    inner = HEADS * DH
    me = lax.axis_index("seq")
    song = lax.axis_index("song")
    y, x, core = me // 8, me // 2 % 4, me % 2

    def other(i, sign):
        return (y + sign * (i // 8) + 4) % 4 * 8 + (x + sign * (i // 2 % 4) + 4) % 4 * 2 + (core + i % 2) % 2

    barrier = pltpu.get_barrier_semaphore()

    def greet(i, carry):
        pl.semaphore_signal(barrier, inc=1, device_id=(other(i, 1), song), device_id_type=MESH)
        return carry

    lax.fori_loop(1, seq, greet, 0)
    lane = lax.broadcasted_iota(jnp.int32, (1, GROUP), 1)
    wq = [split_halves(wqkv_ref[:, g * GROUP : (g + 1) * GROUP]) for g in range(2)]
    wk = [split_halves(wqkv_ref[:, inner + g * GROUP : inner + (g + 1) * GROUP]) for g in range(2)]
    wv = wqkv_ref[:, 2 * inner :]
    pl.semaphore_wait(barrier, seq - 1)

    def copy(i):
        k = other(i, 1)
        return pltpu.make_async_remote_copy(
            src_ref=bands_ref.at[k], dst_ref=got.at[me], send_sem=send_sem.at[i], recv_sem=recv_sem.at[i],
            device_id=(k, song), device_id_type=MESH)

    def start(j, carry):
        copy(8 * (1 + 2 * (j % 2)) + j // 2).start()
        return carry

    def start_rest(j, carry):
        copy(16 + j).start()
        copy(j).start()
        return carry

    lax.fori_loop(0, 16, start, 0)
    copy(16).start()
    lax.fori_loop(1, 8, start_rest, 0)
    got[me] = bands_ref[me]
    length = length_ref[0]

    heads_of = lax.broadcasted_iota(jnp.int32, (GROUP, 128), 0) % 128 // HALF
    per_head = (heads_of == lax.broadcasted_iota(jnp.int32, (GROUP, 128), 1)).astype(F32).astype(BF)

    def longest(rows):
        squares = jnp.dot((rows * rows).astype(BF), per_head, preferred_element_type=F32)
        return jnp.max(squares, axis=0, keepdims=True)

    def project(dy, stats):
        row = (y - dy + 4) % 4

        def wait(i, carry):
            copy(8 * dy + i).wait_recv()
            return carry

        lax.fori_loop(1 if dy == 0 else 0, 8, wait, 0)
        owners = pl.ds(pl.multiple_of(row * 8, 8), 8)
        count = 8 * frames
        base = pl.multiple_of(row * count, count)
        rows = pl.ds(base, count)
        received = got[owners]
        x_ref[owners] = received
        normed = rms_norm(received.reshape(count, width).astype(F32), gain_ref[...])
        cosine = cos_ref[rows, :]
        sines = sin_ref[rows, :]
        alive_row = (lax.broadcasted_iota(jnp.int32, (count, 1), 0) + base) < length
        alive_col = (lax.broadcasted_iota(jnp.int32, (1, count), 1) + base) < length
        here = pl.ds(pl.multiple_of(row * 8 * half, 8 * half), 8 * half)
        kinds = []
        for g in range(2):
            qa, qb = rope(jnp.dot(normed, wq[g], preferred_element_type=F32), cosine, sines)
            scaled = jnp.concatenate([qa, qb], axis=1) * (LOG2E * DH**-0.5)
            parts = scaled.reshape(8, frames, GROUP)
            qa_ref[g, here, :] = parts[:, :half].reshape(8 * half, GROUP).astype(BF)
            qb_ref[g, here, :] = parts[:, half:].reshape(8 * half, GROUP).astype(BF)
            ka, kb = rope(jnp.dot(normed, wk[g], preferred_element_type=F32), cosine, sines)
            keys = jnp.concatenate([ka, kb], axis=1)
            keys = jnp.where(alive_row, keys, 0.0)
            k_ref[g, rows, :] = keys.astype(BF)
            kinds.append(longest(scaled))
            kinds.append(longest(keys))
        values = lax.dot_general(wv, normed, (((0,), (1,)), ((), ())), preferred_element_type=F32)
        values = jnp.where(alive_col, values, 0.0)
        vmost = jnp.max(jnp.max(jnp.abs(values), axis=0, keepdims=True), axis=1, keepdims=True)
        kinds.append(jnp.broadcast_to(vmost, (1, 128)))
        values = values.astype(BF)
        ones = jnp.broadcast_to(jnp.where(alive_col, 1.0, 0.0), (VROWS - DH, count)).astype(BF)
        for h in range(HEADS):
            v_ref[h, :DH, rows] = values[h * DH : (h + 1) * DH]
            v_ref[h, DH:, rows] = ones
        if stats is None:
            return kinds
        return [jnp.maximum(p, n) for p, n in zip(stats, kinds)]

    stats = None
    for dy in (1, 3, 0, 2):
        stats = project(dy, stats)
    for n, row in enumerate(stats):
        most_ref[n : n + 1, :] = row

    def finish(i, carry):
        copy(i).wait_send()
        return carry

    lax.fori_loop(1, seq, finish, 0)


def exchange(computed, lengths, gain, wqkv):
    seq = lax.axis_size("seq")
    bands, frames, width = computed.shape
    count = seq * frames
    cosine, sines = rotary_tables(np.arange(count), 4)
    dma = pltpu.SemaphoreType.DMA
    return pl.pallas_call(
        functools.partial(exchange_kernel, seq),
        out_shape=(
            jax.ShapeDtypeStruct((seq, frames, width), BF),
            jax.ShapeDtypeStruct((2, count // 2, GROUP), BF),
            jax.ShapeDtypeStruct((2, count // 2, GROUP), BF),
            jax.ShapeDtypeStruct((2, count, GROUP), BF),
            jax.ShapeDtypeStruct((HEADS, VROWS, count), BF),
            jax.ShapeDtypeStruct((5, 128), F32),
        ),
        in_specs=[smem()] + [whole()] * 5,
        out_specs=[whole()] * 6,
        scratch_shapes=[VMEM((seq, frames, width), BF), dma((seq,)), dma((seq,))],
        compiler_params=pltpu.CompilerParams(collective_id=1, has_side_effects=True, vmem_limit_bytes=TIME_LIMIT),
        cost_estimate=pl.CostEstimate(flops=4 * 10**9, bytes_accessed=10 * 10**6, transcendentals=0),
    )(lengths, computed, gain[None], wqkv, jnp.asarray(cosine), jnp.asarray(sines))


TIME_LIMIT = 28 * 2**20


def time_kernel(chunk, length_ref, most_ref, x_ref, wout_ref, q_ref, k_ref, v_ref, out_ref, heads_ref):
    owners, frames, width = x_ref.shape
    half = frames // 2
    lane = lax.broadcasted_iota(jnp.int32, (1, GROUP), 1)
    bound = jnp.maximum(most_ref[0:1, :] * most_ref[1:2, :], most_ref[2:3, :] * most_ref[3:4, :])
    fits = (jnp.max(bound) * 1.05 < SAFE * SAFE) & (jnp.max(most_ref[4:5, :]) < VSAFE)

    def attend(shift):
        def head(h, carry):
            g = h // 4
            mine = (lane % 128) // HALF == h % 4
            queries = jnp.where(mine, q_ref[g], jnp.zeros((), BF))
            scores = lax.dot_general(k_ref[g], queries, NT, preferred_element_type=F32)
            if shift:
                alive = lax.broadcasted_iota(jnp.int32, (owners * frames, 1), 0) < length_ref[0]
                scores = jnp.where(alive, scores, -1e30)
                scores = scores - jnp.max(scores, axis=0, keepdims=True)
            powers = jnp.exp2(scores).astype(BF)
            mixed = jnp.dot(v_ref[h], powers, preferred_element_type=F32)
            mixed = mixed[:DH] / mixed[DH : DH + 1]
            heads_ref[pl.ds(pl.multiple_of(h * DH, DH), DH), :] = mixed.astype(BF)
            return carry

        lax.fori_loop(0, HEADS, head, 0)

    @pl.when(fits)
    def _():
        attend(False)

    @pl.when(jnp.logical_not(fits))
    def _():
        attend(True)

    projected = lax.dot_general(heads_ref[...], wout_ref[...], TN, preferred_element_type=F32)
    before = x_ref[:, chunk * half : (chunk + 1) * half, :].astype(F32)
    out_ref[...] = (before + projected.reshape(owners, half, width)).astype(BF)


def time_attention(chunk, lengths, most, sequence, wout, q, k, v):
    owners, frames, width = sequence.shape
    return pl.pallas_call(
        functools.partial(time_kernel, chunk),
        out_shape=jax.ShapeDtypeStruct((owners, frames // 2, width), BF),
        in_specs=[smem()] + [whole()] * 6,
        out_specs=whole(),
        scratch_shapes=[VMEM((HEADS * DH, owners * frames // 2), BF)],
        compiler_params=pltpu.CompilerParams(vmem_limit_bytes=TIME_LIMIT),
        cost_estimate=pl.CostEstimate(flops=2 * 10**10, bytes_accessed=8 * 10**6, transcendentals=0),
    )(lengths, most, sequence, wout, q, k, v)


FRAMES_EACH = 16


def finish_kernel(
    seq, songs, length_ref, early_ref, later_ref, gain_ref, wqkv_ref, wout_ref, cot_hbm, cos_ref, sin_ref,
    out_hbm, sum_ref, got, cot_ref, heads_ref, x_ref, feat_ref, grad_ref, halves, half_in, parts, parts_in, mid, full,
    cot_sem, out_sem, send_sem, recv_sem, core_send, core_recv, plane_send, plane_recv, song_send, song_recv, back_send, back_recv, last_send, last_recv,
):
    bands, chunk, width = early_ref.shape
    inner = HEADS * DH
    rows = bands * FRAMES_EACH
    blocks = chunk // FRAMES_EACH
    half = 256
    me = lax.axis_index("seq")
    song = lax.axis_index("song")
    y, x, core = me // 8, me // 2 % 4, me % 2

    def other(i):
        return (y + i // 8) % 4 * 8 + (x + i // 2 % 4) % 4 * 2 + (core + i % 2) % 2

    cot_copy = pltpu.make_async_copy(cot_hbm, cot_ref, cot_sem)
    cot_copy.start()
    barrier = pltpu.get_barrier_semaphore()

    def greet(i, carry):
        pl.semaphore_signal(barrier, inc=1, device_id=(other(i), song), device_id_type=MESH)
        return carry

    lax.fori_loop(1, seq, greet, 0)
    for d in range(1, songs):
        pl.semaphore_signal(barrier, inc=1, device_id=(me, (song + d) % songs), device_id_type=MESH)

    lane = lax.broadcasted_iota(jnp.int32, (1, GROUP), 1)
    wq = [split_halves(wqkv_ref[:, g * GROUP : (g + 1) * GROUP]) for g in range(2)]
    wk = [split_halves(wqkv_ref[:, inner + g * GROUP : inner + (g + 1) * GROUP]) for g in range(2)]
    wv = wqkv_ref[:, 2 * inner :]
    to = lax.broadcasted_iota(jnp.int32, (rows, rows), 0)
    src = lax.broadcasted_iota(jnp.int32, (rows, rows), 1)
    order = (src == to % bands * FRAMES_EACH + to // bands).astype(F32).astype(BF)
    same = (
        lax.broadcasted_iota(jnp.int32, (4 * half, half), 0) % half // bands
        == lax.broadcasted_iota(jnp.int32, (4 * half, half), 1) // bands
    )
    grad_ref[...] = jnp.zeros_like(grad_ref)
    pl.semaphore_wait(barrier, seq - 1 + songs - 1)

    def copy(i):
        k = other(i)
        return pltpu.make_async_remote_copy(
            src_ref=later_ref.at[k], dst_ref=got.at[me], send_sem=send_sem.at[i], recv_sem=recv_sem.at[i],
            device_id=(k, song), device_id_type=MESH)

    def start(i, carry):
        copy(seq - i).start()
        return carry

    def arrive(i, carry):
        copy(seq - i).wait()
        return carry

    lax.fori_loop(1, seq, start, 0)
    got[me] = later_ref[me]
    length = length_ref[0]
    cot_copy.wait()

    def attend(source_ref, first):
        def block(i, carry):
            piece = source_ref[:, pl.ds(pl.multiple_of(i * FRAMES_EACH, FRAMES_EACH), FRAMES_EACH), :].reshape(rows, width)
            values_x = jnp.dot(order, piece, preferred_element_type=F32)
            here = pl.ds(pl.multiple_of((i + first) * rows, rows), rows)
            x_ref[here, :] = values_x.astype(BF)
            normed = rms_norm(values_x, gain_ref[...])
            cosine = cos_ref[...]
            sines = sin_ref[...]
            values = jnp.dot(normed, wv, preferred_element_type=F32)
            joined_groups = []
            for g in range(2):
                qa, qb = rope(jnp.dot(normed, wq[g], preferred_element_type=F32), cosine, sines)
                queries = (jnp.concatenate([qa, qb], axis=1) * (LOG2E * DH**-0.5)).astype(BF)
                ka, kb = rope(jnp.dot(normed, wk[g], preferred_element_type=F32), cosine, sines)
                keys = jnp.concatenate([ka, kb], axis=1).astype(BF)
                pieces = []
                for s in range(rows // half):
                    part = slice(s * half, (s + 1) * half)
                    stacked = jnp.concatenate(
                        [jnp.where((lane % 128) // HALF == h, queries[part], jnp.zeros((), BF)) for h in range(4)], axis=0)
                    scores = lax.dot_general(stacked, keys[part], NT, preferred_element_type=F32)
                    scores = jnp.where(same, scores, -1e30)
                    powers = jnp.exp2(scores - jnp.max(scores, axis=1, keepdims=True))
                    mixed = jnp.dot(
                        powers.astype(BF), values[part, g * GROUP : (g + 1) * GROUP].astype(BF), preferred_element_type=F32)
                    mixed = mixed / jnp.sum(powers, axis=1, keepdims=True)
                    joined = mixed[:half]
                    for h in range(1, 4):
                        joined = jnp.where(lane // DH == h, mixed[h * half : (h + 1) * half], joined)
                    pieces.append(joined.astype(BF))
                joined_groups.append(jnp.concatenate(pieces, axis=0))
            heads = jnp.concatenate(joined_groups, axis=1)
            heads_ref[here, :] = heads
            frame = me * (2 * chunk) + (i + first) * FRAMES_EACH + lax.broadcasted_iota(jnp.int32, (rows, 1), 0) // bands
            tangent = jnp.where(frame < length, cot_ref[here, :].astype(F32), 0.0).astype(BF)
            grad_ref[...] += lax.dot_general(heads, tangent, TN, preferred_element_type=F32)
            return carry

        lax.fori_loop(0, blocks, block, 0)

    def out_copy(i):
        here = slice(i * rows, (i + 1) * rows)
        return pltpu.make_async_copy(feat_ref.at[here], out_hbm.at[here], out_sem.at[i])

    def features(i):
        here = slice(i * rows, (i + 1) * rows)
        projected = jnp.dot(heads_ref[here, :], wout_ref[...], preferred_element_type=F32)
        feat_ref[here, :] = (x_ref[here, :].astype(F32) + projected).astype(BF)
        out_copy(i).start()

    attend(early_ref, 0)
    lax.fori_loop(1, seq, arrive, 0)
    attend(got, blocks)

    def remote(src_ref, dst_ref, send, recv, device):
        return pltpu.make_async_remote_copy(
            src_ref=src_ref, dst_ref=dst_ref, send_sem=send, recv_sem=recv, device_id=device, device_id_type=MESH)

    twin = (me + 1 - 2 * core, song)
    plane = [(dy, dx) for dy in range(4) for dx in range(4) if dy or dx]

    def at(dy, dx):
        return ((y + dy) % 4 * 8 + (x + dx) % 4 * 2 + core, song)

    halves[...] = grad_ref[...].astype(BF).reshape(halves.shape)
    exchange_half = remote(halves.at[1 - core], half_in, core_send, core_recv, twin)
    exchange_half.start()
    exchange_half.wait()
    parts[...] = (halves[core].astype(F32) + half_in[...].astype(F32)).astype(BF).reshape(parts.shape)
    copies = [
        remote(parts.at[(x + dx) % 4 * 4 + (y + dy) % 4], parts_in.at[dx * 4 + dy], plane_send.at[dx * 4 + dy], plane_recv.at[dx * 4 + dy], at(dy, dx))
        for dy, dx in plane
    ]
    for one in copies:
        one.start()
    parts_in[0] = parts[x * 4 + y]
    features(0)
    features(1)
    for one in copies:
        one.wait()
    total = parts_in[0].astype(F32)
    for n in range(1, 16):
        total = total + parts_in[n].astype(F32)
    mid[song] = total
    copies = [
        remote(mid.at[song], mid.at[song], song_send.at[d], song_recv.at[d], (me, (song + d) % songs)) for d in range(1, songs)
    ]
    for one in copies:
        one.start()
    features(2)
    for one in copies:
        one.wait()
    total = mid[0]
    for n in range(1, songs):
        total = total + mid[n]
    full[core, x * 4 + y] = total.astype(BF)
    copies = [
        remote(full.at[core, x * 4 + y], full.at[core, x * 4 + y], back_send.at[dx * 4 + dy], back_recv.at[dx * 4 + dy], at(dy, dx))
        for dy, dx in plane
    ]
    for one in copies:
        one.start()
    features(3)
    for one in copies:
        one.wait()
    exchange_half = remote(full.at[core], full.at[core], last_send, last_recv, twin)
    exchange_half.start()
    exchange_half.wait()
    sum_ref[...] = full[...].reshape(inner, width)
    for i in range(4):
        out_copy(i).wait()


def finish(lengths, early, later, gain, wqkv, wout, cotangent):
    seq = lax.axis_size("seq")
    songs = lax.axis_size("song")
    bands, chunk, width = early.shape
    inner = HEADS * DH
    rows = bands * FRAMES_EACH
    count = 2 * chunk * bands
    cosine, sines = rotary_tables(np.tile(np.arange(bands), FRAMES_EACH), 4)
    dma = pltpu.SemaphoreType.DMA
    anywhere = pl.BlockSpec(memory_space=pl.ANY)
    return pl.pallas_call(
        functools.partial(finish_kernel, seq, songs),
        out_shape=(jax.ShapeDtypeStruct((count, width), BF), jax.ShapeDtypeStruct((inner, width), BF)),
        in_specs=[smem()] + [whole()] * 5 + [anywhere] + [whole()] * 2,
        out_specs=(anywhere, whole()),
        scratch_shapes=[
            VMEM((bands, chunk, width), BF),
            VMEM((count, width), BF),
            VMEM((count, inner), BF),
            VMEM((count, width), BF),
            VMEM((count, width), BF),
            VMEM((inner, width), F32),
            VMEM((2, inner // 2, width), BF),
            VMEM((inner // 2, width), BF),
            VMEM((16, inner // 32, width), BF),
            VMEM((16, inner // 32, width), BF),
            VMEM((songs, inner // 32, width), F32),
            VMEM((2, 16, inner // 32, width), BF),
            dma, dma((4,)), dma((seq,)), dma((seq,)), dma, dma, dma((16,)), dma((16,)),
            dma((songs,)), dma((songs,)), dma((16,)), dma((16,)), dma, dma,
        ],
        compiler_params=pltpu.CompilerParams(collective_id=2, has_side_effects=True, vmem_limit_bytes=36 * 2**20),
        cost_estimate=pl.CostEstimate(flops=10**10, bytes_accessed=7 * 10**6, transcendentals=0),
    )(lengths, early, later, gain, wqkv, wout, cotangent, jnp.asarray(cosine), jnp.asarray(sines))


def per_device(spectrum, widths, lengths, bin_gain, embed_weight, embed_bias, time_gain, time_qkv, time_out, band_gain, band_qkv, band_out, cotangent):
    local_frames = spectrum.shape[1]
    bands, width = embed_bias.shape
    computed = embed(spectrum[0], widths, bin_gain, embed_weight, embed_bias)
    tangent = cotangent.reshape(local_frames * bands, width)
    owned, early, late, k, v, most = exchange(computed, lengths, time_gain, time_qkv)
    first = time_attention(0, lengths, most, owned, time_out, early, k, v)
    first = lax.all_to_all(first, "seq", split_axis=0, concat_axis=0, tiled=True)
    second = time_attention(1, lengths, most, owned, time_out, late, k, v)
    output, gradient = finish(lengths, first, second, band_gain[None], band_qkv, band_out, tangent)
    return output.reshape(1, local_frames, bands, width), gradient.astype(F32)


def solution(mesh):
    return jax.shard_map(
        per_device,
        mesh=mesh,
        in_specs=(P("song", "seq", None), P(), P("song"), P(), P(), P(), P(), P(), P(), P(), P(), P(), P("song", "seq", None, None)),
        out_specs=(P("song", "seq", None, None), P()),
        check_vma=False,
    )
```

```python
import functools

import jax
import jax.numpy as jnp
import numpy as np
from jax import lax
from jax.experimental import pallas as pl
from jax.experimental.pallas import tpu as pltpu
from jax.sharding import PartitionSpec as P

HEADS = 8
DH = 64
HALF = DH // 2
GROUP = 4 * DH
FLOOR = 0.25
EPSILON = 1e-05
LOG2E = 1.4426950408889634
WINDOW = 1152
NT = (((1,), (1,)), ((), ()))
TN = (((0,), (0,)), ((), ()))
MESH = pl.DeviceIdType.MESH
BF = jnp.bfloat16
F32 = jnp.float32
SAFE = 100.0
VSAFE = 2.0**12
VMEM = pltpu.VMEM
LIMIT = 56 * 2**20


def whole():
    return pl.BlockSpec(memory_space=pltpu.VMEM)


def smem():
    return pl.BlockSpec(memory_space=pltpu.SMEM)


def rotary_tables(positions, repeat):
    frequency = np.exp(-(2.0 * np.arange(HALF, dtype=np.float64) / DH) * np.log(10000.0))
    angles = positions.astype(np.float64)[:, None] * frequency
    cosine = np.tile(np.cos(angles), (1, repeat)).astype(np.float32)
    sines = np.tile(np.sin(angles), (1, repeat)).astype(np.float32)
    return cosine, sines


def split_halves(weights):
    row = lax.broadcasted_iota(jnp.int32, (GROUP, GROUP), 0)
    col = lax.broadcasted_iota(jnp.int32, (GROUP, GROUP), 1)
    source = (col % 128) // HALF * DH + col // 128 * HALF + col % HALF
    one_hot = (row == source).astype(F32).astype(BF)
    return jnp.dot(weights, one_hot, preferred_element_type=F32).astype(BF)


def rms_norm(rows, gain):
    square = jnp.mean(rows * rows, axis=-1, keepdims=True)
    return (rows * lax.rsqrt(square + EPSILON) * gain).astype(BF)


def rope(values, cosine, sines):
    leading = values[:, :128]
    second = values[:, 128:]
    return leading * cosine - second * sines, second * cosine + leading * sines


NARROW = 640


def embed_kernel(bands, widths_ref, x_ref, gain_ref, w_ref, bias_ref, out_ref, starts_ref):
    limit = x_ref.shape[1]
    main = limit // 128 * 128
    total = 0
    for k in range(bands):
        starts_ref[k] = total
        total = total + widths_ref[k] * 4

    def band(k, size):
        first = starts_ref[k]
        count = widths_ref[k] * 4
        begin = pl.multiple_of(jnp.minimum(first // 128, (main - size) // 128) * 128, 128)
        window = pl.ds(begin, size)
        entry = lax.broadcasted_iota(jnp.int32, (1, size), 1) + begin
        piece = x_ref[:, window].astype(F32)
        piece = jnp.where((entry >= first) & (entry < first + count), piece, 0.0)
        tail = jnp.where(k == bands - 1, x_ref[:, main:].astype(F32), 0.0)
        square = jnp.sum(piece * piece, axis=1, keepdims=True) + jnp.sum(tail * tail, axis=1, keepdims=True)
        scale = 1.0 / jnp.sqrt(jnp.maximum(square / count.astype(F32), FLOOR))
        normed = (piece * scale * gain_ref[:, window]).astype(BF)
        summed = jnp.dot(normed, w_ref[window, :], preferred_element_type=F32) + bias_ref[pl.ds(k, 1), :]
        normed = (tail * scale * gain_ref[:, main:]).astype(BF).astype(F32)
        rows = w_ref[main:, :].astype(F32)
        for e in range(limit - main):
            summed = summed + normed[:, e : e + 1] * rows[e : e + 1, :]
        out_ref[k] = summed.astype(BF)

    def step(i, carry):
        narrow = widths_ref[4 * i] * 4 <= NARROW - 124
        for j in range(1, 4):
            narrow = narrow & (widths_ref[4 * i + j] * 4 <= NARROW - 124)

        @pl.when(narrow)
        def _():
            for j in range(4):
                band(4 * i + j, NARROW)

        @pl.when(jnp.logical_not(narrow))
        def _():
            for j in range(4):
                band(4 * i + j, WINDOW)

        return carry

    lax.fori_loop(0, bands // 4, step, 0)


def embed(spectrum, widths, bin_gain, embed_weight, embed_bias):
    frames, feature_count = spectrum.shape
    bands, width = embed_bias.shape
    return pl.pallas_call(
        functools.partial(embed_kernel, bands),
        out_shape=jax.ShapeDtypeStruct((bands, frames, width), BF),
        in_specs=[smem()] + [whole()] * 4,
        out_specs=whole(),
        scratch_shapes=[pltpu.SMEM((bands,), jnp.int32)],
        compiler_params=pltpu.CompilerParams(vmem_limit_bytes=32 * 2**20),
        cost_estimate=pl.CostEstimate(flops=2 * 10**9, bytes_accessed=9 * 10**6, transcendentals=0),
    )(widths, spectrum, bin_gain[None], embed_weight, embed_bias)


VROWS = 80


def exchange_kernel(
    seq, length_ref, bands_ref, gain_ref, wqkv_ref, cos_ref, sin_ref,
    x_ref, q_ref, k_ref, v_ref, most_ref, got, send_sem, recv_sem,
):
    frames, width = got.shape[1:]
    half = frames // 2
    inner = HEADS * DH
    me = lax.axis_index("seq")
    song = lax.axis_index("song")
    y, x, core = me // 8, me // 2 % 4, me % 2

    def other(i, sign):
        return (y + sign * (i // 8) + 4) % 4 * 8 + (x + sign * (i // 2 % 4) + 4) % 4 * 2 + (core + i % 2) % 2

    barrier = pltpu.get_barrier_semaphore()

    def greet(i, carry):
        pl.semaphore_signal(barrier, inc=1, device_id=(other(i, 1), song), device_id_type=MESH)
        return carry

    lax.fori_loop(1, seq, greet, 0)
    lane = lax.broadcasted_iota(jnp.int32, (1, GROUP), 1)
    wq = [split_halves(wqkv_ref[:, g * GROUP : (g + 1) * GROUP]) for g in range(2)]
    wk = [split_halves(wqkv_ref[:, inner + g * GROUP : inner + (g + 1) * GROUP]) for g in range(2)]
    wv = wqkv_ref[:, 2 * inner :]
    pl.semaphore_wait(barrier, seq - 1)

    def copy(i):
        k = other(i, 1)
        return pltpu.make_async_remote_copy(
            src_ref=bands_ref.at[k], dst_ref=got.at[me], send_sem=send_sem.at[i], recv_sem=recv_sem.at[i],
            device_id=(k, song), device_id_type=MESH)

    def start(j, carry):
        copy(8 * (1 + 2 * (j % 2)) + j // 2).start()
        return carry

    def start_rest(j, carry):
        copy(16 + j).start()
        copy(j).start()
        return carry

    lax.fori_loop(0, 16, start, 0)
    copy(16).start()
    lax.fori_loop(1, 8, start_rest, 0)
    got[me] = bands_ref[me]
    length = length_ref[0]

    heads_of = lax.broadcasted_iota(jnp.int32, (GROUP, 128), 0) % 128 // HALF
    per_head = (heads_of == lax.broadcasted_iota(jnp.int32, (GROUP, 128), 1)).astype(F32).astype(BF)

    def longest(rows):
        squares = jnp.dot((rows * rows).astype(BF), per_head, preferred_element_type=F32)
        return jnp.max(squares, axis=0, keepdims=True)

    def project(dy, stats):
        row = (y - dy + 4) % 4

        def wait(i, carry):
            copy(8 * dy + i).wait_recv()
            return carry

        lax.fori_loop(1 if dy == 0 else 0, 8, wait, 0)
        owners = pl.ds(pl.multiple_of(row * 8, 8), 8)
        count = 8 * frames
        base = pl.multiple_of(row * count, count)
        rows = pl.ds(base, count)
        received = got[owners]
        x_ref[0, owners] = received[:, :half]
        x_ref[1, owners] = received[:, half:]
        normed = rms_norm(received.reshape(count, width).astype(F32), gain_ref[...].reshape(1, width))
        cosine = cos_ref[rows, :]
        sines = sin_ref[rows, :]
        alive_row = (lax.broadcasted_iota(jnp.int32, (count, 1), 0) + base) < length
        alive_col = (lax.broadcasted_iota(jnp.int32, (1, count), 1) + base) < length
        here = pl.ds(pl.multiple_of(row * 8 * half, 8 * half), 8 * half)
        kinds = []
        for g in range(2):
            qa, qb = rope(jnp.dot(normed, wq[g], preferred_element_type=F32), cosine, sines)
            scaled = jnp.concatenate([qa, qb], axis=1) * (LOG2E * DH**-0.5)
            parts = scaled.reshape(8, frames, GROUP)
            for n in range(2):
                q_ref[n, g, here, :] = parts[:, n * half : (n + 1) * half].reshape(8 * half, GROUP).astype(BF)
            ka, kb = rope(jnp.dot(normed, wk[g], preferred_element_type=F32), cosine, sines)
            keys = jnp.concatenate([ka, kb], axis=1)
            keys = jnp.where(alive_row, keys, 0.0)
            k_ref[g, rows, :] = keys.astype(BF)
            kinds.append(longest(scaled))
            kinds.append(longest(keys))
        values = lax.dot_general(wv, normed, (((0,), (1,)), ((), ())), preferred_element_type=F32)
        values = jnp.where(alive_col, values, 0.0)
        vmost = jnp.max(jnp.max(jnp.abs(values), axis=0, keepdims=True), axis=1, keepdims=True)
        kinds.append(jnp.broadcast_to(vmost, (1, 128)))
        values = values.astype(BF)
        ones = jnp.broadcast_to(jnp.where(alive_col, 1.0, 0.0), (VROWS - DH, count)).astype(BF)
        for h in range(HEADS):
            v_ref[h, :DH, rows] = values[h * DH : (h + 1) * DH]
            v_ref[h, DH:, rows] = ones
        if stats is None:
            return kinds
        return [jnp.maximum(p, n) for p, n in zip(stats, kinds)]

    stats = None
    for dy in (1, 3, 0, 2):
        stats = project(dy, stats)
    for n, row in enumerate(stats):
        most_ref[n : n + 1, :] = row

    def finish(i, carry):
        copy(i).wait_send()
        return carry

    lax.fori_loop(1, seq, finish, 0)


def exchange(computed, lengths, gain, wqkv):
    seq = lax.axis_size("seq")
    bands, frames, width = computed.shape
    count = seq * frames
    cosine, sines = rotary_tables(np.arange(count), 4)
    dma = pltpu.SemaphoreType.DMA
    return pl.pallas_call(
        functools.partial(exchange_kernel, seq),
        out_shape=(
            jax.ShapeDtypeStruct((2, seq, frames // 2, width), BF),
            jax.ShapeDtypeStruct((2, 2, count // 2, GROUP), BF),
            jax.ShapeDtypeStruct((2, count, GROUP), BF),
            jax.ShapeDtypeStruct((HEADS, VROWS, count), BF),
            jax.ShapeDtypeStruct((5, 128), F32),
        ),
        in_specs=[smem()] + [whole()] * 5,
        out_specs=[whole()] * 5,
        scratch_shapes=[VMEM((seq, frames, width), BF), dma((seq,)), dma((seq,))],
        compiler_params=pltpu.CompilerParams(collective_id=1, has_side_effects=True, vmem_limit_bytes=TIME_LIMIT),
        cost_estimate=pl.CostEstimate(flops=4 * 10**9, bytes_accessed=10 * 10**6, transcendentals=0),
    )(lengths, computed, gain, wqkv, jnp.asarray(cosine), jnp.asarray(sines))


TIME_LIMIT = 28 * 2**20


def time_kernel(length_ref, most_ref, x_ref, wout_ref, q_ref, k_ref, v_ref, out_ref, heads_ref):
    chunks, owners, half, width = x_ref.shape
    lane = lax.broadcasted_iota(jnp.int32, (1, GROUP), 1)
    bound = jnp.maximum(most_ref[0:1, :] * most_ref[1:2, :], most_ref[2:3, :] * most_ref[3:4, :])
    fits = (jnp.max(bound) * 1.05 < SAFE * SAFE) & (jnp.max(most_ref[4:5, :]) < VSAFE)

    def attend(shift):
        def head(n, carry):
            chunk = n // HEADS
            h = n % HEADS
            g = h // 4
            mine = (lane % 128) // HALF == h % 4
            queries = jnp.where(mine, q_ref[chunk, g], jnp.zeros((), BF))
            scores = lax.dot_general(k_ref[g], queries, NT, preferred_element_type=F32)
            if shift:
                alive = lax.broadcasted_iota(jnp.int32, (k_ref.shape[1], 1), 0) < length_ref[0]
                scores = jnp.where(alive, scores, -1e30)
                scores = scores - jnp.max(scores, axis=0, keepdims=True)
            powers = jnp.exp2(scores).astype(BF)
            mixed = jnp.dot(v_ref[h], powers, preferred_element_type=F32)
            mixed = mixed[:DH] / mixed[DH : DH + 1]
            heads_ref[chunk, pl.ds(pl.multiple_of(h * DH, DH), DH), :] = mixed.astype(BF)
            return carry

        lax.fori_loop(0, chunks * HEADS, head, 0)

    @pl.when(fits)
    def _():
        attend(False)

    @pl.when(jnp.logical_not(fits))
    def _():
        attend(True)

    for chunk in range(chunks):
        projected = lax.dot_general(heads_ref[chunk], wout_ref[...], TN, preferred_element_type=F32)
        out_ref[chunk] = (x_ref[chunk].astype(F32) + projected.reshape(owners, half, width)).astype(BF)


def time_attention(lengths, most, sequence, wout, q, k, v):
    chunks, owners, half, width = sequence.shape
    return pl.pallas_call(
        time_kernel,
        out_shape=jax.ShapeDtypeStruct(sequence.shape, BF),
        in_specs=[smem()] + [whole()] * 6,
        out_specs=whole(),
        scratch_shapes=[VMEM((chunks, HEADS * DH, owners * half), BF)],
        compiler_params=pltpu.CompilerParams(vmem_limit_bytes=TIME_LIMIT),
        cost_estimate=pl.CostEstimate(flops=4 * 10**10, bytes_accessed=8 * 10**6, transcendentals=0),
    )(lengths, most, sequence, wout, q, k, v)


FRAMES_EACH = 16


def finish_kernel(
    seq, songs, length_ref, timed_ref, gain_ref, wqkv_ref, wout_ref, cot_hbm, cos_ref, sin_ref,
    out_hbm, sum_ref, got, cot_ref, heads_ref, x_ref, feat_ref, grad_ref, halves, half_in, parts, parts_in, mid, full,
    cot_sem, out_sem, send_sem, recv_sem, core_send, core_recv, plane_send, plane_recv, song_send, song_recv, back_send, back_recv, last_send, last_recv,
):
    _, bands, chunk, width = timed_ref.shape
    inner = HEADS * DH
    rows = bands * FRAMES_EACH
    blocks = chunk // FRAMES_EACH
    half = 256
    me = lax.axis_index("seq")
    song = lax.axis_index("song")
    y, x, core = me // 8, me // 2 % 4, me % 2

    def other(i):
        return (y + i // 8) % 4 * 8 + (x + i // 2 % 4) % 4 * 2 + (core + i % 2) % 2

    cot_copy = pltpu.make_async_copy(cot_hbm, cot_ref, cot_sem)
    cot_copy.start()
    barrier = pltpu.get_barrier_semaphore()

    def greet(i, carry):
        pl.semaphore_signal(barrier, inc=1, device_id=(other(i), song), device_id_type=MESH)
        return carry

    lax.fori_loop(1, seq, greet, 0)
    for d in range(1, songs):
        pl.semaphore_signal(barrier, inc=1, device_id=(me, (song + d) % songs), device_id_type=MESH)

    lane = lax.broadcasted_iota(jnp.int32, (1, GROUP), 1)
    wq = [split_halves(wqkv_ref[:, g * GROUP : (g + 1) * GROUP]) for g in range(2)]
    wk = [split_halves(wqkv_ref[:, inner + g * GROUP : inner + (g + 1) * GROUP]) for g in range(2)]
    wv = wqkv_ref[:, 2 * inner :]
    to = lax.broadcasted_iota(jnp.int32, (rows, rows), 0)
    src = lax.broadcasted_iota(jnp.int32, (rows, rows), 1)
    order = (src == to % bands * FRAMES_EACH + to // bands).astype(F32).astype(BF)
    same = (
        lax.broadcasted_iota(jnp.int32, (4 * half, half), 0) % half // bands
        == lax.broadcasted_iota(jnp.int32, (4 * half, half), 1) // bands
    )
    grad_ref[...] = jnp.zeros_like(grad_ref)
    pl.semaphore_wait(barrier, seq - 1 + songs - 1)

    def copy(n, i):
        k = other(i)
        return pltpu.make_async_remote_copy(
            src_ref=timed_ref.at[n, k], dst_ref=got.at[n, me], send_sem=send_sem.at[n, i], recv_sem=recv_sem.at[n, i],
            device_id=(k, song), device_id_type=MESH)

    for n in range(2):

        def start(i, carry):
            copy(n, seq - i).start()
            return carry

        lax.fori_loop(1, seq, start, 0)
    got[:, me] = timed_ref[:, me]
    length = length_ref[0]
    cot_copy.wait()

    def attend(n):
        def arrive(i, carry):
            copy(n, seq - i).wait()
            return carry

        lax.fori_loop(1, seq, arrive, 0)
        first = n * blocks

        def block(i, carry):
            piece = got[n, :, pl.ds(pl.multiple_of(i * FRAMES_EACH, FRAMES_EACH), FRAMES_EACH), :].reshape(rows, width)
            values_x = jnp.dot(order, piece, preferred_element_type=F32)
            here = pl.ds(pl.multiple_of((i + first) * rows, rows), rows)
            x_ref[here, :] = values_x.astype(BF)
            normed = rms_norm(values_x, gain_ref[...].reshape(1, width))
            cosine = cos_ref[...]
            sines = sin_ref[...]
            values = jnp.dot(normed, wv, preferred_element_type=F32)
            joined_groups = []
            for g in range(2):
                qa, qb = rope(jnp.dot(normed, wq[g], preferred_element_type=F32), cosine, sines)
                queries = (jnp.concatenate([qa, qb], axis=1) * (LOG2E * DH**-0.5)).astype(BF)
                ka, kb = rope(jnp.dot(normed, wk[g], preferred_element_type=F32), cosine, sines)
                keys = jnp.concatenate([ka, kb], axis=1).astype(BF)
                pieces = []
                for s in range(rows // half):
                    part = slice(s * half, (s + 1) * half)
                    stacked = jnp.concatenate(
                        [jnp.where((lane % 128) // HALF == h, queries[part], jnp.zeros((), BF)) for h in range(4)], axis=0)
                    scores = lax.dot_general(stacked, keys[part], NT, preferred_element_type=F32)
                    scores = jnp.where(same, scores, -1e30)
                    powers = jnp.exp2(scores - jnp.max(scores, axis=1, keepdims=True))
                    mixed = jnp.dot(
                        powers.astype(BF), values[part, g * GROUP : (g + 1) * GROUP].astype(BF), preferred_element_type=F32)
                    mixed = mixed / jnp.sum(powers, axis=1, keepdims=True)
                    joined = mixed[:half]
                    for h in range(1, 4):
                        joined = jnp.where(lane // DH == h, mixed[h * half : (h + 1) * half], joined)
                    pieces.append(joined.astype(BF))
                joined_groups.append(jnp.concatenate(pieces, axis=0))
            heads = jnp.concatenate(joined_groups, axis=1)
            heads_ref[here, :] = heads
            frame = me * (2 * chunk) + (i + first) * FRAMES_EACH + lax.broadcasted_iota(jnp.int32, (rows, 1), 0) // bands
            tangent = jnp.where(frame < length, cot_ref[here, :].astype(F32), 0.0).astype(BF)
            grad_ref[...] += lax.dot_general(heads, tangent, TN, preferred_element_type=F32)
            return carry

        lax.fori_loop(0, blocks, block, 0)

    def out_copy(i):
        here = slice(i * rows, (i + 1) * rows)
        return pltpu.make_async_copy(feat_ref.at[here], out_hbm.at[here], out_sem.at[i])

    def features(i):
        here = slice(i * rows, (i + 1) * rows)
        projected = jnp.dot(heads_ref[here, :], wout_ref[...], preferred_element_type=F32)
        feat_ref[here, :] = (x_ref[here, :].astype(F32) + projected).astype(BF)
        out_copy(i).start()

    attend(0)
    attend(1)

    def remote(src_ref, dst_ref, send, recv, device):
        return pltpu.make_async_remote_copy(
            src_ref=src_ref, dst_ref=dst_ref, send_sem=send, recv_sem=recv, device_id=device, device_id_type=MESH)

    twin = (me + 1 - 2 * core, song)
    plane = [(dy, dx) for dy in range(4) for dx in range(4) if dy or dx]

    def at(dy, dx):
        return ((y + dy) % 4 * 8 + (x + dx) % 4 * 2 + core, song)

    halves[...] = grad_ref[...].astype(BF).reshape(halves.shape)
    exchange_half = remote(halves.at[1 - core], half_in, core_send, core_recv, twin)
    exchange_half.start()
    exchange_half.wait()
    parts[...] = (halves[core].astype(F32) + half_in[...].astype(F32)).astype(BF).reshape(parts.shape)
    copies = [
        remote(parts.at[(x + dx) % 4 * 4 + (y + dy) % 4], parts_in.at[dx * 4 + dy], plane_send.at[dx * 4 + dy], plane_recv.at[dx * 4 + dy], at(dy, dx))
        for dy, dx in plane
    ]
    for one in copies:
        one.start()
    parts_in[0] = parts[x * 4 + y]
    features(0)
    features(1)
    for one in copies:
        one.wait()
    total = parts_in[0].astype(F32)
    for n in range(1, 16):
        total = total + parts_in[n].astype(F32)
    mid[song] = total
    copies = [
        remote(mid.at[song], mid.at[song], song_send.at[d], song_recv.at[d], (me, (song + d) % songs)) for d in range(1, songs)
    ]
    for one in copies:
        one.start()
    features(2)
    for one in copies:
        one.wait()
    total = mid[0]
    for n in range(1, songs):
        total = total + mid[n]
    full[core, x * 4 + y] = total.astype(BF)
    copies = [
        remote(full.at[core, x * 4 + y], full.at[core, x * 4 + y], back_send.at[dx * 4 + dy], back_recv.at[dx * 4 + dy], at(dy, dx))
        for dy, dx in plane
    ]
    for one in copies:
        one.start()
    features(3)
    for one in copies:
        one.wait()
    exchange_half = remote(full.at[core], full.at[core], last_send, last_recv, twin)
    exchange_half.start()
    exchange_half.wait()
    sum_ref[...] = full[...].reshape(inner, width)
    for i in range(4):
        out_copy(i).wait()


def finish(lengths, timed, gain, wqkv, wout, cotangent):
    seq = lax.axis_size("seq")
    songs = lax.axis_size("song")
    _, bands, chunk, width = timed.shape
    inner = HEADS * DH
    rows = bands * FRAMES_EACH
    count = 2 * chunk * bands
    cosine, sines = rotary_tables(np.tile(np.arange(bands), FRAMES_EACH), 4)
    dma = pltpu.SemaphoreType.DMA
    anywhere = pl.BlockSpec(memory_space=pl.ANY)
    return pl.pallas_call(
        functools.partial(finish_kernel, seq, songs),
        out_shape=(jax.ShapeDtypeStruct((count, width), BF), jax.ShapeDtypeStruct((inner, width), BF)),
        in_specs=[smem()] + [whole()] * 4 + [anywhere] + [whole()] * 2,
        out_specs=(anywhere, whole()),
        scratch_shapes=[
            VMEM((2, bands, chunk, width), BF),
            VMEM((count, width), BF),
            VMEM((count, inner), BF),
            VMEM((count, width), BF),
            VMEM((count, width), BF),
            VMEM((inner, width), F32),
            VMEM((2, inner // 2, width), BF),
            VMEM((inner // 2, width), BF),
            VMEM((16, inner // 32, width), BF),
            VMEM((16, inner // 32, width), BF),
            VMEM((songs, inner // 32, width), F32),
            VMEM((2, 16, inner // 32, width), BF),
            dma, dma((4,)), dma((2, seq)), dma((2, seq)), dma, dma, dma((16,)), dma((16,)),
            dma((songs,)), dma((songs,)), dma((16,)), dma((16,)), dma, dma,
        ],
        compiler_params=pltpu.CompilerParams(collective_id=2, has_side_effects=True, vmem_limit_bytes=36 * 2**20),
        cost_estimate=pl.CostEstimate(flops=10**10, bytes_accessed=7 * 10**6, transcendentals=0),
    )(lengths, timed, gain, wqkv, wout, cotangent, jnp.asarray(cosine), jnp.asarray(sines))


def per_device(spectrum, widths, lengths, bin_gain, embed_weight, embed_bias, time_gain, time_qkv, time_out, band_gain, band_qkv, band_out, cotangent):
    local_frames = spectrum.shape[1]
    bands, width = embed_bias.shape
    computed = embed(spectrum[0], widths, bin_gain, embed_weight, embed_bias)
    tangent = cotangent.reshape(local_frames * bands, width)
    owned, q, k, v, most = exchange(computed, lengths, time_gain, time_qkv)
    timed = time_attention(lengths, most, owned, time_out, q, k, v)
    output, gradient = finish(lengths, timed, band_gain, band_qkv, band_out, tangent)
    return output.reshape(1, local_frames, bands, width), gradient.astype(F32)


def solution(mesh):
    return jax.shard_map(
        per_device,
        mesh=mesh,
        in_specs=(P("song", "seq", None), P(), P("song"), P(), P(), P(), P(), P(), P(), P(), P(), P(), P("song", "seq", None, None)),
        out_specs=(P("song", "seq", None, None), P()),
        check_vma=False,
    )
```

```python
import functools

import jax
import jax.numpy as jnp
import numpy as np
from jax import lax
from jax.experimental import pallas as pl
from jax.experimental.pallas import tpu as pltpu
from jax.sharding import PartitionSpec as P

HEADS = 8
DH = 64
HALF = DH // 2
GROUP = 4 * DH
FLOOR = 0.25
EPSILON = 1e-05
LOG2E = 1.4426950408889634
WINDOW = 1152
NT = (((1,), (1,)), ((), ()))
TN = (((0,), (0,)), ((), ()))
MESH = pl.DeviceIdType.MESH
BF = jnp.bfloat16
F32 = jnp.float32
SAFE = 100.0
VSAFE = 2.0**12
VMEM = pltpu.VMEM
LIMIT = 56 * 2**20


def whole():
    return pl.BlockSpec(memory_space=pltpu.VMEM)


def smem():
    return pl.BlockSpec(memory_space=pltpu.SMEM)


def rotary_tables(positions, repeat):
    frequency = np.exp(-(2.0 * np.arange(HALF, dtype=np.float64) / DH) * np.log(10000.0))
    angles = positions.astype(np.float64)[:, None] * frequency
    cosine = np.tile(np.cos(angles), (1, repeat)).astype(np.float32)
    sines = np.tile(np.sin(angles), (1, repeat)).astype(np.float32)
    return cosine, sines


def split_halves(weights):
    row = lax.broadcasted_iota(jnp.int32, (GROUP, GROUP), 0)
    col = lax.broadcasted_iota(jnp.int32, (GROUP, GROUP), 1)
    source = (col % 128) // HALF * DH + col // 128 * HALF + col % HALF
    one_hot = (row == source).astype(F32).astype(BF)
    return jnp.dot(weights, one_hot, preferred_element_type=F32).astype(BF)


def rms_norm(rows, gain):
    square = jnp.mean(rows * rows, axis=-1, keepdims=True)
    return (rows * lax.rsqrt(square + EPSILON) * gain).astype(BF)


def rope(values, cosine, sines):
    leading = values[:, :128]
    second = values[:, 128:]
    return leading * cosine - second * sines, second * cosine + leading * sines


NARROW = 640


def embed_kernel(bands, widths_ref, x_ref, gain_ref, w_hbm, last_ref, bias_ref, out_ref, starts_ref, w_ref, normed_ref, tail_ref, w_sem):
    limit = x_ref.shape[1]
    main = limit // 128 * 128
    each = main // 4

    def load(n):
        here = pl.ds(n * each, each)
        return pltpu.make_async_copy(w_hbm.at[here], w_ref.at[here], w_sem.at[n])

    for n in range(4):
        load(n).start()
    total = 0
    for k in range(bands):
        starts_ref[k] = total
        total = total + widths_ref[k] * 4

    def window(k, size):
        return pl.multiple_of(jnp.minimum(starts_ref[k] // 128, (main - size) // 128) * 128, 128)

    def normalise(k, size):
        first = starts_ref[k]
        count = widths_ref[k] * 4
        begin = window(k, size)
        entry = lax.broadcasted_iota(jnp.int32, (1, size), 1) + begin
        piece = x_ref[:, pl.ds(begin, size)].astype(F32)
        piece = jnp.where((entry >= first) & (entry < first + count), piece, 0.0)
        tail = jnp.where(k == bands - 1, x_ref[:, main:].astype(F32), 0.0)
        square = jnp.sum(piece * piece, axis=1, keepdims=True) + jnp.sum(tail * tail, axis=1, keepdims=True)
        scale = 1.0 / jnp.sqrt(jnp.maximum(square / count.astype(F32), FLOOR))
        normed_ref[k, :, :size] = (piece * scale * gain_ref[:, pl.ds(begin, size)]).astype(BF)
        tail_ref[k] = (tail * scale * gain_ref[:, main:]).astype(BF)

    def project(k, size):
        summed = jnp.dot(normed_ref[k, :, :size], w_ref[pl.ds(window(k, size), size), :], preferred_element_type=F32)
        summed = summed + bias_ref[pl.ds(k, 1), :]
        tail = tail_ref[k].astype(F32)
        rows = last_ref[...].astype(F32)
        for e in range(limit - main):
            summed = summed + tail[:, e : e + 1] * rows[e : e + 1, :]
        out_ref[k] = summed.astype(BF)

    def step(work, i, carry):
        narrow = widths_ref[4 * i] * 4 <= NARROW - 124
        for j in range(1, 4):
            narrow = narrow & (widths_ref[4 * i + j] * 4 <= NARROW - 124)

        @pl.when(narrow)
        def _():
            for j in range(4):
                work(4 * i + j, NARROW)

        @pl.when(jnp.logical_not(narrow))
        def _():
            for j in range(4):
                work(4 * i + j, WINDOW)

        return carry

    lax.fori_loop(0, bands // 4, functools.partial(step, normalise), 0)
    for n in range(4):
        load(n).wait()
    lax.fori_loop(0, bands // 4, functools.partial(step, project), 0)


def embed(spectrum, widths, bin_gain, embed_weight, embed_bias):
    frames, feature_count = spectrum.shape
    bands, width = embed_bias.shape
    main = feature_count // 128 * 128

    def full(*shape):
        return pl.BlockSpec(shape, lambda i: (0,) * len(shape))

    return pl.pallas_call(
        functools.partial(embed_kernel, bands),
        grid=(1,),
        out_shape=jax.ShapeDtypeStruct((bands, frames, width), BF),
        in_specs=[
            smem(), full(frames, feature_count), full(1, feature_count), pl.BlockSpec(memory_space=pl.ANY),
            pl.BlockSpec((16, width), lambda i: (main // 16, 0)), full(bands, width),
        ],
        out_specs=full(bands, frames, width),
        scratch_shapes=[
            pltpu.SMEM((bands,), jnp.int32),
            VMEM((main, width), BF),
            VMEM((bands, frames, WINDOW), BF),
            VMEM((bands, frames, feature_count - main), BF),
            pltpu.SemaphoreType.DMA((4,)),
        ],
        compiler_params=pltpu.CompilerParams(vmem_limit_bytes=60 * 2**20),
        cost_estimate=pl.CostEstimate(flops=2 * 10**9, bytes_accessed=9 * 10**6, transcendentals=0),
    )(widths, spectrum, bin_gain[None], embed_weight, embed_weight, embed_bias)


VROWS = 128


def exchange_kernel(
    seq, length_ref, bands_ref, gain_ref, wqkv_ref, cos_ref, sin_ref,
    x_ref, q_ref, k_ref, v_ref, most_ref, got, send_sem, recv_sem,
):
    frames, width = got.shape[1:]
    half = frames // 2
    inner = HEADS * DH
    me = lax.axis_index("seq")
    song = lax.axis_index("song")
    y, x, core = me // 8, me // 2 % 4, me % 2

    def other(i, sign):
        return (y + sign * (i // 8) + 4) % 4 * 8 + (x + sign * (i // 2 % 4) + 4) % 4 * 2 + (core + i % 2) % 2

    barrier = pltpu.get_barrier_semaphore()

    def greet(i, carry):
        pl.semaphore_signal(barrier, inc=1, device_id=(other(i, 1), song), device_id_type=MESH)
        return carry

    lax.fori_loop(1, seq, greet, 0)
    lane = lax.broadcasted_iota(jnp.int32, (1, GROUP), 1)
    wq = [split_halves(wqkv_ref[:, g * GROUP : (g + 1) * GROUP]) for g in range(2)]
    wk = [split_halves(wqkv_ref[:, inner + g * GROUP : inner + (g + 1) * GROUP]) for g in range(2)]
    wv = wqkv_ref[:, 2 * inner :]
    pl.semaphore_wait(barrier, seq - 1)

    def copy(i):
        k = other(i, 1)
        return pltpu.make_async_remote_copy(
            src_ref=bands_ref.at[k], dst_ref=got.at[me], send_sem=send_sem.at[i], recv_sem=recv_sem.at[i],
            device_id=(k, song), device_id_type=MESH)

    def start(j, carry):
        copy(8 * (1 + 2 * (j % 2)) + j // 2).start()
        return carry

    def start_rest(j, carry):
        copy(16 + j).start()
        copy(j).start()
        return carry

    lax.fori_loop(0, 16, start, 0)
    copy(16).start()
    lax.fori_loop(1, 8, start_rest, 0)
    got[me] = bands_ref[me]
    length = length_ref[0]

    heads_of = lax.broadcasted_iota(jnp.int32, (GROUP, 128), 0) % 128 // HALF
    per_head = (heads_of == lax.broadcasted_iota(jnp.int32, (GROUP, 128), 1)).astype(F32).astype(BF)

    def longest(rows):
        squares = jnp.dot((rows * rows).astype(BF), per_head, preferred_element_type=F32)
        return jnp.max(squares, axis=0, keepdims=True)

    def project(dy, stats):
        row = (y - dy + 4) % 4

        def wait(i, carry):
            copy(8 * dy + i).wait_recv()
            return carry

        lax.fori_loop(1 if dy == 0 else 0, 8, wait, 0)
        owners = pl.ds(pl.multiple_of(row * 8, 8), 8)
        count = 8 * frames
        base = pl.multiple_of(row * count, count)
        rows = pl.ds(base, count)
        received = got[owners]
        x_ref[0, owners] = received[:, :half]
        x_ref[1, owners] = received[:, half:]
        normed = rms_norm(received.reshape(count, width).astype(F32), gain_ref[...].reshape(1, width))
        cosine = cos_ref[rows, :]
        sines = sin_ref[rows, :]
        alive_row = (lax.broadcasted_iota(jnp.int32, (count, 1), 0) + base) < length
        alive_col = (lax.broadcasted_iota(jnp.int32, (1, count), 1) + base) < length
        kinds = []
        for g in range(2):
            qa, qb = rope(jnp.dot(normed, wq[g], preferred_element_type=F32), cosine, sines)
            scaled = jnp.concatenate([qa, qb], axis=1) * (LOG2E * DH**-0.5)
            parts = scaled.reshape(8, frames, GROUP)
            for n in range(2):
                later = pl.ds(pl.multiple_of(row * 8 * half + n * seq * half, 8 * half), 8 * half)
                q_ref[g, later, :] = parts[:, n * half : (n + 1) * half].reshape(8 * half, GROUP).astype(BF)
            ka, kb = rope(jnp.dot(normed, wk[g], preferred_element_type=F32), cosine, sines)
            keys = jnp.concatenate([ka, kb], axis=1)
            keys = jnp.where(alive_row, keys, 0.0)
            k_ref[g, rows, :] = keys.astype(BF)
            kinds.append(longest(scaled))
            kinds.append(longest(keys))
        values = lax.dot_general(wv, normed, (((0,), (1,)), ((), ())), preferred_element_type=F32)
        values = jnp.where(alive_col, values, 0.0)
        vmost = jnp.max(jnp.max(jnp.abs(values), axis=0, keepdims=True), axis=1, keepdims=True)
        kinds.append(jnp.broadcast_to(vmost, (1, 128)))
        values = values.astype(BF)
        ones = jnp.broadcast_to(jnp.where(alive_col, 1.0, 0.0), (VROWS - DH, count)).astype(BF)
        for h in range(HEADS):
            v_ref[h, :DH, rows] = values[h * DH : (h + 1) * DH]
            v_ref[h, DH:, rows] = ones
        if stats is None:
            return kinds
        return [jnp.maximum(p, n) for p, n in zip(stats, kinds)]

    stats = None
    for dy in (1, 3, 0, 2):
        stats = project(dy, stats)
    for n, row in enumerate(stats):
        most_ref[n : n + 1, :] = row

    def finish(i, carry):
        copy(i).wait_send()
        return carry

    lax.fori_loop(1, seq, finish, 0)


def exchange(computed, lengths, gain, wqkv):
    seq = lax.axis_size("seq")
    bands, frames, width = computed.shape
    count = seq * frames
    cosine, sines = rotary_tables(np.arange(count), 4)
    dma = pltpu.SemaphoreType.DMA
    return pl.pallas_call(
        functools.partial(exchange_kernel, seq),
        out_shape=(
            jax.ShapeDtypeStruct((2, seq, frames // 2, width), BF),
            jax.ShapeDtypeStruct((2, count, GROUP), BF),
            jax.ShapeDtypeStruct((2, count, GROUP), BF),
            jax.ShapeDtypeStruct((HEADS, VROWS, count), BF),
            jax.ShapeDtypeStruct((5, 128), F32),
        ),
        in_specs=[smem()] + [whole()] * 5,
        out_specs=[whole()] * 5,
        scratch_shapes=[VMEM((seq, frames, width), BF), dma((seq,)), dma((seq,))],
        compiler_params=pltpu.CompilerParams(collective_id=1, has_side_effects=True, vmem_limit_bytes=TIME_LIMIT),
        cost_estimate=pl.CostEstimate(flops=4 * 10**9, bytes_accessed=10 * 10**6, transcendentals=0),
    )(lengths, computed, gain, wqkv, jnp.asarray(cosine), jnp.asarray(sines))


TIME_LIMIT = 28 * 2**20


def time_kernel(length_ref, most_ref, x_ref, wout_ref, q_ref, k_ref, v_ref, out_ref, heads_ref):
    chunks, owners, half, width = x_ref.shape
    lane = lax.broadcasted_iota(jnp.int32, (1, GROUP), 1)
    bound = jnp.maximum(most_ref[0:1, :] * most_ref[1:2, :], most_ref[2:3, :] * most_ref[3:4, :])
    fits = (jnp.max(bound) * 1.05 < SAFE * SAFE) & (jnp.max(most_ref[4:5, :]) < VSAFE)

    def head(h, rows, shift):
        g = h // 4
        mine = (lane % 128) // HALF == h % 4
        queries = jnp.where(mine, q_ref[g, rows, :], jnp.zeros((), BF))
        scores = lax.dot_general(k_ref[g], queries, NT, preferred_element_type=F32)
        if shift:
            alive = lax.broadcasted_iota(jnp.int32, (k_ref.shape[1], 1), 0) < length_ref[0]
            scores = jnp.where(alive, scores, -1e30)
            scores = scores - jnp.max(scores, axis=0, keepdims=True)
        powers = jnp.exp2(scores).astype(BF)
        mixed = jnp.dot(v_ref[h], powers, preferred_element_type=F32)
        mixed = mixed[:DH] * (1.0 / mixed[DH : DH + 1])
        heads_ref[pl.ds(pl.multiple_of(h * DH, DH), DH), rows] = mixed.astype(BF)

    columns = owners * half

    @pl.when(fits)
    def _():
        def step(h, carry):
            head(h, slice(0, chunks * columns), False)
            return carry

        lax.fori_loop(0, HEADS, step, 0)

    @pl.when(jnp.logical_not(fits))
    def _():
        def step(n, carry):
            head(n % HEADS, pl.ds(pl.multiple_of(n // HEADS * columns, columns), columns), True)
            return carry

        lax.fori_loop(0, chunks * HEADS, step, 0)

    for chunk in range(chunks):
        heads = heads_ref[:, chunk * columns : (chunk + 1) * columns]
        projected = lax.dot_general(heads, wout_ref[...], TN, preferred_element_type=F32)
        out_ref[chunk] = (x_ref[chunk].astype(F32) + projected.reshape(owners, half, width)).astype(BF)


def time_attention(lengths, most, sequence, wout, q, k, v):
    chunks, owners, half, width = sequence.shape
    return pl.pallas_call(
        time_kernel,
        out_shape=jax.ShapeDtypeStruct(sequence.shape, BF),
        in_specs=[smem()] + [whole()] * 6,
        out_specs=whole(),
        scratch_shapes=[VMEM((HEADS * DH, chunks * owners * half), BF)],
        compiler_params=pltpu.CompilerParams(vmem_limit_bytes=44 * 2**20),
        cost_estimate=pl.CostEstimate(flops=4 * 10**10, bytes_accessed=8 * 10**6, transcendentals=0),
    )(lengths, most, sequence, wout, q, k, v)


FRAMES_EACH = 16


def finish_kernel(
    seq, songs, length_ref, timed_ref, gain_ref, wqkv_ref, wout_ref, cot_hbm, cos_ref, sin_ref,
    out_hbm, sum_ref, got, cot_ref, heads_ref, x_ref, feat_ref, grad_ref, halves, half_in, parts, parts_in, mid, full,
    cot_sem, out_sem, send_sem, recv_sem, core_send, core_recv, plane_send, plane_recv, song_send, song_recv, back_send, back_recv, last_send, last_recv,
):
    _, bands, chunk, width = timed_ref.shape
    inner = HEADS * DH
    rows = bands * FRAMES_EACH
    blocks = chunk // FRAMES_EACH
    half = 256
    me = lax.axis_index("seq")
    song = lax.axis_index("song")
    y, x, core = me // 8, me // 2 % 4, me % 2

    def other(i):
        return (y + i // 8) % 4 * 8 + (x + i // 2 % 4) % 4 * 2 + (core + i % 2) % 2

    cot_copy = pltpu.make_async_copy(cot_hbm, cot_ref, cot_sem)
    cot_copy.start()
    barrier = pltpu.get_barrier_semaphore()

    def greet(i, carry):
        pl.semaphore_signal(barrier, inc=1, device_id=(other(i), song), device_id_type=MESH)
        return carry

    lax.fori_loop(1, seq, greet, 0)
    for d in range(1, songs):
        pl.semaphore_signal(barrier, inc=1, device_id=(me, (song + d) % songs), device_id_type=MESH)

    lane = lax.broadcasted_iota(jnp.int32, (1, GROUP), 1)
    wq = [split_halves(wqkv_ref[:, g * GROUP : (g + 1) * GROUP]) for g in range(2)]
    wk = [split_halves(wqkv_ref[:, inner + g * GROUP : inner + (g + 1) * GROUP]) for g in range(2)]
    wv = wqkv_ref[:, 2 * inner :]
    to = lax.broadcasted_iota(jnp.int32, (rows, rows), 0)
    src = lax.broadcasted_iota(jnp.int32, (rows, rows), 1)
    order = (src == to % bands * FRAMES_EACH + to // bands).astype(F32).astype(BF)
    same = (
        lax.broadcasted_iota(jnp.int32, (4 * half, half), 0) % half // bands
        == lax.broadcasted_iota(jnp.int32, (4 * half, half), 1) // bands
    )
    grad_ref[...] = jnp.zeros_like(grad_ref)
    pl.semaphore_wait(barrier, seq - 1 + songs - 1)

    pieces = [(0, slice(0, chunk)), (1, slice(0, FRAMES_EACH)), (1, slice(FRAMES_EACH, 2 * FRAMES_EACH))]

    def copy(p, i):
        k = other(i)
        n, frames = pieces[p]
        return pltpu.make_async_remote_copy(
            src_ref=timed_ref.at[n, k, frames], dst_ref=got.at[n, me, frames], send_sem=send_sem.at[p, i], recv_sem=recv_sem.at[p, i],
            device_id=(k, song), device_id_type=MESH)

    for p in range(3):

        def start(i, carry):
            copy(p, seq - i).start()
            return carry

        lax.fori_loop(1, seq, start, 0)
    got[:, me] = timed_ref[:, me]
    length = length_ref[0]
    cot_copy.wait()

    def attend(p):
        def arrive(i, carry):
            copy(p, seq - i).wait()
            return carry

        lax.fori_loop(1, seq, arrive, 0)
        n, frames = pieces[p]

        def block(i, carry):
            first = n * blocks
            piece = got[n, :, pl.ds(pl.multiple_of(i * FRAMES_EACH, FRAMES_EACH), FRAMES_EACH), :].reshape(rows, width)
            values_x = jnp.dot(order, piece, preferred_element_type=F32)
            here = pl.ds(pl.multiple_of((i + first) * rows, rows), rows)
            x_ref[here, :] = values_x.astype(BF)
            normed = rms_norm(values_x, gain_ref[...].reshape(1, width))
            cosine = cos_ref[...]
            sines = sin_ref[...]
            values = jnp.dot(normed, wv, preferred_element_type=F32)
            joined_groups = []
            for g in range(2):
                qa, qb = rope(jnp.dot(normed, wq[g], preferred_element_type=F32), cosine, sines)
                queries = (jnp.concatenate([qa, qb], axis=1) * (LOG2E * DH**-0.5)).astype(BF)
                ka, kb = rope(jnp.dot(normed, wk[g], preferred_element_type=F32), cosine, sines)
                keys = jnp.concatenate([ka, kb], axis=1).astype(BF)
                stacks = []
                for s in range(rows // half):
                    part = slice(s * half, (s + 1) * half)
                    stacked = jnp.concatenate(
                        [jnp.where((lane % 128) // HALF == h, queries[part], jnp.zeros((), BF)) for h in range(4)], axis=0)
                    scores = lax.dot_general(stacked, keys[part], NT, preferred_element_type=F32)
                    scores = jnp.where(same, scores, -1e30)
                    powers = jnp.exp2(scores - jnp.max(scores, axis=1, keepdims=True))
                    mixed = jnp.dot(
                        powers.astype(BF), values[part, g * GROUP : (g + 1) * GROUP].astype(BF), preferred_element_type=F32)
                    mixed = mixed / jnp.sum(powers, axis=1, keepdims=True)
                    joined = mixed[:half]
                    for h in range(1, 4):
                        joined = jnp.where(lane // DH == h, mixed[h * half : (h + 1) * half], joined)
                    stacks.append(joined.astype(BF))
                joined_groups.append(jnp.concatenate(stacks, axis=0))
            heads = jnp.concatenate(joined_groups, axis=1)
            heads_ref[here, :] = heads
            frame = me * (2 * chunk) + (i + first) * FRAMES_EACH + lax.broadcasted_iota(jnp.int32, (rows, 1), 0) // bands
            tangent = jnp.where(frame < length, cot_ref[here, :].astype(F32), 0.0).astype(BF)
            grad_ref[...] += lax.dot_general(heads, tangent, TN, preferred_element_type=F32)
            return carry

        lax.fori_loop(frames.start // FRAMES_EACH, frames.stop // FRAMES_EACH, block, 0)

    def out_copy(i):
        here = slice(i * rows, (i + 1) * rows)
        return pltpu.make_async_copy(feat_ref.at[here], out_hbm.at[here], out_sem.at[i])

    def features(i):
        here = slice(i * rows, (i + 1) * rows)
        projected = jnp.dot(heads_ref[here, :], wout_ref[...], preferred_element_type=F32)
        feat_ref[here, :] = (x_ref[here, :].astype(F32) + projected).astype(BF)
        out_copy(i).start()

    attend(0)
    attend(1)
    attend(2)

    def remote(src_ref, dst_ref, send, recv, device):
        return pltpu.make_async_remote_copy(
            src_ref=src_ref, dst_ref=dst_ref, send_sem=send, recv_sem=recv, device_id=device, device_id_type=MESH)

    twin = (me + 1 - 2 * core, song)
    plane = [(dy, dx) for dy in range(4) for dx in range(4) if dy or dx]

    def at(dy, dx):
        return ((y + dy) % 4 * 8 + (x + dx) % 4 * 2 + core, song)

    halves[...] = grad_ref[...].astype(BF).reshape(halves.shape)
    exchange_half = remote(halves.at[1 - core], half_in, core_send, core_recv, twin)
    exchange_half.start()
    exchange_half.wait()
    parts[...] = (halves[core].astype(F32) + half_in[...].astype(F32)).astype(BF).reshape(parts.shape)
    copies = [
        remote(parts.at[(x + dx) % 4 * 4 + (y + dy) % 4], parts_in.at[dx * 4 + dy], plane_send.at[dx * 4 + dy], plane_recv.at[dx * 4 + dy], at(dy, dx))
        for dy, dx in plane
    ]
    for one in copies:
        one.start()
    parts_in[0] = parts[x * 4 + y]
    features(0)
    features(1)
    for one in copies:
        one.wait()
    total = parts_in[0].astype(F32)
    for n in range(1, 16):
        total = total + parts_in[n].astype(F32)
    mid[song] = total
    copies = [
        remote(mid.at[song], mid.at[song], song_send.at[d], song_recv.at[d], (me, (song + d) % songs)) for d in range(1, songs)
    ]
    for one in copies:
        one.start()
    features(2)
    for one in copies:
        one.wait()
    total = mid[0]
    for n in range(1, songs):
        total = total + mid[n]
    full[core, x * 4 + y] = total.astype(BF)
    copies = [
        remote(full.at[core, x * 4 + y], full.at[core, x * 4 + y], back_send.at[dx * 4 + dy], back_recv.at[dx * 4 + dy], at(dy, dx))
        for dy, dx in plane
    ]
    for one in copies:
        one.start()
    features(3)
    for one in copies:
        one.wait()
    exchange_half = remote(full.at[core], full.at[core], last_send, last_recv, twin)
    exchange_half.start()
    exchange_half.wait()
    sum_ref[...] = full[...].reshape(inner, width)
    for i in range(4):
        out_copy(i).wait()


def finish(lengths, timed, gain, wqkv, wout, cotangent):
    seq = lax.axis_size("seq")
    songs = lax.axis_size("song")
    _, bands, chunk, width = timed.shape
    inner = HEADS * DH
    rows = bands * FRAMES_EACH
    count = 2 * chunk * bands
    cosine, sines = rotary_tables(np.tile(np.arange(bands), FRAMES_EACH), 4)
    dma = pltpu.SemaphoreType.DMA
    anywhere = pl.BlockSpec(memory_space=pl.ANY)
    return pl.pallas_call(
        functools.partial(finish_kernel, seq, songs),
        out_shape=(jax.ShapeDtypeStruct((count, width), BF), jax.ShapeDtypeStruct((inner, width), BF)),
        in_specs=[smem()] + [whole()] * 4 + [anywhere] + [whole()] * 2,
        out_specs=(anywhere, whole()),
        scratch_shapes=[
            VMEM((2, bands, chunk, width), BF),
            VMEM((count, width), BF),
            VMEM((count, inner), BF),
            VMEM((count, width), BF),
            VMEM((count, width), BF),
            VMEM((inner, width), F32),
            VMEM((2, inner // 2, width), BF),
            VMEM((inner // 2, width), BF),
            VMEM((16, inner // 32, width), BF),
            VMEM((16, inner // 32, width), BF),
            VMEM((songs, inner // 32, width), F32),
            VMEM((2, 16, inner // 32, width), BF),
            dma, dma((4,)), dma((3, seq)), dma((3, seq)), dma, dma, dma((16,)), dma((16,)),
            dma((songs,)), dma((songs,)), dma((16,)), dma((16,)), dma, dma,
        ],
        compiler_params=pltpu.CompilerParams(collective_id=2, has_side_effects=True, vmem_limit_bytes=36 * 2**20),
        cost_estimate=pl.CostEstimate(flops=10**10, bytes_accessed=7 * 10**6, transcendentals=0),
    )(lengths, timed, gain, wqkv, wout, cotangent, jnp.asarray(cosine), jnp.asarray(sines))


def per_device(spectrum, widths, lengths, bin_gain, embed_weight, embed_bias, time_gain, time_qkv, time_out, band_gain, band_qkv, band_out, cotangent):
    local_frames = spectrum.shape[1]
    bands, width = embed_bias.shape
    computed = embed(spectrum[0], widths, bin_gain, embed_weight, embed_bias)
    tangent = cotangent.reshape(local_frames * bands, width)
    owned, q, k, v, most = exchange(computed, lengths, time_gain, time_qkv)
    timed = time_attention(lengths, most, owned, time_out, q, k, v)
    output, gradient = finish(lengths, timed, band_gain, band_qkv, band_out, tangent)
    return output.reshape(1, local_frames, bands, width), gradient.astype(F32)


def solution(mesh):
    return jax.shard_map(
        per_device,
        mesh=mesh,
        in_specs=(P("song", "seq", None), P(), P("song"), P(), P(), P(), P(), P(), P(), P(), P(), P(), P("song", "seq", None, None)),
        out_specs=(P("song", "seq", None, None), P()),
        check_vma=False,
    )
```

```python
import functools

import jax
import jax.numpy as jnp
import numpy as np
from jax import lax
from jax.experimental import pallas as pl
from jax.experimental.pallas import tpu as pltpu
from jax.sharding import PartitionSpec as P

HEADS = 8
DH = 64
HALF = DH // 2
GROUP = 4 * DH
FLOOR = 0.25
EPSILON = 1e-05
LOG2E = 1.4426950408889634
WINDOW = 1152
NT = (((1,), (1,)), ((), ()))
TN = (((0,), (0,)), ((), ()))
MESH = pl.DeviceIdType.MESH
BF = jnp.bfloat16
F32 = jnp.float32
SAFE = 100.0
VSAFE = 2.0**12
VMEM = pltpu.VMEM
LIMIT = 56 * 2**20


def whole():
    return pl.BlockSpec(memory_space=pltpu.VMEM)


def smem():
    return pl.BlockSpec(memory_space=pltpu.SMEM)


def rotary_tables(positions, repeat):
    frequency = np.exp(-(2.0 * np.arange(HALF, dtype=np.float64) / DH) * np.log(10000.0))
    angles = positions.astype(np.float64)[:, None] * frequency
    cosine = np.tile(np.cos(angles), (1, repeat)).astype(np.float32)
    sines = np.tile(np.sin(angles), (1, repeat)).astype(np.float32)
    return cosine, sines


def split_halves(weights):
    row = lax.broadcasted_iota(jnp.int32, (GROUP, GROUP), 0)
    col = lax.broadcasted_iota(jnp.int32, (GROUP, GROUP), 1)
    source = (col % 128) // HALF * DH + col // 128 * HALF + col % HALF
    one_hot = (row == source).astype(F32).astype(BF)
    return jnp.dot(weights, one_hot, preferred_element_type=F32).astype(BF)


def rms_norm(rows, gain):
    square = jnp.mean(rows * rows, axis=-1, keepdims=True)
    return (rows * lax.rsqrt(square + EPSILON) * gain).astype(BF)


def rope(values, cosine, sines):
    leading = values[:, :128]
    second = values[:, 128:]
    return leading * cosine - second * sines, second * cosine + leading * sines


VROWS = 128


def exchange_kernel(
    seq, length_ref, meta_ref, spectrum_ref, bin_gain_ref, w_hbm, last_ref, bias_ref, gain_ref, wqkv_ref, cos_ref, sin_ref,
    x_ref, q_ref, k_ref, v_ref, most_ref, got, stage, w_ref, spec_ref, spec_gain_ref, w_sem, send_sem, recv_sem,
):
    frames, width = got.shape[1:]
    half = frames // 2
    inner = HEADS * DH
    me = lax.axis_index("seq")
    song = lax.axis_index("song")
    y, x, core = me // 8, me // 2 % 4, me % 2

    def other(i, sign):
        return (y + sign * (i // 8) + 4) % 4 * 8 + (x + sign * (i // 2 % 4) + 4) % 4 * 2 + (core + i % 2) % 2

    barrier = pltpu.get_barrier_semaphore()

    def greet(i, carry):
        pl.semaphore_signal(barrier, inc=1, device_id=(other(i, 1), song), device_id_type=MESH)
        return carry

    lax.fori_loop(1, seq, greet, 0)
    blocks = w_ref.shape[0]
    main = blocks * 128
    bands = bias_ref.shape[0]

    def load(n):
        return pltpu.make_async_copy(w_hbm.at[pl.ds(pl.multiple_of(n * 128, 128), 128)], w_ref.at[n], w_sem.at[n])

    def start_load(n, carry):
        load(n).start()
        return carry

    def wait_load(n, carry):
        load(n).wait()
        return carry

    lax.fori_loop(0, blocks, start_load, 0)
    for n in range(blocks):
        spec_ref[n] = spectrum_ref[:, n * 128 : (n + 1) * 128]
        spec_gain_ref[n] = bin_gain_ref[:, n * 128 : (n + 1) * 128]
    lane = lax.broadcasted_iota(jnp.int32, (1, GROUP), 1)
    wq = [split_halves(wqkv_ref[:, g * GROUP : (g + 1) * GROUP]) for g in range(2)]
    wk = [split_halves(wqkv_ref[:, inner + g * GROUP : inner + (g + 1) * GROUP]) for g in range(2)]
    wv = wqkv_ref[:, 2 * inner :]
    lax.fori_loop(0, blocks, wait_load, 0)

    def band(k):
        first = meta_ref[0, k]
        count = meta_ref[1, k]
        block = meta_ref[2, k]
        near = range(WINDOW // 128)
        entry = lax.broadcasted_iota(jnp.int32, (1, WINDOW), 1) + block * 128
        piece = jnp.concatenate([spec_ref[block + n] for n in near], axis=1).astype(F32)
        gains = jnp.concatenate([spec_gain_ref[block + n] for n in near], axis=1)
        weights = jnp.concatenate([w_ref[block + n] for n in near], axis=0)
        piece = jnp.where((entry >= first) & (entry < first + count), piece, 0.0)
        tail = jnp.where(k == bands - 1, spectrum_ref[:, main:].astype(F32), 0.0)
        square = jnp.sum(piece * piece, axis=1, keepdims=True) + jnp.sum(tail * tail, axis=1, keepdims=True)
        scale = 1.0 / jnp.sqrt(jnp.maximum(square / count.astype(F32), FLOOR))
        normed = (piece * scale * gains).astype(BF)
        summed = jnp.dot(normed, weights, preferred_element_type=F32) + bias_ref[pl.ds(k, 1), :]
        tail = (tail * scale * bin_gain_ref[:, main:]).astype(BF).astype(F32)
        rows = last_ref[...].astype(F32)
        for e in range(spectrum_ref.shape[1] - main):
            summed = summed + tail[:, e : e + 1] * rows[e : e + 1, :]
        stage[k] = summed.astype(BF)

    def copy(i):
        k = other(i, 1)
        return pltpu.make_async_remote_copy(
            src_ref=stage.at[k], dst_ref=got.at[me], send_sem=send_sem.at[i], recv_sem=recv_sem.at[i],
            device_id=(k, song), device_id_type=MESH)

    def front(j, carry):
        for n in range(2):
            band(other(8 + 16 * n + j, 1))
        for n in range(2):
            copy(8 + 16 * n + j).start()
        return carry

    def back(j, carry):
        for n in range(2):
            band(other(j + 16 * n, 1))
        for n in range(2):
            copy(j + 16 * n).start()
        return carry

    pl.semaphore_wait(barrier, seq - 1)
    lax.fori_loop(0, 8, front, 0)
    band(other(16, 1))
    copy(16).start()
    lax.fori_loop(1, 8, back, 0)
    band(me)
    got[me] = stage[me]
    length = length_ref[0]

    heads_of = lax.broadcasted_iota(jnp.int32, (GROUP, 128), 0) % 128 // HALF
    per_head = (heads_of == lax.broadcasted_iota(jnp.int32, (GROUP, 128), 1)).astype(F32).astype(BF)

    def longest(rows):
        squares = jnp.dot((rows * rows).astype(BF), per_head, preferred_element_type=F32)
        return jnp.max(squares, axis=0, keepdims=True)

    def project(dy, stats):
        row = (y - dy + 4) % 4

        def wait(i, carry):
            copy(8 * dy + i).wait_recv()
            return carry

        lax.fori_loop(1 if dy == 0 else 0, 8, wait, 0)
        owners = pl.ds(pl.multiple_of(row * 8, 8), 8)
        count = 8 * frames
        base = pl.multiple_of(row * count, count)
        rows = pl.ds(base, count)
        received = got[owners]
        x_ref[0, owners] = received[:, :half]
        x_ref[1, owners] = received[:, half:]
        normed = rms_norm(received.reshape(count, width).astype(F32), gain_ref[...].reshape(1, width))
        cosine = cos_ref[rows, :]
        sines = sin_ref[rows, :]
        alive_row = (lax.broadcasted_iota(jnp.int32, (count, 1), 0) + base) < length
        alive_col = (lax.broadcasted_iota(jnp.int32, (1, count), 1) + base) < length
        kinds = []
        for g in range(2):
            qa, qb = rope(jnp.dot(normed, wq[g], preferred_element_type=F32), cosine, sines)
            scaled = jnp.concatenate([qa, qb], axis=1) * (LOG2E * DH**-0.5)
            parts = scaled.reshape(8, frames, GROUP)
            for n in range(2):
                later = pl.ds(pl.multiple_of(row * 8 * half + n * seq * half, 8 * half), 8 * half)
                q_ref[g, later, :] = parts[:, n * half : (n + 1) * half].reshape(8 * half, GROUP).astype(BF)
            ka, kb = rope(jnp.dot(normed, wk[g], preferred_element_type=F32), cosine, sines)
            keys = jnp.concatenate([ka, kb], axis=1)
            keys = jnp.where(alive_row, keys, 0.0)
            k_ref[g, rows, :] = keys.astype(BF)
            kinds.append(longest(scaled))
            kinds.append(longest(keys))
        values = lax.dot_general(wv, normed, (((0,), (1,)), ((), ())), preferred_element_type=F32)
        values = jnp.where(alive_col, values, 0.0)
        vmost = jnp.max(jnp.max(jnp.abs(values), axis=0, keepdims=True), axis=1, keepdims=True)
        kinds.append(jnp.broadcast_to(vmost, (1, 128)))
        values = values.astype(BF)
        ones = jnp.broadcast_to(jnp.where(alive_col, 1.0, 0.0), (VROWS - DH, count)).astype(BF)
        for h in range(HEADS):
            v_ref[h, :DH, rows] = values[h * DH : (h + 1) * DH]
            v_ref[h, DH:, rows] = ones
        if stats is None:
            return kinds
        return [jnp.maximum(p, n) for p, n in zip(stats, kinds)]

    stats = None
    for dy in (1, 3, 0, 2):
        stats = project(dy, stats)
    for n, row in enumerate(stats):
        most_ref[n : n + 1, :] = row

    def finish(i, carry):
        copy(i).wait_send()
        return carry

    lax.fori_loop(1, seq, finish, 0)


def exchange(spectrum, widths, bin_gain, embed_weight, embed_bias, lengths, gain, wqkv):
    seq = lax.axis_size("seq")
    frames, feature_count = spectrum.shape
    bands, width = embed_bias.shape
    count = seq * frames
    blocks = feature_count // 128
    main = blocks * 128
    starts = (jnp.cumsum(widths) - widths) * 4
    meta = jnp.stack([starts, widths * 4, jnp.minimum(starts // 128, blocks - WINDOW // 128)]).astype(jnp.int32)
    cosine, sines = rotary_tables(np.arange(count), 4)
    dma = pltpu.SemaphoreType.DMA

    def full(*shape):
        return pl.BlockSpec(shape, lambda i: (0,) * len(shape))

    shapes = [(2, seq, frames // 2, width), (2, count, GROUP), (2, count, GROUP), (HEADS, VROWS, count)]
    return pl.pallas_call(
        functools.partial(exchange_kernel, seq),
        grid=(1,),
        out_shape=[jax.ShapeDtypeStruct(shape, BF) for shape in shapes] + [jax.ShapeDtypeStruct((5, 128), F32)],
        in_specs=[
            smem(), smem(), full(frames, feature_count), full(1, feature_count), pl.BlockSpec(memory_space=pl.ANY),
            pl.BlockSpec((16, width), lambda i: (main // 16, 0)), full(bands, width), full(width), full(*wqkv.shape),
            full(count, 128), full(count, 128),
        ],
        out_specs=[full(*shape) for shape in shapes] + [full(5, 128)],
        scratch_shapes=[
            VMEM((seq, frames, width), BF),
            VMEM((bands, frames, width), BF),
            VMEM((blocks, 128, width), BF),
            VMEM((blocks, frames, 128), BF),
            VMEM((blocks, 1, 128), F32),
            dma((blocks,)), dma((seq,)), dma((seq,)),
        ],
        compiler_params=pltpu.CompilerParams(collective_id=1, has_side_effects=True, vmem_limit_bytes=36 * 2**20),
        cost_estimate=pl.CostEstimate(flops=4 * 10**9, bytes_accessed=10 * 10**6, transcendentals=0),
    )(lengths, meta, spectrum, bin_gain[None], embed_weight, embed_weight, embed_bias, gain, wqkv, jnp.asarray(cosine), jnp.asarray(sines))


TIME_LIMIT = 28 * 2**20


def time_kernel(length_ref, most_ref, x_ref, wout_ref, q_ref, k_ref, v_ref, out_ref, heads_ref):
    chunks, owners, half, width = x_ref.shape
    lane = lax.broadcasted_iota(jnp.int32, (1, GROUP), 1)
    bound = jnp.maximum(most_ref[0:1, :] * most_ref[1:2, :], most_ref[2:3, :] * most_ref[3:4, :])
    fits = (jnp.max(bound) * 1.05 < SAFE * SAFE) & (jnp.max(most_ref[4:5, :]) < VSAFE)

    def head(h, rows, shift):
        g = h // 4
        mine = (lane % 128) // HALF == h % 4
        queries = jnp.where(mine, q_ref[g, rows, :], jnp.zeros((), BF))
        scores = lax.dot_general(k_ref[g], queries, NT, preferred_element_type=F32)
        if shift:
            alive = lax.broadcasted_iota(jnp.int32, (k_ref.shape[1], 1), 0) < length_ref[0]
            scores = jnp.where(alive, scores, -1e30)
            scores = scores - jnp.max(scores, axis=0, keepdims=True)
        powers = jnp.exp2(scores).astype(BF)
        mixed = jnp.dot(v_ref[h], powers, preferred_element_type=F32)
        mixed = mixed[:DH] * (1.0 / mixed[DH : DH + 1])
        heads_ref[pl.ds(pl.multiple_of(h * DH, DH), DH), rows] = mixed.astype(BF)

    columns = owners * half

    @pl.when(fits)
    def _():
        def step(h, carry):
            head(h, slice(0, chunks * columns), False)
            return carry

        lax.fori_loop(0, HEADS, step, 0)

    @pl.when(jnp.logical_not(fits))
    def _():
        def step(n, carry):
            head(n % HEADS, pl.ds(pl.multiple_of(n // HEADS * columns, columns), columns), True)
            return carry

        lax.fori_loop(0, chunks * HEADS, step, 0)

    for chunk in range(chunks):
        heads = heads_ref[:, chunk * columns : (chunk + 1) * columns]
        projected = lax.dot_general(heads, wout_ref[...], TN, preferred_element_type=F32)
        out_ref[chunk] = (x_ref[chunk].astype(F32) + projected.reshape(owners, half, width)).astype(BF)


def time_attention(lengths, most, sequence, wout, q, k, v):
    chunks, owners, half, width = sequence.shape
    return pl.pallas_call(
        time_kernel,
        out_shape=jax.ShapeDtypeStruct(sequence.shape, BF),
        in_specs=[smem()] + [whole()] * 6,
        out_specs=whole(),
        scratch_shapes=[VMEM((HEADS * DH, chunks * owners * half), BF)],
        compiler_params=pltpu.CompilerParams(vmem_limit_bytes=36 * 2**20),
        cost_estimate=pl.CostEstimate(flops=4 * 10**10, bytes_accessed=8 * 10**6, transcendentals=0),
    )(lengths, most, sequence, wout, q, k, v)


FRAMES_EACH = 16


def finish_kernel(
    seq, songs, length_ref, timed_ref, gain_ref, wqkv_ref, wout_ref, cot_hbm, cos_ref, sin_ref,
    out_hbm, sum_ref, got, cot_ref, heads_ref, x_ref, feat_ref, grad_ref, halves, half_in, parts, parts_in, mid, full,
    cot_sem, out_sem, send_sem, recv_sem, core_send, core_recv, plane_send, plane_recv, song_send, song_recv, back_send, back_recv, last_send, last_recv,
):
    _, bands, chunk, width = timed_ref.shape
    inner = HEADS * DH
    rows = bands * FRAMES_EACH
    blocks = chunk // FRAMES_EACH
    half = 256
    me = lax.axis_index("seq")
    song = lax.axis_index("song")
    y, x, core = me // 8, me // 2 % 4, me % 2

    def other(i):
        return (y + i // 8) % 4 * 8 + (x + i // 2 % 4) % 4 * 2 + (core + i % 2) % 2

    cot_copy = pltpu.make_async_copy(cot_hbm, cot_ref, cot_sem)
    cot_copy.start()
    barrier = pltpu.get_barrier_semaphore()

    def greet(i, carry):
        pl.semaphore_signal(barrier, inc=1, device_id=(other(i), song), device_id_type=MESH)
        return carry

    lax.fori_loop(1, seq, greet, 0)
    for d in range(1, songs):
        pl.semaphore_signal(barrier, inc=1, device_id=(me, (song + d) % songs), device_id_type=MESH)

    lane = lax.broadcasted_iota(jnp.int32, (1, GROUP), 1)
    wq = [split_halves(wqkv_ref[:, g * GROUP : (g + 1) * GROUP]) for g in range(2)]
    wk = [split_halves(wqkv_ref[:, inner + g * GROUP : inner + (g + 1) * GROUP]) for g in range(2)]
    wv = wqkv_ref[:, 2 * inner :]
    to = lax.broadcasted_iota(jnp.int32, (rows, rows), 0)
    src = lax.broadcasted_iota(jnp.int32, (rows, rows), 1)
    order = (src == to % bands * FRAMES_EACH + to // bands).astype(F32).astype(BF)
    same = (
        lax.broadcasted_iota(jnp.int32, (4 * half, half), 0) % half // bands
        == lax.broadcasted_iota(jnp.int32, (4 * half, half), 1) // bands
    )
    grad_ref[...] = jnp.zeros_like(grad_ref)
    pl.semaphore_wait(barrier, seq - 1 + songs - 1)

    pieces = [(0, slice(0, chunk)), (1, slice(0, FRAMES_EACH)), (1, slice(FRAMES_EACH, 2 * FRAMES_EACH))]

    def copy(p, i):
        k = other(i)
        n, frames = pieces[p]
        return pltpu.make_async_remote_copy(
            src_ref=timed_ref.at[n, k, frames], dst_ref=got.at[n, me, frames], send_sem=send_sem.at[p, i], recv_sem=recv_sem.at[p, i],
            device_id=(k, song), device_id_type=MESH)

    for p in range(3):

        def start(i, carry):
            copy(p, seq - i).start()
            return carry

        lax.fori_loop(1, seq, start, 0)
    got[:, me] = timed_ref[:, me]
    length = length_ref[0]
    cot_copy.wait()

    def attend(p):
        def arrive(i, carry):
            copy(p, seq - i).wait()
            return carry

        lax.fori_loop(1, seq, arrive, 0)
        n, frames = pieces[p]

        def block(i, carry):
            first = n * blocks
            piece = got[n, :, pl.ds(pl.multiple_of(i * FRAMES_EACH, FRAMES_EACH), FRAMES_EACH), :].reshape(rows, width)
            values_x = jnp.dot(order, piece, preferred_element_type=F32)
            here = pl.ds(pl.multiple_of((i + first) * rows, rows), rows)
            x_ref[here, :] = values_x.astype(BF)
            normed = rms_norm(values_x, gain_ref[...].reshape(1, width))
            cosine = cos_ref[...]
            sines = sin_ref[...]
            values = jnp.dot(normed, wv, preferred_element_type=F32)
            joined_groups = []
            for g in range(2):
                qa, qb = rope(jnp.dot(normed, wq[g], preferred_element_type=F32), cosine, sines)
                queries = (jnp.concatenate([qa, qb], axis=1) * (LOG2E * DH**-0.5)).astype(BF)
                ka, kb = rope(jnp.dot(normed, wk[g], preferred_element_type=F32), cosine, sines)
                keys = jnp.concatenate([ka, kb], axis=1).astype(BF)
                stacks = []
                for s in range(rows // half):
                    part = slice(s * half, (s + 1) * half)
                    stacked = jnp.concatenate(
                        [jnp.where((lane % 128) // HALF == h, queries[part], jnp.zeros((), BF)) for h in range(4)], axis=0)
                    scores = lax.dot_general(stacked, keys[part], NT, preferred_element_type=F32)
                    scores = jnp.where(same, scores, -1e30)
                    powers = jnp.exp2(scores - jnp.max(scores, axis=1, keepdims=True))
                    mixed = jnp.dot(
                        powers.astype(BF), values[part, g * GROUP : (g + 1) * GROUP].astype(BF), preferred_element_type=F32)
                    mixed = mixed / jnp.sum(powers, axis=1, keepdims=True)
                    joined = mixed[:half]
                    for h in range(1, 4):
                        joined = jnp.where(lane // DH == h, mixed[h * half : (h + 1) * half], joined)
                    stacks.append(joined.astype(BF))
                joined_groups.append(jnp.concatenate(stacks, axis=0))
            heads = jnp.concatenate(joined_groups, axis=1)
            heads_ref[here, :] = heads
            frame = me * (2 * chunk) + (i + first) * FRAMES_EACH + lax.broadcasted_iota(jnp.int32, (rows, 1), 0) // bands
            tangent = jnp.where(frame < length, cot_ref[here, :].astype(F32), 0.0).astype(BF)
            grad_ref[...] += lax.dot_general(heads, tangent, TN, preferred_element_type=F32)
            return carry

        lax.fori_loop(frames.start // FRAMES_EACH, frames.stop // FRAMES_EACH, block, 0)

    def out_copy(i):
        here = slice(i * rows, (i + 1) * rows)
        return pltpu.make_async_copy(feat_ref.at[here], out_hbm.at[here], out_sem.at[i])

    def features(i):
        here = slice(i * rows, (i + 1) * rows)
        projected = jnp.dot(heads_ref[here, :], wout_ref[...], preferred_element_type=F32)
        feat_ref[here, :] = (x_ref[here, :].astype(F32) + projected).astype(BF)
        out_copy(i).start()

    attend(0)
    attend(1)
    attend(2)

    def remote(src_ref, dst_ref, send, recv, device):
        return pltpu.make_async_remote_copy(
            src_ref=src_ref, dst_ref=dst_ref, send_sem=send, recv_sem=recv, device_id=device, device_id_type=MESH)

    twin = (me + 1 - 2 * core, song)
    plane = [(dy, dx) for dy in range(4) for dx in range(4) if dy or dx]

    def at(dy, dx):
        return ((y + dy) % 4 * 8 + (x + dx) % 4 * 2 + core, song)

    halves[...] = grad_ref[...].astype(BF).reshape(halves.shape)
    exchange_half = remote(halves.at[1 - core], half_in, core_send, core_recv, twin)
    exchange_half.start()
    exchange_half.wait()
    parts[...] = (halves[core].astype(F32) + half_in[...].astype(F32)).astype(BF).reshape(parts.shape)
    copies = [
        remote(parts.at[(x + dx) % 4 * 4 + (y + dy) % 4], parts_in.at[dx * 4 + dy], plane_send.at[dx * 4 + dy], plane_recv.at[dx * 4 + dy], at(dy, dx))
        for dy, dx in plane
    ]
    for one in copies:
        one.start()
    parts_in[0] = parts[x * 4 + y]
    features(0)
    features(1)
    for one in copies:
        one.wait()
    total = parts_in[0].astype(F32)
    for n in range(1, 16):
        total = total + parts_in[n].astype(F32)
    mid[song] = total
    copies = [
        remote(mid.at[song], mid.at[song], song_send.at[d], song_recv.at[d], (me, (song + d) % songs)) for d in range(1, songs)
    ]
    for one in copies:
        one.start()
    features(2)
    for one in copies:
        one.wait()
    total = mid[0]
    for n in range(1, songs):
        total = total + mid[n]
    full[core, x * 4 + y] = total.astype(BF)
    copies = [
        remote(full.at[core, x * 4 + y], full.at[core, x * 4 + y], back_send.at[dx * 4 + dy], back_recv.at[dx * 4 + dy], at(dy, dx))
        for dy, dx in plane
    ]
    for one in copies:
        one.start()
    features(3)
    for one in copies:
        one.wait()
    exchange_half = remote(full.at[core], full.at[core], last_send, last_recv, twin)
    exchange_half.start()
    exchange_half.wait()
    sum_ref[...] = full[...].reshape(inner, width)
    for i in range(4):
        out_copy(i).wait()


def finish(lengths, timed, gain, wqkv, wout, cotangent):
    seq = lax.axis_size("seq")
    songs = lax.axis_size("song")
    _, bands, chunk, width = timed.shape
    inner = HEADS * DH
    rows = bands * FRAMES_EACH
    count = 2 * chunk * bands
    cosine, sines = rotary_tables(np.tile(np.arange(bands), FRAMES_EACH), 4)
    dma = pltpu.SemaphoreType.DMA
    anywhere = pl.BlockSpec(memory_space=pl.ANY)
    return pl.pallas_call(
        functools.partial(finish_kernel, seq, songs),
        out_shape=(jax.ShapeDtypeStruct((count, width), BF), jax.ShapeDtypeStruct((inner, width), BF)),
        in_specs=[smem()] + [whole()] * 4 + [anywhere] + [whole()] * 2,
        out_specs=(anywhere, whole()),
        scratch_shapes=[
            VMEM((2, bands, chunk, width), BF),
            VMEM((count, width), BF),
            VMEM((count, inner), BF),
            VMEM((count, width), BF),
            VMEM((count, width), BF),
            VMEM((inner, width), F32),
            VMEM((2, inner // 2, width), BF),
            VMEM((inner // 2, width), BF),
            VMEM((16, inner // 32, width), BF),
            VMEM((16, inner // 32, width), BF),
            VMEM((songs, inner // 32, width), F32),
            VMEM((2, 16, inner // 32, width), BF),
            dma, dma((4,)), dma((3, seq)), dma((3, seq)), dma, dma, dma((16,)), dma((16,)),
            dma((songs,)), dma((songs,)), dma((16,)), dma((16,)), dma, dma,
        ],
        compiler_params=pltpu.CompilerParams(collective_id=2, has_side_effects=True, vmem_limit_bytes=36 * 2**20),
        cost_estimate=pl.CostEstimate(flops=10**10, bytes_accessed=7 * 10**6, transcendentals=0),
    )(lengths, timed, gain, wqkv, wout, cotangent, jnp.asarray(cosine), jnp.asarray(sines))


def per_device(spectrum, widths, lengths, bin_gain, embed_weight, embed_bias, time_gain, time_qkv, time_out, band_gain, band_qkv, band_out, cotangent):
    local_frames = spectrum.shape[1]
    bands, width = embed_bias.shape
    tangent = cotangent.reshape(local_frames * bands, width)
    owned, q, k, v, most = exchange(spectrum[0], widths, bin_gain, embed_weight, embed_bias, lengths, time_gain, time_qkv)
    timed = time_attention(lengths, most, owned, time_out, q, k, v)
    output, gradient = finish(lengths, timed, band_gain, band_qkv, band_out, tangent)
    return output.reshape(1, local_frames, bands, width), gradient.astype(F32)


def solution(mesh):
    return jax.shard_map(
        per_device,
        mesh=mesh,
        in_specs=(P("song", "seq", None), P(), P("song"), P(), P(), P(), P(), P(), P(), P(), P(), P(), P("song", "seq", None, None)),
        out_specs=(P("song", "seq", None, None), P()),
        check_vma=False,
    )
```

```python
import functools

import jax
import jax.numpy as jnp
import numpy as np
from jax import lax
from jax.experimental import pallas as pl
from jax.experimental.pallas import tpu as pltpu
from jax.sharding import PartitionSpec as P

HEADS = 8
DH = 64
HALF = DH // 2
GROUP = 4 * DH
FLOOR = 0.25
EPSILON = 1e-05
LOG2E = 1.4426950408889634
WINDOW = 1152
NT = (((1,), (1,)), ((), ()))
TN = (((0,), (0,)), ((), ()))
MESH = pl.DeviceIdType.MESH
BF = jnp.bfloat16
F32 = jnp.float32
SAFE = 100.0
VSAFE = 2.0**12
VMEM = pltpu.VMEM
LIMIT = 56 * 2**20


def whole():
    return pl.BlockSpec(memory_space=pltpu.VMEM)


def smem():
    return pl.BlockSpec(memory_space=pltpu.SMEM)


def rotary_tables(positions, repeat):
    frequency = np.exp(-(2.0 * np.arange(HALF, dtype=np.float64) / DH) * np.log(10000.0))
    angles = positions.astype(np.float64)[:, None] * frequency
    cosine = np.tile(np.cos(angles), (1, repeat)).astype(np.float32)
    sines = np.tile(np.sin(angles), (1, repeat)).astype(np.float32)
    return cosine, sines


def split_halves(weights):
    row = lax.broadcasted_iota(jnp.int32, (GROUP, GROUP), 0)
    col = lax.broadcasted_iota(jnp.int32, (GROUP, GROUP), 1)
    source = (col % 128) // HALF * DH + col // 128 * HALF + col % HALF
    one_hot = (row == source).astype(F32).astype(BF)
    return jnp.dot(weights, one_hot, preferred_element_type=F32).astype(BF)


def rms_norm(rows, gain):
    square = jnp.mean(rows * rows, axis=-1, keepdims=True)
    return (rows * lax.rsqrt(square + EPSILON) * gain).astype(BF)


def rope(values, cosine, sines):
    leading = values[:, :128]
    second = values[:, 128:]
    return leading * cosine - second * sines, second * cosine + leading * sines


VROWS = 128


def exchange_kernel(
    seq, length_ref, meta_ref, spectrum_ref, bin_gain_ref, w_hbm, last_ref, bias_ref, gain_ref, wqkv_ref, table_ref,
    x_ref, q_ref, k_ref, v_ref, most_ref, got, stage, w_ref, spec_ref, spec_gain_ref, w_sem, send_sem, recv_sem,
):
    frames, width = got.shape[1:]
    half = frames // 2
    inner = HEADS * DH
    me = lax.axis_index("seq")
    song = lax.axis_index("song")
    y, x, core = me // 8, me // 2 % 4, me % 2

    def other(i, sign):
        return (y + sign * (i // 8) + 4) % 4 * 8 + (x + sign * (i // 2 % 4) + 4) % 4 * 2 + (core + i % 2) % 2

    barrier = pltpu.get_barrier_semaphore()

    def greet(i, carry):
        pl.semaphore_signal(barrier, inc=1, device_id=(other(i, 1), song), device_id_type=MESH)
        return carry

    lax.fori_loop(1, seq, greet, 0)
    blocks = w_ref.shape[0]
    main = blocks * 128
    bands = bias_ref.shape[0]

    def load(n):
        return pltpu.make_async_copy(w_hbm.at[pl.ds(pl.multiple_of(n * 128, 128), 128)], w_ref.at[n], w_sem.at[n])

    def start_load(n, carry):
        load(n).start()
        return carry

    def wait_load(n, carry):
        load(n).wait()
        return carry

    lax.fori_loop(0, blocks, start_load, 0)
    for n in range(blocks):
        spec_ref[n] = spectrum_ref[:, n * 128 : (n + 1) * 128]
        spec_gain_ref[n] = bin_gain_ref[:, n * 128 : (n + 1) * 128]
    lane = lax.broadcasted_iota(jnp.int32, (1, GROUP), 1)
    wq = [split_halves(wqkv_ref[:, g * GROUP : (g + 1) * GROUP]) for g in range(2)]
    wk = [split_halves(wqkv_ref[:, inner + g * GROUP : inner + (g + 1) * GROUP]) for g in range(2)]
    wv = wqkv_ref[:, 2 * inner :]
    lax.fori_loop(0, blocks, wait_load, 0)

    def band(k):
        first = meta_ref[0, k]
        count = meta_ref[1, k]
        block = meta_ref[2, k]
        near = range(WINDOW // 128)
        entry = lax.broadcasted_iota(jnp.int32, (1, WINDOW), 1) + block * 128
        piece = jnp.concatenate([spec_ref[block + n] for n in near], axis=1).astype(F32)
        gains = jnp.concatenate([spec_gain_ref[block + n] for n in near], axis=1)
        weights = jnp.concatenate([w_ref[block + n] for n in near], axis=0)
        piece = jnp.where((entry >= first) & (entry < first + count), piece, 0.0)
        tail = jnp.where(k == bands - 1, spectrum_ref[:, main:].astype(F32), 0.0)
        square = jnp.sum(piece * piece, axis=1, keepdims=True) + jnp.sum(tail * tail, axis=1, keepdims=True)
        scale = 1.0 / jnp.sqrt(jnp.maximum(square / count.astype(F32), FLOOR))
        normed = (piece * scale * gains).astype(BF)
        summed = jnp.dot(normed, weights, preferred_element_type=F32) + bias_ref[pl.ds(k, 1), :]
        tail = (tail * scale * bin_gain_ref[:, main:]).astype(BF).astype(F32)
        rows = last_ref[...].astype(F32)
        for e in range(spectrum_ref.shape[1] - main):
            summed = summed + tail[:, e : e + 1] * rows[e : e + 1, :]
        stage[k] = summed.astype(BF)

    def copy(i):
        k = other(i, 1)
        return pltpu.make_async_remote_copy(
            src_ref=stage.at[k], dst_ref=got.at[me], send_sem=send_sem.at[i], recv_sem=recv_sem.at[i],
            device_id=(k, song), device_id_type=MESH)

    def front(j, carry):
        for n in range(2):
            band(other(8 + 16 * n + j, 1))
        for n in range(2):
            copy(8 + 16 * n + j).start()
        return carry

    def back(j, carry):
        for n in range(2):
            band(other(j + 16 * n, 1))
        for n in range(2):
            copy(j + 16 * n).start()
        return carry

    pl.semaphore_wait(barrier, seq - 1)
    lax.fori_loop(0, 8, front, 0)
    band(other(16, 1))
    copy(16).start()
    lax.fori_loop(1, 8, back, 0)
    band(me)
    got[me] = stage[me]
    length = length_ref[0]

    heads_of = lax.broadcasted_iota(jnp.int32, (GROUP, 128), 0) % 128 // HALF
    per_head = (heads_of == lax.broadcasted_iota(jnp.int32, (GROUP, 128), 1)).astype(F32).astype(BF)

    def longest(rows):
        squares = jnp.dot((rows * rows).astype(BF), per_head, preferred_element_type=F32)
        return jnp.max(squares, axis=0, keepdims=True)

    def project(dy, stats):
        row = (y - dy + 4) % 4

        def wait(i, carry):
            copy(8 * dy + i).wait_recv()
            return carry

        lax.fori_loop(1 if dy == 0 else 0, 8, wait, 0)
        owners = pl.ds(pl.multiple_of(row * 8, 8), 8)
        count = 8 * frames
        base = pl.multiple_of(row * count, count)
        rows = pl.ds(base, count)
        received = got[owners]
        x_ref[0, owners] = received[:, :half]
        x_ref[1, owners] = received[:, half:]
        normed = rms_norm(received.reshape(count, width).astype(F32), gain_ref[...].reshape(1, width))
        cosines, sine_parts = [], []
        for o in range(8):
            far = pl.ds(row * 8 + o, 1)
            cosines.append(table_ref[0, far, :] * table_ref[0, seq:, :] - table_ref[1, far, :] * table_ref[1, seq:, :])
            sine_parts.append(table_ref[1, far, :] * table_ref[0, seq:, :] + table_ref[0, far, :] * table_ref[1, seq:, :])
        cosine = jnp.concatenate(cosines, axis=0)
        sines = jnp.concatenate(sine_parts, axis=0)
        alive_row = (lax.broadcasted_iota(jnp.int32, (count, 1), 0) + base) < length
        alive_col = (lax.broadcasted_iota(jnp.int32, (1, count), 1) + base) < length
        kinds = []
        for g in range(2):
            qa, qb = rope(jnp.dot(normed, wq[g], preferred_element_type=F32), cosine, sines)
            scaled = jnp.concatenate([qa, qb], axis=1) * (LOG2E * DH**-0.5)
            parts = scaled.reshape(8, frames, GROUP)
            for n in range(2):
                later = pl.ds(pl.multiple_of(row * 8 * half + n * seq * half, 8 * half), 8 * half)
                q_ref[g, later, :] = parts[:, n * half : (n + 1) * half].reshape(8 * half, GROUP).astype(BF)
            ka, kb = rope(jnp.dot(normed, wk[g], preferred_element_type=F32), cosine, sines)
            keys = jnp.concatenate([ka, kb], axis=1)
            keys = jnp.where(alive_row, keys, 0.0)
            k_ref[g, rows, :] = keys.astype(BF)
            kinds.append(longest(scaled))
            kinds.append(longest(keys))
        values = lax.dot_general(wv, normed, (((0,), (1,)), ((), ())), preferred_element_type=F32)
        values = jnp.where(alive_col, values, 0.0)
        vmost = jnp.max(jnp.max(jnp.abs(values), axis=0, keepdims=True), axis=1, keepdims=True)
        kinds.append(jnp.broadcast_to(vmost, (1, 128)))
        values = values.astype(BF)
        ones = jnp.broadcast_to(jnp.where(alive_col, 1.0, 0.0), (VROWS - DH, count)).astype(BF)
        for h in range(HEADS):
            v_ref[h, :DH, rows] = values[h * DH : (h + 1) * DH]
            v_ref[h, DH:, rows] = ones
        if stats is None:
            return kinds
        return [jnp.maximum(p, n) for p, n in zip(stats, kinds)]

    stats = None
    for dy in (1, 3, 0, 2):
        stats = project(dy, stats)
    for n, row in enumerate(stats):
        most_ref[n : n + 1, :] = row

    def finish(i, carry):
        copy(i).wait_send()
        return carry

    lax.fori_loop(1, seq, finish, 0)


def exchange(spectrum, widths, bin_gain, embed_weight, embed_bias, lengths, gain, wqkv):
    seq = lax.axis_size("seq")
    frames, feature_count = spectrum.shape
    bands, width = embed_bias.shape
    count = seq * frames
    blocks = feature_count // 128
    main = blocks * 128
    starts = (jnp.cumsum(widths) - widths) * 4
    meta = jnp.stack([starts, widths * 4, jnp.minimum(starts // 128, blocks - WINDOW // 128)]).astype(jnp.int32)
    positions = np.concatenate([np.arange(seq) * frames, np.arange(frames)])
    table = np.stack(rotary_tables(positions, 4))
    dma = pltpu.SemaphoreType.DMA

    def full(*shape):
        return pl.BlockSpec(shape, lambda i: (0,) * len(shape))

    anywhere = pl.BlockSpec(memory_space=pl.ANY)
    shapes = [(2, seq, frames // 2, width), (2, count, GROUP), (2, count, GROUP), (HEADS, VROWS, count)]
    return pl.pallas_call(
        functools.partial(exchange_kernel, seq),
        grid=(1,),
        out_shape=[jax.ShapeDtypeStruct(shape, BF) for shape in shapes] + [jax.ShapeDtypeStruct((5, 128), F32)],
        in_specs=[
            smem(), smem(), full(frames, feature_count), full(1, feature_count), anywhere,
            pl.BlockSpec((16, width), lambda i: (main // 16, 0)), full(bands, width), full(width), full(*wqkv.shape),
            full(*table.shape),
        ],
        out_specs=[full(*shape) for shape in shapes] + [full(5, 128)],
        scratch_shapes=[
            VMEM((seq, frames, width), BF),
            VMEM((bands, frames, width), BF),
            VMEM((blocks, 128, width), BF),
            VMEM((blocks, frames, 128), BF),
            VMEM((blocks, 1, 128), F32),
            dma((blocks,)), dma((seq,)), dma((seq,)),
        ],
        compiler_params=pltpu.CompilerParams(collective_id=1, has_side_effects=True, vmem_limit_bytes=42 * 2**20),
        cost_estimate=pl.CostEstimate(flops=4 * 10**9, bytes_accessed=10 * 10**6, transcendentals=0),
    )(lengths, meta, spectrum, bin_gain[None], embed_weight, embed_weight, embed_bias, gain, wqkv, jnp.asarray(table))


TIME_LIMIT = 28 * 2**20


def time_kernel(length_ref, most_ref, x_ref, wout_ref, q_ref, k_ref, v_ref, out_ref, heads_ref):
    chunks, owners, half, width = x_ref.shape
    lane = lax.broadcasted_iota(jnp.int32, (1, GROUP), 1)
    bound = jnp.maximum(most_ref[0:1, :] * most_ref[1:2, :], most_ref[2:3, :] * most_ref[3:4, :])
    fits = (jnp.max(bound) * 1.05 < SAFE * SAFE) & (jnp.max(most_ref[4:5, :]) < VSAFE)

    def head(h, rows, shift):
        g = h // 4
        mine = (lane % 128) // HALF == h % 4
        queries = jnp.where(mine, q_ref[g, rows, :], jnp.zeros((), BF))
        scores = lax.dot_general(k_ref[g], queries, NT, preferred_element_type=F32)
        if shift:
            alive = lax.broadcasted_iota(jnp.int32, (k_ref.shape[1], 1), 0) < length_ref[0]
            scores = jnp.where(alive, scores, -1e30)
            scores = scores - jnp.max(scores, axis=0, keepdims=True)
        powers = jnp.exp2(scores).astype(BF)
        mixed = jnp.dot(v_ref[h], powers, preferred_element_type=F32)
        mixed = mixed[:DH] * (1.0 / mixed[DH : DH + 1])
        heads_ref[pl.ds(pl.multiple_of(h * DH, DH), DH), rows] = mixed.astype(BF)

    columns = owners * half

    @pl.when(fits)
    def _():
        def step(h, carry):
            head(h, slice(0, chunks * columns), False)
            return carry

        lax.fori_loop(0, HEADS, step, 0)

    @pl.when(jnp.logical_not(fits))
    def _():
        def step(n, carry):
            head(n % HEADS, pl.ds(pl.multiple_of(n // HEADS * columns, columns), columns), True)
            return carry

        lax.fori_loop(0, chunks * HEADS, step, 0)

    for chunk in range(chunks):
        heads = heads_ref[:, chunk * columns : (chunk + 1) * columns]
        projected = lax.dot_general(heads, wout_ref[...], TN, preferred_element_type=F32)
        out_ref[chunk] = (x_ref[chunk].astype(F32) + projected.reshape(owners, half, width)).astype(BF)


def time_attention(lengths, most, sequence, wout, q, k, v):
    chunks, owners, half, width = sequence.shape
    return pl.pallas_call(
        time_kernel,
        out_shape=jax.ShapeDtypeStruct(sequence.shape, BF),
        in_specs=[smem()] + [whole()] * 6,
        out_specs=whole(),
        scratch_shapes=[VMEM((HEADS * DH, chunks * owners * half), BF)],
        compiler_params=pltpu.CompilerParams(vmem_limit_bytes=36 * 2**20),
        cost_estimate=pl.CostEstimate(flops=4 * 10**10, bytes_accessed=8 * 10**6, transcendentals=0),
    )(lengths, most, sequence, wout, q, k, v)


FRAMES_EACH = 16


def finish_kernel(
    seq, songs, length_ref, timed_ref, gain_ref, wqkv_ref, wout_ref, cot_hbm, cos_ref, sin_ref,
    out_hbm, sum_ref, got, cot_ref, heads_ref, x_ref, feat_ref, grad_ref, halves, half_in, parts, parts_in, mid, full,
    cot_sem, out_sem, send_sem, recv_sem, core_send, core_recv, plane_send, plane_recv, song_send, song_recv, back_send, back_recv, last_send, last_recv,
):
    _, bands, chunk, width = timed_ref.shape
    inner = HEADS * DH
    rows = bands * FRAMES_EACH
    blocks = chunk // FRAMES_EACH
    half = 256
    me = lax.axis_index("seq")
    song = lax.axis_index("song")
    y, x, core = me // 8, me // 2 % 4, me % 2

    def other(i):
        return (y + i // 8) % 4 * 8 + (x + i // 2 % 4) % 4 * 2 + (core + i % 2) % 2

    cot_copy = pltpu.make_async_copy(cot_hbm, cot_ref, cot_sem)
    cot_copy.start()
    barrier = pltpu.get_barrier_semaphore()

    def greet(i, carry):
        pl.semaphore_signal(barrier, inc=1, device_id=(other(i), song), device_id_type=MESH)
        return carry

    lax.fori_loop(1, seq, greet, 0)
    for d in range(1, songs):
        pl.semaphore_signal(barrier, inc=1, device_id=(me, (song + d) % songs), device_id_type=MESH)

    lane = lax.broadcasted_iota(jnp.int32, (1, GROUP), 1)
    wq = [split_halves(wqkv_ref[:, g * GROUP : (g + 1) * GROUP]) for g in range(2)]
    wk = [split_halves(wqkv_ref[:, inner + g * GROUP : inner + (g + 1) * GROUP]) for g in range(2)]
    wv = wqkv_ref[:, 2 * inner :]
    to = lax.broadcasted_iota(jnp.int32, (rows, rows), 0)
    src = lax.broadcasted_iota(jnp.int32, (rows, rows), 1)
    order = (src == to % bands * FRAMES_EACH + to // bands).astype(F32).astype(BF)
    same = (
        lax.broadcasted_iota(jnp.int32, (4 * half, half), 0) % half // bands
        == lax.broadcasted_iota(jnp.int32, (4 * half, half), 1) // bands
    )
    grad_ref[...] = jnp.zeros_like(grad_ref)
    pl.semaphore_wait(barrier, seq - 1 + songs - 1)

    pieces = [(0, slice(0, chunk)), (1, slice(0, FRAMES_EACH)), (1, slice(FRAMES_EACH, 2 * FRAMES_EACH))]

    def copy(p, i):
        k = other(i)
        n, frames = pieces[p]
        return pltpu.make_async_remote_copy(
            src_ref=timed_ref.at[n, k, frames], dst_ref=got.at[n, me, frames], send_sem=send_sem.at[p, i], recv_sem=recv_sem.at[p, i],
            device_id=(k, song), device_id_type=MESH)

    for p in range(3):

        def start(i, carry):
            copy(p, seq - i).start()
            return carry

        lax.fori_loop(1, seq, start, 0)
    got[:, me] = timed_ref[:, me]
    length = length_ref[0]
    cot_copy.wait()

    def attend(p):
        def arrive(i, carry):
            copy(p, seq - i).wait()
            return carry

        lax.fori_loop(1, seq, arrive, 0)
        n, frames = pieces[p]

        def block(i, carry):
            first = n * blocks
            piece = got[n, :, pl.ds(pl.multiple_of(i * FRAMES_EACH, FRAMES_EACH), FRAMES_EACH), :].reshape(rows, width)
            values_x = jnp.dot(order, piece, preferred_element_type=F32)
            here = pl.ds(pl.multiple_of((i + first) * rows, rows), rows)
            x_ref[here, :] = values_x.astype(BF)
            normed = rms_norm(values_x, gain_ref[...].reshape(1, width))
            cosine = cos_ref[...]
            sines = sin_ref[...]
            values = jnp.dot(normed, wv, preferred_element_type=F32)
            joined_groups = []
            for g in range(2):
                qa, qb = rope(jnp.dot(normed, wq[g], preferred_element_type=F32), cosine, sines)
                queries = (jnp.concatenate([qa, qb], axis=1) * (LOG2E * DH**-0.5)).astype(BF)
                ka, kb = rope(jnp.dot(normed, wk[g], preferred_element_type=F32), cosine, sines)
                keys = jnp.concatenate([ka, kb], axis=1).astype(BF)
                stacks = []
                for s in range(rows // half):
                    part = slice(s * half, (s + 1) * half)
                    stacked = jnp.concatenate(
                        [jnp.where((lane % 128) // HALF == h, queries[part], jnp.zeros((), BF)) for h in range(4)], axis=0)
                    scores = lax.dot_general(stacked, keys[part], NT, preferred_element_type=F32)
                    scores = jnp.where(same, scores, -1e30)
                    powers = jnp.exp2(scores - jnp.max(scores, axis=1, keepdims=True))
                    mixed = jnp.dot(
                        powers.astype(BF), values[part, g * GROUP : (g + 1) * GROUP].astype(BF), preferred_element_type=F32)
                    mixed = mixed / jnp.sum(powers, axis=1, keepdims=True)
                    joined = mixed[:half]
                    for h in range(1, 4):
                        joined = jnp.where(lane // DH == h, mixed[h * half : (h + 1) * half], joined)
                    stacks.append(joined.astype(BF))
                joined_groups.append(jnp.concatenate(stacks, axis=0))
            heads = jnp.concatenate(joined_groups, axis=1)
            heads_ref[here, :] = heads
            frame = me * (2 * chunk) + (i + first) * FRAMES_EACH + lax.broadcasted_iota(jnp.int32, (rows, 1), 0) // bands
            tangent = jnp.where(frame < length, cot_ref[here, :].astype(F32), 0.0).astype(BF)
            grad_ref[...] += lax.dot_general(heads, tangent, TN, preferred_element_type=F32)
            return carry

        lax.fori_loop(frames.start // FRAMES_EACH, frames.stop // FRAMES_EACH, block, 0)

    def out_copy(i):
        here = slice(i * rows, (i + 1) * rows)
        return pltpu.make_async_copy(feat_ref.at[here], out_hbm.at[here], out_sem.at[i])

    def features(i):
        here = slice(i * rows, (i + 1) * rows)
        projected = jnp.dot(heads_ref[here, :], wout_ref[...], preferred_element_type=F32)
        feat_ref[here, :] = (x_ref[here, :].astype(F32) + projected).astype(BF)
        out_copy(i).start()

    attend(0)
    attend(1)
    attend(2)

    def remote(src_ref, dst_ref, send, recv, device):
        return pltpu.make_async_remote_copy(
            src_ref=src_ref, dst_ref=dst_ref, send_sem=send, recv_sem=recv, device_id=device, device_id_type=MESH)

    twin = (me + 1 - 2 * core, song)
    plane = [(dy, dx) for dy in range(4) for dx in range(4) if dy or dx]

    def at(dy, dx):
        return ((y + dy) % 4 * 8 + (x + dx) % 4 * 2 + core, song)

    halves[...] = grad_ref[...].astype(BF).reshape(halves.shape)
    exchange_half = remote(halves.at[1 - core], half_in, core_send, core_recv, twin)
    exchange_half.start()
    exchange_half.wait()
    parts[...] = (halves[core].astype(F32) + half_in[...].astype(F32)).astype(BF).reshape(parts.shape)
    copies = [
        remote(parts.at[(x + dx) % 4 * 4 + (y + dy) % 4], parts_in.at[dx * 4 + dy], plane_send.at[dx * 4 + dy], plane_recv.at[dx * 4 + dy], at(dy, dx))
        for dy, dx in plane
    ]
    for one in copies:
        one.start()
    parts_in[0] = parts[x * 4 + y]
    features(0)
    features(1)
    for one in copies:
        one.wait()
    total = parts_in[0].astype(F32)
    for n in range(1, 16):
        total = total + parts_in[n].astype(F32)
    mid[song] = total
    copies = [
        remote(mid.at[song], mid.at[song], song_send.at[d], song_recv.at[d], (me, (song + d) % songs)) for d in range(1, songs)
    ]
    for one in copies:
        one.start()
    features(2)
    for one in copies:
        one.wait()
    total = mid[0]
    for n in range(1, songs):
        total = total + mid[n]
    full[core, x * 4 + y] = total.astype(BF)
    copies = [
        remote(full.at[core, x * 4 + y], full.at[core, x * 4 + y], back_send.at[dx * 4 + dy], back_recv.at[dx * 4 + dy], at(dy, dx))
        for dy, dx in plane
    ]
    for one in copies:
        one.start()
    features(3)
    for one in copies:
        one.wait()
    exchange_half = remote(full.at[core], full.at[core], last_send, last_recv, twin)
    exchange_half.start()
    exchange_half.wait()
    sum_ref[...] = full[...].reshape(inner, width)
    for i in range(4):
        out_copy(i).wait()


def finish(lengths, timed, gain, wqkv, wout, cotangent):
    seq = lax.axis_size("seq")
    songs = lax.axis_size("song")
    _, bands, chunk, width = timed.shape
    inner = HEADS * DH
    rows = bands * FRAMES_EACH
    count = 2 * chunk * bands
    cosine, sines = rotary_tables(np.tile(np.arange(bands), FRAMES_EACH), 4)
    dma = pltpu.SemaphoreType.DMA
    anywhere = pl.BlockSpec(memory_space=pl.ANY)
    return pl.pallas_call(
        functools.partial(finish_kernel, seq, songs),
        out_shape=(jax.ShapeDtypeStruct((count, width), BF), jax.ShapeDtypeStruct((inner, width), BF)),
        in_specs=[smem()] + [whole()] * 4 + [anywhere] + [whole()] * 2,
        out_specs=(anywhere, whole()),
        scratch_shapes=[
            VMEM((2, bands, chunk, width), BF),
            VMEM((count, width), BF),
            VMEM((count, inner), BF),
            VMEM((count, width), BF),
            VMEM((count, width), BF),
            VMEM((inner, width), F32),
            VMEM((2, inner // 2, width), BF),
            VMEM((inner // 2, width), BF),
            VMEM((16, inner // 32, width), BF),
            VMEM((16, inner // 32, width), BF),
            VMEM((songs, inner // 32, width), F32),
            VMEM((2, 16, inner // 32, width), BF),
            dma, dma((4,)), dma((3, seq)), dma((3, seq)), dma, dma, dma((16,)), dma((16,)),
            dma((songs,)), dma((songs,)), dma((16,)), dma((16,)), dma, dma,
        ],
        compiler_params=pltpu.CompilerParams(collective_id=2, has_side_effects=True, vmem_limit_bytes=36 * 2**20),
        cost_estimate=pl.CostEstimate(flops=10**10, bytes_accessed=7 * 10**6, transcendentals=0),
    )(lengths, timed, gain, wqkv, wout, cotangent, jnp.asarray(cosine), jnp.asarray(sines))


def per_device(spectrum, widths, lengths, bin_gain, embed_weight, embed_bias, time_gain, time_qkv, time_out, band_gain, band_qkv, band_out, cotangent):
    local_frames = spectrum.shape[1]
    bands, width = embed_bias.shape
    tangent = cotangent.reshape(local_frames * bands, width)
    owned, q, k, v, most = exchange(spectrum[0], widths, bin_gain, embed_weight, embed_bias, lengths, time_gain, time_qkv)
    timed = time_attention(lengths, most, owned, time_out, q, k, v)
    output, gradient = finish(lengths, timed, band_gain, band_qkv, band_out, tangent)
    return output.reshape(1, local_frames, bands, width), gradient.astype(F32)


def solution(mesh):
    return jax.shard_map(
        per_device,
        mesh=mesh,
        in_specs=(P("song", "seq", None), P(), P("song"), P(), P(), P(), P(), P(), P(), P(), P(), P(), P("song", "seq", None, None)),
        out_specs=(P("song", "seq", None, None), P()),
        check_vma=False,
    )
```

```python
import functools

import jax
import jax.numpy as jnp
import numpy as np
from jax import lax
from jax.experimental import pallas as pl
from jax.experimental.pallas import tpu as pltpu
from jax.sharding import PartitionSpec as P

HEADS = 8
DH = 64
HALF = DH // 2
GROUP = 4 * DH
FLOOR = 0.25
EPSILON = 1e-05
LOG2E = 1.4426950408889634
WINDOW = 1152
NT = (((1,), (1,)), ((), ()))
TN = (((0,), (0,)), ((), ()))
MESH = pl.DeviceIdType.MESH
BF = jnp.bfloat16
F32 = jnp.float32
SAFE = 100.0
VSAFE = 2.0**12
VMEM = pltpu.VMEM
LIMIT = 56 * 2**20


def whole():
    return pl.BlockSpec(memory_space=pltpu.VMEM)


def smem():
    return pl.BlockSpec(memory_space=pltpu.SMEM)


def rotary_tables(positions, repeat):
    frequency = np.exp(-(2.0 * np.arange(HALF, dtype=np.float64) / DH) * np.log(10000.0))
    angles = positions.astype(np.float64)[:, None] * frequency
    cosine = np.tile(np.cos(angles), (1, repeat)).astype(np.float32)
    sines = np.tile(np.sin(angles), (1, repeat)).astype(np.float32)
    return cosine, sines


def split_halves(weights):
    row = lax.broadcasted_iota(jnp.int32, (GROUP, GROUP), 0)
    col = lax.broadcasted_iota(jnp.int32, (GROUP, GROUP), 1)
    source = (col % 128) // HALF * DH + col // 128 * HALF + col % HALF
    one_hot = (row == source).astype(F32).astype(BF)
    return jnp.dot(weights, one_hot, preferred_element_type=F32).astype(BF)


def rms_norm(rows, gain):
    square = jnp.mean(rows * rows, axis=-1, keepdims=True)
    return (rows * lax.rsqrt(square + EPSILON) * gain).astype(BF)


def rope(values, cosine, sines):
    leading = values[:, :128]
    second = values[:, 128:]
    return leading * cosine - second * sines, second * cosine + leading * sines


VROWS = 128


def exchange_kernel(
    seq, length_ref, meta_ref, spectrum_ref, bin_gain_ref, w_hbm, last_ref, bias_ref, gain_ref, wqkv_ref, table_ref,
    x_ref, q_ref, k_ref, v_ref, most_ref, got, stage, w_ref, spec_ref, spec_gain_ref, w_sem, send_sem, recv_sem,
):
    frames, width = got.shape[1:]
    half = frames // 2
    inner = HEADS * DH
    me = lax.axis_index("seq")
    song = lax.axis_index("song")
    y, x, core = me // 8, me // 2 % 4, me % 2

    def other(i, sign):
        return (y + sign * (i // 8) + 4) % 4 * 8 + (x + sign * (i // 2 % 4) + 4) % 4 * 2 + (core + i % 2) % 2

    barrier = pltpu.get_barrier_semaphore()

    def greet(i, carry):
        pl.semaphore_signal(barrier, inc=1, device_id=(other(i, 1), song), device_id_type=MESH)
        return carry

    lax.fori_loop(1, seq, greet, 0)
    blocks = w_ref.shape[0]
    main = blocks * 128
    bands = bias_ref.shape[0]

    def load(n):
        return pltpu.make_async_copy(w_hbm.at[pl.ds(pl.multiple_of(n * 128, 128), 128)], w_ref.at[n], w_sem.at[n])

    def start_load(n, carry):
        load(n).start()
        return carry

    def wait_load(n, carry):
        load(n).wait()
        return carry

    lax.fori_loop(0, blocks, start_load, 0)
    for n in range(blocks):
        spec_ref[n] = spectrum_ref[:, n * 128 : (n + 1) * 128]
        spec_gain_ref[n] = bin_gain_ref[:, n * 128 : (n + 1) * 128]
    lane = lax.broadcasted_iota(jnp.int32, (1, GROUP), 1)
    wq = [split_halves(wqkv_ref[:, g * GROUP : (g + 1) * GROUP]) for g in range(2)]
    wk = [split_halves(wqkv_ref[:, inner + g * GROUP : inner + (g + 1) * GROUP]) for g in range(2)]
    wv = wqkv_ref[:, 2 * inner :]
    lax.fori_loop(0, blocks, wait_load, 0)

    def band(k):
        first = meta_ref[0, k]
        count = meta_ref[1, k]
        block = meta_ref[2, k]
        near = range(WINDOW // 128)
        entry = lax.broadcasted_iota(jnp.int32, (1, WINDOW), 1) + block * 128
        piece = jnp.concatenate([spec_ref[block + n] for n in near], axis=1).astype(F32)
        gains = jnp.concatenate([spec_gain_ref[block + n] for n in near], axis=1)
        weights = jnp.concatenate([w_ref[block + n] for n in near], axis=0)
        piece = jnp.where((entry >= first) & (entry < first + count), piece, 0.0)
        tail = jnp.where(k == bands - 1, spectrum_ref[:, main:].astype(F32), 0.0)
        square = jnp.sum(piece * piece, axis=1, keepdims=True) + jnp.sum(tail * tail, axis=1, keepdims=True)
        scale = 1.0 / jnp.sqrt(jnp.maximum(square / count.astype(F32), FLOOR))
        normed = (piece * scale * gains).astype(BF)
        summed = jnp.dot(normed, weights, preferred_element_type=F32) + bias_ref[pl.ds(k, 1), :]
        tail = (tail * scale * bin_gain_ref[:, main:]).astype(BF).astype(F32)
        rows = last_ref[...].astype(F32)
        for e in range(spectrum_ref.shape[1] - main):
            summed = summed + tail[:, e : e + 1] * rows[e : e + 1, :]
        stage[k] = summed.astype(BF)

    def copy(i):
        k = other(i, 1)
        return pltpu.make_async_remote_copy(
            src_ref=stage.at[k], dst_ref=got.at[me], send_sem=send_sem.at[i], recv_sem=recv_sem.at[i],
            device_id=(k, song), device_id_type=MESH)

    def front(j, carry):
        for n in range(2):
            band(other(8 + 16 * n + j, 1))
        for n in range(2):
            copy(8 + 16 * n + j).start()
        return carry

    def back(j, carry):
        for n in range(2):
            band(other(j + 16 * n, 1))
        for n in range(2):
            copy(j + 16 * n).start()
        return carry

    pl.semaphore_wait(barrier, seq - 1)
    lax.fori_loop(0, 8, front, 0)
    band(other(16, 1))
    copy(16).start()
    lax.fori_loop(1, 8, back, 0)
    band(me)
    got[me] = stage[me]
    length = length_ref[0]

    heads_of = lax.broadcasted_iota(jnp.int32, (GROUP, 128), 0) % 128 // HALF
    per_head = (heads_of == lax.broadcasted_iota(jnp.int32, (GROUP, 128), 1)).astype(F32).astype(BF)

    def longest(rows):
        squares = jnp.dot((rows * rows).astype(BF), per_head, preferred_element_type=F32)
        return jnp.max(squares, axis=0, keepdims=True)

    def project(dy, stats):
        row = (y - dy + 4) % 4

        def wait(i, carry):
            copy(8 * dy + i).wait_recv()
            return carry

        lax.fori_loop(1 if dy == 0 else 0, 8, wait, 0)
        owners = pl.ds(pl.multiple_of(row * 8, 8), 8)
        count = 8 * frames
        base = pl.multiple_of(row * count, count)
        rows = pl.ds(base, count)
        received = got[owners]
        x_ref[0, owners] = received[:, :half]
        x_ref[1, owners] = received[:, half:]
        normed = rms_norm(received.reshape(count, width).astype(F32), gain_ref[...].reshape(1, width))
        cosines, sine_parts = [], []
        for o in range(8):
            far = pl.ds(row * 8 + o, 1)
            cosines.append(table_ref[0, far, :] * table_ref[0, seq:, :] - table_ref[1, far, :] * table_ref[1, seq:, :])
            sine_parts.append(table_ref[1, far, :] * table_ref[0, seq:, :] + table_ref[0, far, :] * table_ref[1, seq:, :])
        cosine = jnp.concatenate(cosines, axis=0)
        sines = jnp.concatenate(sine_parts, axis=0)
        alive_row = (lax.broadcasted_iota(jnp.int32, (count, 1), 0) + base) < length
        alive_col = (lax.broadcasted_iota(jnp.int32, (1, count), 1) + base) < length
        kinds = []
        for g in range(2):
            qa, qb = rope(jnp.dot(normed, wq[g], preferred_element_type=F32), cosine, sines)
            scaled = jnp.concatenate([qa, qb], axis=1) * (LOG2E * DH**-0.5)
            parts = scaled.reshape(8, frames, GROUP)
            for n in range(2):
                later = pl.ds(pl.multiple_of(row * 8 * half + n * seq * half, 8 * half), 8 * half)
                q_ref[g, later, :] = parts[:, n * half : (n + 1) * half].reshape(8 * half, GROUP).astype(BF)
            ka, kb = rope(jnp.dot(normed, wk[g], preferred_element_type=F32), cosine, sines)
            keys = jnp.concatenate([ka, kb], axis=1)
            keys = jnp.where(alive_row, keys, 0.0)
            k_ref[g, rows, :] = keys.astype(BF)
            kinds.append(longest(scaled))
            kinds.append(longest(keys))
        values = lax.dot_general(wv, normed, (((0,), (1,)), ((), ())), preferred_element_type=F32)
        values = jnp.where(alive_col, values, 0.0)
        vmost = jnp.max(jnp.max(jnp.abs(values), axis=0, keepdims=True), axis=1, keepdims=True)
        kinds.append(jnp.broadcast_to(vmost, (1, 128)))
        values = values.astype(BF)
        ones = jnp.broadcast_to(jnp.where(alive_col, 1.0, 0.0), (VROWS - DH, count)).astype(BF)
        for h in range(HEADS):
            v_ref[h, :DH, rows] = values[h * DH : (h + 1) * DH]
            v_ref[h, DH:, rows] = ones
        if stats is None:
            return kinds
        return [jnp.maximum(p, n) for p, n in zip(stats, kinds)]

    stats = None
    for dy in (1, 3, 0, 2):
        stats = project(dy, stats)
    for n, row in enumerate(stats):
        most_ref[n : n + 1, :] = row

    def finish(i, carry):
        copy(i).wait_send()
        return carry

    lax.fori_loop(1, seq, finish, 0)


def exchange(spectrum, widths, bin_gain, embed_weight, embed_bias, lengths, gain, wqkv):
    seq = lax.axis_size("seq")
    frames, feature_count = spectrum.shape
    bands, width = embed_bias.shape
    count = seq * frames
    blocks = feature_count // 128
    main = blocks * 128
    starts = (jnp.cumsum(widths) - widths) * 4
    meta = jnp.stack([starts, widths * 4, jnp.minimum(starts // 128, blocks - WINDOW // 128)]).astype(jnp.int32)
    positions = np.concatenate([np.arange(seq) * frames, np.arange(frames)])
    table = np.stack(rotary_tables(positions, 4))
    dma = pltpu.SemaphoreType.DMA

    def full(*shape):
        return pl.BlockSpec(shape, lambda i: (0,) * len(shape))

    anywhere = pl.BlockSpec(memory_space=pl.ANY)
    shapes = [(2, seq, frames // 2, width), (2, count, GROUP), (2, count, GROUP), (HEADS, VROWS, count)]
    return pl.pallas_call(
        functools.partial(exchange_kernel, seq),
        grid=(1,),
        out_shape=[jax.ShapeDtypeStruct(shape, BF) for shape in shapes] + [jax.ShapeDtypeStruct((5, 128), F32)],
        in_specs=[
            smem(), smem(), full(frames, feature_count), full(1, feature_count), anywhere,
            pl.BlockSpec((16, width), lambda i: (main // 16, 0)), full(bands, width), full(width), full(*wqkv.shape),
            full(*table.shape),
        ],
        out_specs=[full(*shape) for shape in shapes] + [full(5, 128)],
        scratch_shapes=[
            VMEM((seq, frames, width), BF),
            VMEM((bands, frames, width), BF),
            VMEM((blocks, 128, width), BF),
            VMEM((blocks, frames, 128), BF),
            VMEM((blocks, 1, 128), F32),
            dma((blocks,)), dma((seq,)), dma((seq,)),
        ],
        compiler_params=pltpu.CompilerParams(collective_id=1, has_side_effects=True, vmem_limit_bytes=42 * 2**20),
        cost_estimate=pl.CostEstimate(flops=4 * 10**9, bytes_accessed=10 * 10**6, transcendentals=0),
    )(lengths, meta, spectrum, bin_gain[None], embed_weight, embed_weight, embed_bias, gain, wqkv, jnp.asarray(table))


TIME_LIMIT = 28 * 2**20


def time_kernel(length_ref, most_ref, x_ref, wout_ref, q_ref, k_ref, v_ref, out_ref, heads_ref):
    chunks, owners, half, width = x_ref.shape
    lane = lax.broadcasted_iota(jnp.int32, (1, GROUP), 1)
    bound = jnp.maximum(most_ref[0:1, :] * most_ref[1:2, :], most_ref[2:3, :] * most_ref[3:4, :])
    fits = (jnp.max(bound) * 1.05 < SAFE * SAFE) & (jnp.max(most_ref[4:5, :]) < VSAFE)

    def head(h, rows, shift):
        g = h // 4
        mine = (lane % 128) // HALF == h % 4
        queries = jnp.where(mine, q_ref[g, rows, :], jnp.zeros((), BF))
        scores = lax.dot_general(k_ref[g], queries, NT, preferred_element_type=F32)
        if shift:
            alive = lax.broadcasted_iota(jnp.int32, (k_ref.shape[1], 1), 0) < length_ref[0]
            scores = jnp.where(alive, scores, -1e30)
            scores = scores - jnp.max(scores, axis=0, keepdims=True)
        powers = jnp.exp2(scores).astype(BF)
        mixed = jnp.dot(v_ref[h], powers, preferred_element_type=F32)
        mixed = mixed[:DH] * (1.0 / mixed[DH : DH + 1])
        heads_ref[pl.ds(pl.multiple_of(h * DH, DH), DH), rows] = mixed.astype(BF)

    columns = owners * half

    @pl.when(fits)
    def _():
        def step(h, carry):
            head(h, slice(0, chunks * columns), False)
            return carry

        lax.fori_loop(0, HEADS, step, 0)

    @pl.when(jnp.logical_not(fits))
    def _():
        def step(n, carry):
            head(n % HEADS, pl.ds(pl.multiple_of(n // HEADS * columns, columns), columns), True)
            return carry

        lax.fori_loop(0, chunks * HEADS, step, 0)

    for chunk in range(chunks):
        heads = heads_ref[:, chunk * columns : (chunk + 1) * columns]
        projected = lax.dot_general(heads, wout_ref[...], TN, preferred_element_type=F32)
        out_ref[chunk] = (x_ref[chunk].astype(F32) + projected.reshape(owners, half, width)).astype(BF)


def time_attention(lengths, most, sequence, wout, q, k, v):
    chunks, owners, half, width = sequence.shape
    return pl.pallas_call(
        time_kernel,
        out_shape=jax.ShapeDtypeStruct(sequence.shape, BF),
        in_specs=[smem()] + [whole()] * 6,
        out_specs=whole(),
        scratch_shapes=[VMEM((HEADS * DH, chunks * owners * half), BF)],
        compiler_params=pltpu.CompilerParams(vmem_limit_bytes=36 * 2**20),
        cost_estimate=pl.CostEstimate(flops=4 * 10**10, bytes_accessed=8 * 10**6, transcendentals=0),
    )(lengths, most, sequence, wout, q, k, v)


FRAMES_EACH = 16


def finish_kernel(
    seq, songs, length_ref, timed_ref, gain_ref, wqkv_ref, wout_ref, cot_hbm, cos_ref, sin_ref,
    out_hbm, sum_ref, got, cot_ref, heads_ref, x_ref, feat_ref, grad_ref, halves, half_in, parts, parts_in, mid, full,
    cot_sem, out_sem, send_sem, recv_sem, core_send, core_recv, plane_send, plane_recv, song_send, song_recv, back_send, back_recv, last_send, last_recv,
):
    _, bands, chunk, width = timed_ref.shape
    inner = HEADS * DH
    rows = bands * FRAMES_EACH
    blocks = chunk // FRAMES_EACH
    half = 256
    me = lax.axis_index("seq")
    song = lax.axis_index("song")
    y, x, core = me // 8, me // 2 % 4, me % 2

    def other(i):
        return (y + i // 8) % 4 * 8 + (x + i // 2 % 4) % 4 * 2 + (core + i % 2) % 2

    cot_copy = pltpu.make_async_copy(cot_hbm, cot_ref, cot_sem)
    cot_copy.start()
    barrier = pltpu.get_barrier_semaphore()

    def greet(i, carry):
        pl.semaphore_signal(barrier, inc=1, device_id=(other(i), song), device_id_type=MESH)
        return carry

    lax.fori_loop(1, seq, greet, 0)
    for d in range(1, songs):
        pl.semaphore_signal(barrier, inc=1, device_id=(me, (song + d) % songs), device_id_type=MESH)

    lane = lax.broadcasted_iota(jnp.int32, (1, GROUP), 1)
    wq = [split_halves(wqkv_ref[:, g * GROUP : (g + 1) * GROUP]) for g in range(2)]
    wk = [split_halves(wqkv_ref[:, inner + g * GROUP : inner + (g + 1) * GROUP]) for g in range(2)]
    wv = wqkv_ref[:, 2 * inner :]
    to = lax.broadcasted_iota(jnp.int32, (rows, rows), 0)
    src = lax.broadcasted_iota(jnp.int32, (rows, rows), 1)
    order = (src == to % bands * FRAMES_EACH + to // bands).astype(F32).astype(BF)
    same = (
        lax.broadcasted_iota(jnp.int32, (4 * half, half), 0) % half // bands
        == lax.broadcasted_iota(jnp.int32, (4 * half, half), 1) // bands
    )
    grad_ref[...] = jnp.zeros_like(grad_ref)
    pl.semaphore_wait(barrier, seq - 1 + songs - 1)

    pieces = [(0, slice(0, chunk)), (1, slice(0, FRAMES_EACH)), (1, slice(FRAMES_EACH, 2 * FRAMES_EACH))]

    def copy(p, i):
        k = other(i)
        n, frames = pieces[p]
        return pltpu.make_async_remote_copy(
            src_ref=timed_ref.at[n, k, frames], dst_ref=got.at[n, me, frames], send_sem=send_sem.at[p, i], recv_sem=recv_sem.at[p, i],
            device_id=(k, song), device_id_type=MESH)

    for p in range(3):

        def start(i, carry):
            copy(p, seq - i).start()
            return carry

        lax.fori_loop(1, seq, start, 0)
    got[:, me] = timed_ref[:, me]
    length = length_ref[0]
    cot_copy.wait()

    def attend(p):
        def arrive(i, carry):
            copy(p, seq - i).wait()
            return carry

        lax.fori_loop(1, seq, arrive, 0)
        n, frames = pieces[p]

        def block(i, carry):
            first = n * blocks
            piece = got[n, :, pl.ds(pl.multiple_of(i * FRAMES_EACH, FRAMES_EACH), FRAMES_EACH), :].reshape(rows, width)
            values_x = jnp.dot(order, piece, preferred_element_type=F32)
            here = pl.ds(pl.multiple_of((i + first) * rows, rows), rows)
            x_ref[here, :] = values_x.astype(BF)
            normed = rms_norm(values_x, gain_ref[...].reshape(1, width))
            cosine = cos_ref[...]
            sines = sin_ref[...]
            values = jnp.dot(normed, wv, preferred_element_type=F32)
            joined_groups = []
            for g in range(2):
                qa, qb = rope(jnp.dot(normed, wq[g], preferred_element_type=F32), cosine, sines)
                queries = (jnp.concatenate([qa, qb], axis=1) * (LOG2E * DH**-0.5)).astype(BF)
                ka, kb = rope(jnp.dot(normed, wk[g], preferred_element_type=F32), cosine, sines)
                keys = jnp.concatenate([ka, kb], axis=1).astype(BF)
                stacks = []
                for s in range(rows // half):
                    part = slice(s * half, (s + 1) * half)
                    stacked = jnp.concatenate(
                        [jnp.where((lane % 128) // HALF == h, queries[part], jnp.zeros((), BF)) for h in range(4)], axis=0)
                    scores = lax.dot_general(stacked, keys[part], NT, preferred_element_type=F32)
                    scores = jnp.where(same, scores, -1e30)
                    powers = jnp.exp2(scores - jnp.max(scores, axis=1, keepdims=True))
                    mixed = jnp.dot(
                        powers.astype(BF), values[part, g * GROUP : (g + 1) * GROUP].astype(BF), preferred_element_type=F32)
                    mixed = mixed * (1.0 / jnp.sum(powers, axis=1, keepdims=True))
                    joined = mixed[:half]
                    for h in range(1, 4):
                        joined = jnp.where(lane // DH == h, mixed[h * half : (h + 1) * half], joined)
                    stacks.append(joined.astype(BF))
                joined_groups.append(jnp.concatenate(stacks, axis=0))
            heads = jnp.concatenate(joined_groups, axis=1)
            heads_ref[here, :] = heads
            frame = me * (2 * chunk) + (i + first) * FRAMES_EACH + lax.broadcasted_iota(jnp.int32, (rows, 1), 0) // bands
            tangent = jnp.where(frame < length, cot_ref[here, :].astype(F32), 0.0).astype(BF)
            grad_ref[...] += lax.dot_general(heads, tangent, TN, preferred_element_type=F32)
            return carry

        lax.fori_loop(frames.start // FRAMES_EACH, frames.stop // FRAMES_EACH, block, 0)

    def out_copy(i):
        here = slice(i * rows, (i + 1) * rows)
        return pltpu.make_async_copy(feat_ref.at[here], out_hbm.at[here], out_sem.at[i])

    def features(i):
        here = slice(i * rows, (i + 1) * rows)
        projected = jnp.dot(heads_ref[here, :], wout_ref[...], preferred_element_type=F32)
        feat_ref[here, :] = (x_ref[here, :].astype(F32) + projected).astype(BF)
        out_copy(i).start()

    attend(0)
    attend(1)
    attend(2)

    def remote(src_ref, dst_ref, send, recv, device):
        return pltpu.make_async_remote_copy(
            src_ref=src_ref, dst_ref=dst_ref, send_sem=send, recv_sem=recv, device_id=device, device_id_type=MESH)

    twin = (me + 1 - 2 * core, song)
    plane = [(dy, dx) for dy in range(4) for dx in range(4) if dy or dx]

    def at(dy, dx):
        return ((y + dy) % 4 * 8 + (x + dx) % 4 * 2 + core, song)

    halves[...] = grad_ref[...].astype(BF).reshape(halves.shape)
    exchange_half = remote(halves.at[1 - core], half_in, core_send, core_recv, twin)
    exchange_half.start()
    exchange_half.wait()
    parts[...] = (halves[core].astype(F32) + half_in[...].astype(F32)).astype(BF).reshape(parts.shape)
    copies = [
        remote(parts.at[(x + dx) % 4 * 4 + (y + dy) % 4], parts_in.at[dx * 4 + dy], plane_send.at[dx * 4 + dy], plane_recv.at[dx * 4 + dy], at(dy, dx))
        for dy, dx in plane
    ]
    for one in copies:
        one.start()
    parts_in[0] = parts[x * 4 + y]
    features(0)
    features(1)
    for one in copies:
        one.wait()
    total = parts_in[0].astype(F32)
    for n in range(1, 16):
        total = total + parts_in[n].astype(F32)
    mid[song] = total
    copies = [
        remote(mid.at[song], mid.at[song], song_send.at[d], song_recv.at[d], (me, (song + d) % songs)) for d in range(1, songs)
    ]
    for one in copies:
        one.start()
    features(2)
    for one in copies:
        one.wait()
    total = mid[0]
    for n in range(1, songs):
        total = total + mid[n]
    full[core, x * 4 + y] = total.astype(BF)
    copies = [
        remote(full.at[core, x * 4 + y], full.at[core, x * 4 + y], back_send.at[dx * 4 + dy], back_recv.at[dx * 4 + dy], at(dy, dx))
        for dy, dx in plane
    ]
    for one in copies:
        one.start()
    features(3)
    for one in copies:
        one.wait()
    exchange_half = remote(full.at[core], full.at[core], last_send, last_recv, twin)
    exchange_half.start()
    exchange_half.wait()
    sum_ref[...] = full[...].reshape(inner, width)
    for i in range(4):
        out_copy(i).wait()


def finish(lengths, timed, gain, wqkv, wout, cotangent):
    seq = lax.axis_size("seq")
    songs = lax.axis_size("song")
    _, bands, chunk, width = timed.shape
    inner = HEADS * DH
    rows = bands * FRAMES_EACH
    count = 2 * chunk * bands
    cosine, sines = rotary_tables(np.tile(np.arange(bands), FRAMES_EACH), 4)
    dma = pltpu.SemaphoreType.DMA
    anywhere = pl.BlockSpec(memory_space=pl.ANY)
    return pl.pallas_call(
        functools.partial(finish_kernel, seq, songs),
        out_shape=(jax.ShapeDtypeStruct((count, width), BF), jax.ShapeDtypeStruct((inner, width), BF)),
        in_specs=[smem()] + [whole()] * 4 + [anywhere] + [whole()] * 2,
        out_specs=(anywhere, whole()),
        scratch_shapes=[
            VMEM((2, bands, chunk, width), BF),
            VMEM((count, width), BF),
            VMEM((count, inner), BF),
            VMEM((count, width), BF),
            VMEM((count, width), BF),
            VMEM((inner, width), F32),
            VMEM((2, inner // 2, width), BF),
            VMEM((inner // 2, width), BF),
            VMEM((16, inner // 32, width), BF),
            VMEM((16, inner // 32, width), BF),
            VMEM((songs, inner // 32, width), F32),
            VMEM((2, 16, inner // 32, width), BF),
            dma, dma((4,)), dma((3, seq)), dma((3, seq)), dma, dma, dma((16,)), dma((16,)),
            dma((songs,)), dma((songs,)), dma((16,)), dma((16,)), dma, dma,
        ],
        compiler_params=pltpu.CompilerParams(collective_id=2, has_side_effects=True, vmem_limit_bytes=36 * 2**20),
        cost_estimate=pl.CostEstimate(flops=10**10, bytes_accessed=7 * 10**6, transcendentals=0),
    )(lengths, timed, gain, wqkv, wout, cotangent, jnp.asarray(cosine), jnp.asarray(sines))


def per_device(spectrum, widths, lengths, bin_gain, embed_weight, embed_bias, time_gain, time_qkv, time_out, band_gain, band_qkv, band_out, cotangent):
    local_frames = spectrum.shape[1]
    bands, width = embed_bias.shape
    tangent = cotangent.reshape(local_frames * bands, width)
    owned, q, k, v, most = exchange(spectrum[0], widths, bin_gain, embed_weight, embed_bias, lengths, time_gain, time_qkv)
    timed = time_attention(lengths, most, owned, time_out, q, k, v)
    output, gradient = finish(lengths, timed, band_gain, band_qkv, band_out, tangent)
    return output.reshape(1, local_frames, bands, width), gradient.astype(F32)


def solution(mesh):
    return jax.shard_map(
        per_device,
        mesh=mesh,
        in_specs=(P("song", "seq", None), P(), P("song"), P(), P(), P(), P(), P(), P(), P(), P(), P(), P("song", "seq", None, None)),
        out_specs=(P("song", "seq", None, None), P()),
        check_vma=False,
    )
```
